128 devices in a mesh: freq: 8 (over y, core), lat: 16 (over z, x).
Axes of the slice: x: 4, y: 4, z: 4, core: 2. Of those that a mesh axis runs over, the one named last changes fastest.
Arguments:
- spectra: float32 [2, 8, 131072], P(None, None, ('freq', 'lat')), may hold values from -6 to 6
- tile_route: int32 [131072, 1], P(('freq', 'lat')), may hold values from 0 to 255; in each aligned block of 1024 rows (0 to 1023, 1024 to 2047, ...) at most 8 rows name the same one
- bin_in_tile: int32 [131072], P(('freq', 'lat')), may hold values from 0 to 1023
- trace_offset: float32 [2, 131072], P(None, ('freq', 'lat')), may hold values from -0.5 to 0.5
- weights: float32 [131072], P(('freq', 'lat')), may hold values from 0.2 to 5
- frequency: float32 [8], P('freq'), may hold values from 0.5 to 1.5
- slowness: float32 [2, 8], replicated, may hold values from 0.6 to 1.6
- vel_index: int32 [2, 512, 512], P(None, 'lat'), may hold values from 0 to 7
Outputs:
- wavefield: float32 [2, 8, 512, 512], P(None, 'freq', 'lat')
- depth_image: float32 [2, 512, 512], P(None, 'lat', 'freq')
The draws below stay inside these ranges and needn't reach their ends.
Inputs may be any that keep to these rules, and one draw needn't show every extreme that they name: `tile_route`: tiles of 32 x 32 bins, numbered row by row over the grid; among the rows of one device no tile is named by more than 8 traces. `bin_in_tile`: row * 32 + column of the bin within the tile.
All inputs are finite; a program needn't handle non-finite values.
Results may differ from the reference program's by a relative error of at most 0.0003.
Values sent between devices are 32-bit elements; how exact they have to be, the bound alone decides.
No kernel may reach another device: no remote copies, remote signals or barrier semaphores. Data moves between devices by JAX's collectives and lax.ppermute only.
A program may use at most 64 MiB of HBM per device.

```python
import math
import jax
import jax.numpy as jnp
import numpy as np
from jax import lax

NX = 512
NY = 512
TB = 32
MODES = 8
TR_DEV = 1024
NSTEPS = 2
NREF = 2
NVEL = 8
NF = 8
TRACES = 131072
TILES = 256
CAP = 8
N_LAT = 16
DEVICES = 128


def plant(values, rng, least, largest):
    shape = values.shape
    place = [jax.random.randint(jax.random.fold_in(rng, axis), (), 0, shape[axis]) for axis in range(len(shape))]
    values = values.at[tuple(place)].set(least)
    longest = shape.index(max(shape))
    place[longest] = (place[longest] + 1) % shape[longest]
    return values.at[tuple(place)].set(largest)


def block_scale(key, dims, shards, low, top_value):
    loudness, own = 1.0, jax.random.fold_in(key, 6)
    for dim, parts in shards:
        steps = jnp.exp(jax.random.uniform(jax.random.fold_in(own, dim), (parts,), jnp.float32, low / len(shards), top_value / len(shards)))
        loudness = loudness * jnp.repeat(steps, dims[dim] // parts).reshape([-1 if axis == dim else 1 for axis in range(len(dims))])
    return loudness


def shared_out(rng, own, number, rows, count, top, most, skew):
    order = jax.random.permutation(rng, count)
    heavy_load, common = load_shares(count, rows * top, most, skew, True), load_shares(count, rows * top, most, skew, False)
    places = jnp.arange(count)

    def named(sizes, turn):
        used = int((sizes > 0).sum())
        fixed = max(1, used // 4)
        moved = fixed + (places - fixed + turn * (used - fixed)) % max(1, count - fixed)
        return jnp.zeros((count,), jnp.int32).at[order[jnp.where(places < fixed, places, moved)]].set(jnp.asarray(sizes, jnp.int32))

    sizes = jnp.where(number % 4 == 0, named(heavy_load, number // 4), named(common, number - number // 4 - 1))
    mixed = jax.random.permutation(jax.random.fold_in(own, 3), count)
    donor, sink = mixed[0:count // 2 * 2:2], mixed[1:count // 2 * 2:2]
    room = jnp.minimum(sizes[donor] - 1, most - sizes[sink]) // 2
    room = jnp.where((donor == order[0]) | (sink == order[0]) | (sizes[sink] == 0), 0, jnp.maximum(room, 0))
    moved = jax.random.randint(jax.random.fold_in(own, 4), (count // 2,), 0, 1 << 20) % (room + 1)
    sizes = sizes.at[donor].add(-moved).at[sink].add(moved)
    labels = jnp.searchsorted(jnp.cumsum(sizes), jnp.arange(rows * top), side="right").astype(jnp.int32)
    table = labels.reshape(top, rows).T
    table = table[jax.random.permutation(jax.random.fold_in(own, 1), rows)]
    turn = jax.random.randint(jax.random.fold_in(own, 2), (rows, 1), 0, top)
    return jnp.take_along_axis(table, (jnp.arange(top)[None, :] + turn) % top, axis=1)


def load_shares(amount, total, reach, lean, full):
    portions = [(1 << 20) // math.isqrt(grade ** lean) + 1 for grade in range(1, amount + 1)]
    largest = reach if full else min(reach, max(-(-total // amount), total * portions[0] // sum(portions)))
    least = 1 if total - largest >= amount - 1 else 0
    given, spare = [largest] + [least] * (amount - 1), total - largest - least * (amount - 1)
    while spare > 0:
        candidates = [i for i in range(1, amount) if given[i] < largest] or [i for i in range(1, amount) if given[i] < reach]
        mass, budget = sum([portions[i] for i in candidates]), spare
        for i in candidates:
            more = min(reach - given[i], max(1, budget * portions[i] // mass), spare)
            given[i] = given[i] + more
            spare = spare - more
    return np.array(given)


def gaussian(key, dims, deviation, reach, pieces=(), kind=jnp.bfloat16):
    result = jax.random.normal(key, dims, jnp.float32) * deviation
    if len(pieces) > 0:
        result = block_scale(key, dims, pieces, -0.22, 0.18) * result
    return jnp.clip(result, min=-reach, max=reach).astype(kind)


def setup_inputs(seed: int = 0) -> dict:
    streams_of = jax.random.split(jax.random.key(seed), 9)
    spectra = gaussian(streams_of[0], (2, NF, TRACES), 1.0, 6.0, ((2, 128),), jnp.float32)
    tile_route_keys = jax.random.split(jax.random.fold_in(streams_of[1], 1), TRACES // TR_DEV)
    tile_route_turns = jax.random.permutation(jax.random.fold_in(streams_of[1], 3), TRACES // TR_DEV)
    tile_route = jax.vmap(lambda own, number: shared_out(jax.random.fold_in(streams_of[1], 2), own, number, TR_DEV, TILES, 1, CAP, 2))(tile_route_keys, tile_route_turns).reshape((TRACES, 1))
    bin_in_tile = plant(jax.random.randint(streams_of[2], (TRACES,), 0, TB * TB), jax.random.fold_in(streams_of[2], 1), 0, (TB * TB) - 1).astype(jnp.int32)
    trace_offset = jnp.clip(jax.random.uniform(streams_of[3], (2, TRACES), jnp.float32, -0.5, 0.5) * block_scale(streams_of[3], (2, TRACES), ((1, 128),), -0.4, 0.0), -0.5, 0.5)
    weights = jnp.clip(jnp.exp(math.log(5.0) - 3.218876 * jax.random.uniform(streams_of[4], (TRACES,), jnp.float32) ** block_scale(streams_of[4], (TRACES,), ((0, 128),), -0.2, 0.2)), 0.2, 5.0)
    frequency = jnp.clip(0.5 + 1.0 * jax.random.uniform(streams_of[5], (NF,), jnp.float32) ** block_scale(streams_of[5], (NF,), ((0, 8),), -0.2, 0.2), 0.5, 1.5)
    slowness = jnp.clip(jnp.exp(jax.random.uniform(streams_of[6], (NSTEPS, NVEL), jnp.float32, math.log(0.6), math.log(1.6))), 0.6, 1.6)
    vel_index = plant(jax.random.randint(streams_of[7], (NSTEPS, NX, NY), 0, NVEL), jax.random.fold_in(streams_of[7], 1), 0, NVEL - 1).astype(jnp.int32)
    return dict(spectra=spectra, tile_route=tile_route, bin_in_tile=bin_in_tile, trace_offset=trace_offset, weights=weights, frequency=frequency, slowness=slowness, vel_index=vel_index)


damping = 1.0
depth_step = 1.0

def basis_of(cell_x, cell_y):
    mode_ids = jnp.arange(MODES).astype(jnp.float32)
    along_x = jnp.cos(math.pi * mode_ids.reshape((MODES,) + (1,) * cell_x.ndim) * (cell_x[None] + 0.5) / TB)
    along_y = jnp.cos(math.pi * mode_ids.reshape((MODES,) + (1,) * cell_y.ndim) * (cell_y[None] + 0.5) / TB)
    return (along_x[:, None] * along_y[None, :]).reshape((MODES * MODES,) + cell_x.shape)

def fit_grid(normal, right_side, row_count):
    tile_count = normal.shape[0]
    system = normal + damping * jnp.eye(MODES * MODES, dtype=jnp.float32)
    factor = jnp.linalg.cholesky(system)
    flat_rhs = right_side.reshape(tile_count, MODES * MODES, -1)
    middle = jax.scipy.linalg.solve_triangular(factor, flat_rhs, lower=True)
    coeffs = jax.scipy.linalg.solve_triangular(factor, middle, lower=True, trans='T')
    coeffs = coeffs.reshape(row_count // TB, NY // TB, MODES, MODES, 2, -1)
    cell_pos = jnp.arange(TB).astype(jnp.float32)
    cos_table = jnp.cos(math.pi * jnp.arange(MODES).astype(jnp.float32)[:, None] * (cell_pos[None, :] + 0.5) / TB)
    viewed = jnp.einsum('xyabpq,ai,bj->pqxiyj', coeffs, cos_table, cos_table, precision=lax.Precision.HIGHEST)
    return viewed.reshape(2, viewed.shape[1], row_count, NY)

def reference(spectra, tile_route, bin_in_tile, trace_offset, weights, frequency, slowness, vel_index):
    tile_id = tile_route[:, 0].astype(jnp.int32)
    trace_count = tile_id.shape[0]
    per_tile = DEVICES * CAP
    ranking = jnp.argsort(tile_id, stable=True).astype(jnp.int32)
    sorted_tiles = tile_id[ranking]
    firsts = jnp.searchsorted(sorted_tiles, sorted_tiles, side='left').astype(jnp.int32)
    position = sorted_tiles * per_tile + jnp.arange(trace_count, dtype=jnp.int32) - firsts
    lookup = jnp.full((TILES * per_tile,), trace_count, jnp.int32).at[position].set(ranking)
    cell_x = (bin_in_tile // TB).astype(jnp.float32) + trace_offset[0]
    cell_y = (bin_in_tile % TB).astype(jnp.float32) + trace_offset[1]
    trace_meta = jnp.stack([weights, cell_x, cell_y], 0)
    padded_meta = jnp.concatenate([trace_meta, jnp.zeros((3, 1), jnp.float32)], 1)
    padded_spec = jnp.concatenate([spectra, jnp.zeros((2, NF, 1), jnp.float32)], 2)
    tile_dev = TILES // N_LAT
    row_count = NX // N_LAT

    def one_owner(owner_at):
        picks = lax.dynamic_slice_in_dim(lookup, owner_at * tile_dev * per_tile, tile_dev * per_tile)
        meta_here = padded_meta[:, picks].reshape(3, tile_dev, per_tile)
        spec_here = padded_spec[:, :, picks].reshape(2, NF, tile_dev, per_tile)
        basis_vals = basis_of(meta_here[1], meta_here[2])
        weighted = basis_vals * meta_here[0][None]
        normal = jnp.einsum('itc,jtc->tij', weighted, basis_vals, precision=lax.Precision.HIGHEST)
        right_side = jnp.einsum('itc,pqtc->tipq', weighted, spec_here, precision=lax.Precision.HIGHEST)
        return fit_grid(normal, right_side, row_count)
    slabs = lax.map(one_owner, jnp.arange(N_LAT, dtype=jnp.int32))
    gridded = jnp.moveaxis(slabs, 0, 2).reshape(2, NF, NX, NY)
    wave_field = gridded[0] + 1j * gridded[1]
    index_x = jnp.arange(NX)
    index_y = jnp.arange(NY)
    signed_x = jnp.where(index_x >= NX // 2, index_x - NX, index_x)
    signed_y = jnp.where(index_y >= NY // 2, index_y - NY, index_y)
    kx_vals = 2.0 * math.pi / NX * signed_x.astype(jnp.float32)
    ky_vals = 2.0 * math.pi / NY * signed_y.astype(jnp.float32)
    per_group = NVEL // NREF
    images = []
    for depth_at in range(NSTEPS):
        table_row = slowness[depth_at]
        references = table_row.reshape(NREF, per_group).mean(axis=1)
        spectrum = jnp.fft.fft2(wave_field)
        wave_num = frequency[None, :] * references[:, None]
        vertical = (wave_num * wave_num)[:, :, None, None] - (kx_vals * kx_vals)[None, None, :, None] - (ky_vals * ky_vals)[None, None, None, :]
        phase_angle = jnp.sqrt(jnp.maximum(vertical, 0.0)) * depth_step
        damped = jnp.exp(-jnp.sqrt(jnp.maximum(-vertical, 0.0)) * depth_step)
        returned = jnp.fft.ifft2(spectrum[None] * (damped * jnp.exp(1j * phase_angle)))
        velocity = vel_index[depth_at]
        local_slow = table_row[velocity]
        group_of = velocity // per_group
        split_phase = frequency[None, :, None, None] * (local_slow[None, None] - references[:, None, None, None]) * depth_step
        group_mask = group_of[None] == jnp.arange(NREF)[:, None, None]
        wave_field = lax.optimization_barrier(jnp.sum(jnp.where(group_mask[:, None], returned * jnp.exp(1j * split_phase), 0.0), 0))
        images.append(lax.optimization_barrier(jnp.sum(jnp.real(wave_field), 0)).astype(jnp.float32))
    wavefield = jnp.stack([jnp.real(wave_field), jnp.imag(wave_field)], 0).astype(jnp.float32)
    return (wavefield, jnp.stack(images, 0))
```

```python
import math

import jax
import jax.numpy as jnp
import ml_dtypes
import numpy as np
from jax import lax
from jax.experimental import pallas as pl
from jax.experimental.pallas import tpu as pltpu
from jax.sharding import PartitionSpec as P

NX = 512
NY = 512
TB = 32
MODES = 8
HALF = 256
SCALE = 1.0 / (NX * NY)
STEP = 2.0 * math.pi / 512

f32 = jnp.float32
bf16 = jnp.bfloat16
VM = pl.BlockSpec(memory_space=pltpu.VMEM)
SM = pl.BlockSpec(memory_space=pltpu.SMEM)
ANY = pl.BlockSpec(memory_space=pl.ANY)


def pair(table):
    table = np.asarray(table, np.float32)
    high = table.astype(ml_dtypes.bfloat16)
    low = (table - high.astype(np.float32)).astype(ml_dtypes.bfloat16)
    return high, low


def column_order():
    out = []
    for q in range(2):
        first = 2 * np.arange(128) + q
        mirror = (512 - first) % 512
        if q == 0:
            mirror[0] = 256
        out.append(np.concatenate([first, mirror]))
    return np.stack(out)


def row_order():
    first = np.arange(256)
    mirror = (512 - first) % 512
    mirror[0] = 256
    return np.concatenate([first, mirror])


def angle(left, right):
    return 2.0 * np.pi / 512 * ((left[:, None] * right[None, :]) % 512)


def mode_spectrum(order):
    cell = np.arange(TB)
    modes = np.cos(np.pi * np.arange(MODES)[:, None] * (cell[None, :] + 0.5) / TB)
    place = np.arange(16)[:, None] * TB + cell[None, :]
    wave = np.exp(-2j * np.pi / 512 * ((place[:, :, None] * order[None, None, :]) % 512))
    return np.einsum("aj,yjn->yan", modes, wave).reshape(16 * MODES, -1)


def tables():
    cols, rows = column_order(), row_order()
    every = cols.reshape(-1)
    ey = mode_spectrum(every)
    ey = np.concatenate([ey.real, ey.imag], 1)
    ex = mode_spectrum(rows).T
    ex = np.concatenate(
        [np.concatenate([ex.real, -ex.imag], 1), np.concatenate([ex.imag, ex.real], 1)], 0
    )
    own = []
    for slab in range(16):
        x_at = np.concatenate([32 * slab + 2 * np.arange(16) + h for h in range(2)])
        turn = angle(x_at, rows)
        own.append(np.concatenate([np.cos(turn), np.sin(turn)], 0))
    own_high, own_low = pair(np.stack(own))
    own = np.concatenate([own_high, own_low], 1)
    half = np.arange(HALF)
    back_y, forth_y = [], []
    for q in range(2):
        turn = angle(cols[q], half)
        back_y.append(np.concatenate([np.cos(turn), np.sin(turn)], 1))
        forth_y.append(np.concatenate([np.cos(turn.T), np.sin(turn.T)], 1))
    forth_x, back_x = [], []
    for h in range(2):
        turn = angle(half, 2 * half + h)
        forth_x.append(np.concatenate([np.cos(turn), np.sin(turn)], 0))
        back_x.append(np.concatenate([np.cos(turn.T), np.sin(turn.T)], 0))
    return dict(
        ey=pair(ey),
        ex=pair(ex),
        own=own,
        back_y=pair(np.stack(back_y)),
        forth_y=pair(np.stack(forth_y)),
        forth_x=pair(np.stack(forth_x)),
        back_x=pair(np.stack(back_x)),
    )


def split(value):
    high = value.astype(bf16)
    low = (value - high.astype(f32)).astype(bf16)
    return high, low


def mm(left, right):
    return jnp.dot(left, right, preferred_element_type=f32)


def dot3(left, right):
    return mm(left[0], right[0]) + (mm(left[0], right[1]) + mm(left[1], right[0]))


def lanes(shape):
    return lax.broadcasted_iota(jnp.int32, shape, len(shape) - 1)


def turned(value, shift, axis=1):
    size = value.shape[axis]
    shift = shift % size
    return value if shift == 0 else pltpu.roll(value, shift, axis)


def cos_sin(turn):
    half = 0.5 * turn
    sq = half * half
    cosine = 1.0 / 479001600
    for c in (-1.0 / 3628800, 1.0 / 40320, -1.0 / 720, 1.0 / 24, -0.5, 1.0):
        cosine = cosine * sq + c
    sine = 1.0 / 6227020800
    for c in (-1.0 / 39916800, 1.0 / 362880, -1.0 / 5040, 1.0 / 120, -1.0 / 6, 1.0):
        sine = sine * sq + c
    sine = sine * half
    return 1.0 - 2.0 * sine * sine, 2.0 * sine * cosine


def shift_factor(wave_sq, kx, ky):
    vertical = wave_sq - kx * kx - ky * ky
    root = jnp.sqrt(jnp.abs(vertical))
    cosine, sine = cos_sin(root)
    moving = vertical > 0.0
    return jnp.where(moving, cosine, jnp.exp(-root)), jnp.where(moving, sine, 0.0)


def references_of(slow_ref, step):
    values = [slow_ref[step, i] for i in range(8)]
    refs = [
        (values[4 * g] + values[4 * g + 1] + values[4 * g + 2] + values[4 * g + 3]) * 0.25
        for g in range(2)
    ]
    return values, refs


def velocity_rows(vel_ref, vel_tmp, step):
    for c in range(4):
        vel_tmp[c] = vel_ref[step, :, 128 * c : 128 * c + 128]
    return jnp.concatenate(
        [
            jnp.concatenate([vel_tmp[c, pl.ds(h, 16, stride=2), :] for c in range(4)], 1)
            for h in range(2)
        ],
        0,
    )


def rows_to_field(step, parts, back_high, back_low, vel_ref, vel_tmp, slow_ref, freq_ref):
    halves = []
    for q in range(2):
        both = dot3(split(parts[q]), (back_high[q], back_low[q]))
        with_cos, with_sin = both[:, :HALF], both[:, HALF:]
        halves.append(
            (with_cos[:64] - with_sin[64:], with_cos[64:] + with_sin[:64])
        )
    back = [
        jnp.concatenate([halves[0][p] + halves[1][p], halves[0][p] - halves[1][p]], 1)
        for p in range(2)
    ]
    velocity = velocity_rows(vel_ref, vel_tmp, step)
    values, refs = references_of(slow_ref, step)
    picked = [jnp.where(velocity >= 4, back[p][32:], back[p][:32]) for p in range(2)]
    turn = jnp.zeros(velocity.shape, f32)
    for i in range(8):
        turn = jnp.where(velocity == i, freq_ref[0] * (values[i] - refs[i // 4]), turn)
    cosine, sine = cos_sin(turn)
    cosine, sine = cosine * SCALE, sine * SCALE
    return (
        picked[0] * cosine - picked[1] * sine,
        picked[0] * sine + picked[1] * cosine,
    )


def route_kernel(tile_ref, bin_ref, offset_ref, weight_ref, spectra_ref, out_ref):
    tile = tile_ref[...]
    tile_f = tile.astype(f32)
    below = lax.broadcasted_iota(jnp.int32, (128, 128), 0) < lanes((128, 128))
    columns = []
    ranks = []
    for j in range(8):
        here = tile_f[:, 128 * j : 128 * (j + 1)]
        here_all = jnp.broadcast_to(here, (128, 128))
        columns.append(here_all.T)
        found = jnp.where((columns[j] == here_all) & below, 1.0, 0.0)
        for i in range(j):
            found = found + jnp.where(columns[i] == here_all, 1.0, 0.0)
        ranks.append(jnp.sum(found, axis=0, keepdims=True))
    rank = jnp.concatenate(ranks, 1).astype(jnp.int32)
    row_at = (tile >> 1) * 4 + (rank & 3)
    group_at = (tile & 1) * 2 + (rank >> 2)
    place = bin_ref[...]
    cell_x = (place >> 5).astype(f32) + offset_ref[0:1, :]
    cell_y = (place & 31).astype(f32) + offset_ref[1:2, :]
    values = jnp.concatenate(
        [
            spectra_ref[...],
            jnp.concatenate([weight_ref[...], cell_x, cell_y, jnp.zeros((5, 1024), f32)], 0),
            jnp.zeros((8, 1024), f32),
        ],
        0,
    )
    spread = jnp.concatenate([jnp.where(group_at == s, values, 0.0) for s in range(4)], 0)
    high = spread.astype(bf16)
    rest = spread - high.astype(f32)
    mid = rest.astype(bf16)
    low = (rest - mid.astype(f32)).astype(bf16)
    wide = jnp.concatenate([high, mid, low], 0)
    rows = lax.broadcasted_iota(jnp.int32, (512, 1024), 0)
    chosen = jnp.where(rows == row_at, 1.0, 0.0).astype(bf16)
    moved = lax.dot_general(
        chosen, wide, (((1,), (1,)), ((), ())), preferred_element_type=f32
    )
    out_ref[...] = (moved[:, :128] + moved[:, 128:256]) + moved[:, 256:]


def solve_kernel(got_ref, out_ref):
    turned_in = got_ref[...].T
    blocks = []
    mode = lax.broadcasted_iota(jnp.int32, (8, 1024), 0).astype(f32)
    eye_rows = lax.broadcasted_iota(jnp.int32, (64, 128), 0)
    eye = jnp.where(eye_rows == lanes((64, 128)), 1.0, 0.0)
    for t in range(2):
        both = jnp.concatenate(
            [turned_in[64 * t : 64 * t + 24], turned_in[64 * t + 32 : 64 * t + 56]], 1
        )
        along_x = jnp.cos(math.pi * mode * (both[17:18] + 0.5) / TB)
        along_y = jnp.cos(math.pi * mode * (both[18:19] + 0.5) / TB)
        basis = jnp.concatenate([along_x[a : a + 1] * along_y for a in range(8)], 0)
        wide = jnp.concatenate([basis, both[0:16], jnp.zeros((48, 1024), f32)], 0)
        system = lax.dot_general(
            basis * both[16:17],
            wide,
            (((1,), (1,)), ((), ())),
            preferred_element_type=f32,
            precision=lax.Precision.HIGHEST,
        )
        system = system + eye
        blocks.append([system[8 * a : 8 * a + 8] for a in range(8)])
    sub = lax.broadcasted_iota(jnp.int32, (8, 128), 0)
    for j in range(64):
        at, inner = j // 8, j % 8
        for t in range(2):
            mine = blocks[t]
            row = mine[at][inner : inner + 1]
            row = row / row[:, j : j + 1]
            fresh = []
            for a in range(8):
                new = mine[a] - mine[a][:, j : j + 1] * row
                if a == at:
                    new = jnp.where(sub == inner, row, new)
                fresh.append(new)
            blocks[t] = fresh
    stacked = jnp.concatenate([blocks[t][a] for a in range(8) for t in range(2)], 0)
    final = stacked.T
    odd = (lax.broadcasted_iota(jnp.int32, (32, 128), 0) & 1) == 1
    for f in range(8):
        out_ref[32 * f : 32 * f + 32] = jnp.where(
            odd, final[72 + f : 73 + f], final[64 + f : 65 + f]
        )


def first_kernel(
    lat_ref,
    freq_ref,
    slow_ref,
    got_ref,
    vel_ref,
    own_hbm,
    ey_h,
    ey_l,
    ex_h,
    ex_l,
    by_h,
    by_l,
    fy_h,
    fy_l,
    out_ref,
    image_ref,
    own_ref,
    vel_tmp,
    sem,
):
    fetch = pltpu.make_async_copy(own_hbm.at[lat_ref[0]], own_ref, sem)
    fetch.start()
    rows = lax.broadcasted_iota(jnp.int32, (128, 128), 0)
    groups = lanes((128, 128)) >> 4
    stacked = []
    for p in range(2):
        value = got_ref[pl.ds(p, 128, stride=2), :]
        for k in (1, 2, 4):
            s_bit, g_bit = (rows & k) != 0, (groups & k) != 0
            down = turned(turned(value, k, 0), -16 * k, 1)
            up = turned(turned(value, -k, 0), 16 * k, 1)
            value = jnp.where(
                s_bit & ~g_bit, down, jnp.where(~s_bit & g_bit, up, value)
            )
        stacked.append(value)
    both = dot3(split(jnp.concatenate(stacked, 0)), (ey_h[...], ey_l[...]))
    along_y = jnp.concatenate(
        [both[:128, :512] - both[128:, 512:], both[:128, 512:] + both[128:, :512]], 0
    )
    along_y = split(along_y)
    fetch.wait()
    own_high, own_both = own_ref[:64], own_ref[...]
    values, refs = references_of(slow_ref, 0)
    row_at = lax.broadcasted_iota(jnp.int32, (HALF, 128), 0)
    kx = row_at.astype(f32) * STEP
    kx_edge = jnp.where(row_at[:8] == 0, 256, row_at[:8]).astype(f32) * STEP
    parts = []
    for q in range(2):
        here = tuple(a[:, 256 * q : 256 * q + 256] for a in along_y)
        spectrum = dot3((ex_h[...], ex_l[...]), here)
        at = 2 * lanes((1, 128)) + q
        at_mirror = jnp.where(at == 0, 256, at) if q == 0 else at
        per_ref = []
        for g in range(2):
            wave = freq_ref[0] * refs[g]
            wave_sq = wave * wave
            ky = at.astype(f32) * STEP
            straight = shift_factor(wave_sq, kx, ky)
            edge = shift_factor(wave_sq, kx_edge, ky)
            if q == 0:
                ky_mirror = at_mirror.astype(f32) * STEP
                straight_m = shift_factor(wave_sq, kx, ky_mirror)
                edge_m = shift_factor(wave_sq, kx_edge, ky_mirror)
            else:
                straight_m, edge_m = straight, edge
            factor = []
            for p in range(2):
                top = jnp.concatenate([straight[p], straight_m[p]], 1)
                border = jnp.concatenate([edge[p], edge_m[p]], 1)
                factor.append(jnp.concatenate([top, border, top[8:]], 0))
            re, im = spectrum[:512], spectrum[512:]
            moved = jnp.concatenate(
                [re * factor[0] - im * factor[1], re * factor[1] + im * factor[0]], 1
            )
            high, low = split(moved)
            with_high = mm(own_both, high)
            total = with_high[:64] + (with_high[64:] + mm(own_high, low))
            per_ref.append(
                (
                    total[:32, :256] - total[32:, 256:],
                    total[:32, 256:] + total[32:, :256],
                )
            )
        parts.append(
            jnp.concatenate([per_ref[g][p] for p in range(2) for g in range(2)], 0)
        )
    field = rows_to_field(0, parts, by_h, by_l, vel_ref, vel_tmp, slow_ref, freq_ref)
    image_ref[...] = field[0]
    stacked = jnp.concatenate(field, 0)
    group = lanes((16, 128)) >> 5
    for q in range(2):
        lower, upper = stacked[:, :HALF], stacked[:, HALF:]
        mixed = lower + upper if q == 0 else lower - upper
        both = dot3(split(mixed), (fy_h[q], fy_l[q]))
        with_cos, with_sin = both[:, :HALF], both[:, HALF:]
        result = (with_cos[:32] + with_sin[32:], with_cos[32:] - with_sin[:32])
        for jj in range(8):
            col, pos = jj // 4, jj % 4
            packed = None
            for p in range(2):
                for h in range(2):
                    piece = result[p][16 * h : 16 * h + 16, 128 * col : 128 * col + 128]
                    piece = turned(piece, 32 * (2 * p + h - pos))
                    packed = piece if packed is None else jnp.where(group == 2 * p + h, piece, packed)
            dest = 2 * jj + q
            out_ref[16 * dest : 16 * dest + 16] = packed


def column_kernel(lat_ref, freq_ref, slow_ref, got_ref, fx_h, fx_l, bx_h, bx_l, out_ref):
    data = got_ref[...]
    lane = lanes((HALF, 128))
    group = lane >> 5
    rolled = [turned(data, 32 * d) for d in range(4)]

    def spread(source):
        out = rolled[(0 - source) % 4]
        for t in range(1, 4):
            out = jnp.where(group == t, rolled[(t - source) % 4], out)
        return out

    found = []
    for h in range(2):
        weights = split(jnp.concatenate([spread(h), spread(2 + h)], 1))
        both = dot3((fx_h[h], fx_l[h]), weights)
        found.append(
            (
                both[:256, :128] + both[256:, 128:],
                both[:256, 128:] - both[256:, :128],
            )
        )
    upper = lane >= 64
    re, im = [
        jnp.where(upper, found[0][p] - found[1][p], found[0][p] + found[1][p]) for p in range(2)
    ]
    values, refs = references_of(slow_ref, 1)
    band = lat_ref[0]
    q, jj = band & 1, band >> 1
    row_lane = lanes((1, 128))
    at = 2 * (32 * (jj & 3) + (row_lane & 31)) + q
    at = jnp.where((at == 0) & (jj >= 4), 256, at)
    ky = at.astype(f32) * STEP
    wave = freq_ref[0] * jnp.where(((row_lane >> 5) & 1) == 1, refs[1], refs[0])
    row_at = lax.broadcasted_iota(jnp.int32, (HALF, 128), 0)
    kx = jnp.where(upper, row_at - 256, row_at).astype(f32) * STEP
    fac_re, fac_im = shift_factor(wave * wave, kx, ky)
    moved_re, moved_im = re * fac_re - im * fac_im, re * fac_im + im * fac_re
    turned_re, turned_im = turned(moved_re, 64), turned(moved_im, 64)
    for h in range(2):
        if h == 0:
            mixed = jnp.where(upper, moved_im + turned_im, moved_re + turned_re)
        else:
            mixed = jnp.where(upper, turned_im - moved_im, moved_re - turned_re)
        both = dot3((bx_h[h], bx_l[h]), split(mixed))
        crossed = turned(both[256:], 64)
        result = both[:256] + jnp.where(upper, crossed, -crossed)
        out_ref[:, h] = result.reshape(16, 16, 128)


def last_kernel(
    freq_ref, slow_ref, got_ref, vel_ref, image_ref, by_h, by_l, wave_ref, out_ref, vel_tmp, wave_tmp
):
    group = lanes((16, 128)) >> 5
    parts = []
    for q in range(2):
        rows = []
        for p in range(2):
            for g in range(2):
                for h in range(2):
                    cols = []
                    for col in range(2):
                        packed = None
                        for pos in range(4):
                            piece = got_ref[2 * (4 * col + pos) + q, h]
                            piece = turned(piece, 32 * (pos - (2 * p + g)))
                            packed = piece if packed is None else jnp.where(group == pos, piece, packed)
                        cols.append(packed)
                    rows.append(jnp.concatenate(cols, 1))
        parts.append(jnp.concatenate(rows, 0))
    field = rows_to_field(1, parts, by_h, by_l, vel_ref, vel_tmp, slow_ref, freq_ref)
    for p in range(2):
        for h in range(2):
            for c in range(4):
                wave_tmp[p, c, pl.ds(h, 16, stride=2), :] = field[p][
                    16 * h : 16 * h + 16, 128 * c : 128 * c + 128
                ]
    for p in range(2):
        wave_ref[p] = jnp.concatenate([wave_tmp[p, c] for c in range(4)], 1)
    upper = lanes((32, 128)) >= 64
    for d in range(8):
        col, pos = d // 2, d % 2
        first = turned(image_ref[:, 128 * col : 128 * col + 128], -64 * pos)
        second = turned(field[0][:, 128 * col : 128 * col + 128], 64 - 64 * pos)
        out_ref[d] = jnp.where(upper, second, first)


def sum_kernel(got_ref, out_ref, image_tmp):
    total = got_ref[0]
    for d in range(1, 8):
        total = total + got_ref[d]
    for h in range(2):
        image_tmp[pl.ds(h, 16, stride=2), :] = total[16 * h : 16 * h + 16]
    total = image_tmp[...]
    out_ref[0] = total[:, :64]
    out_ref[1] = total[:, 64:]


def call(kernel, outs, in_specs, mega, scratch=()):
    many = isinstance(outs, list)
    shapes = [jax.ShapeDtypeStruct(s, f32) for s in (outs if many else [outs])]
    return pl.pallas_call(
        kernel,
        out_shape=shapes if many else shapes[0],
        in_specs=in_specs,
        out_specs=[VM] * len(shapes) if many else VM,
        scratch_shapes=list(scratch),
        compiler_params=pltpu.CompilerParams(vmem_limit_bytes=mega * 1024 * 1024),
    )


def local(spectra, tile_route, bin_in_tile, trace_offset, weights, frequency, slowness, vel_index):
    const = tables()
    lat_at = lax.axis_index("lat").astype(jnp.int32).reshape(1)
    everyone = ("freq", "lat")
    sent = call(route_kernel, (512, 128), [VM] * 5, 24)(
        tile_route.reshape(1, 1024),
        bin_in_tile.reshape(1, 1024),
        trace_offset,
        weights.reshape(1, 1024),
        spectra.reshape(16, 1024),
    )
    got = lax.all_to_all(sent.reshape(128, 4, 128), everyone, 0, 0, tiled=True)
    sent = call(solve_kernel, (256, 128), [VM], 24)(got.reshape(512, 128))
    got = lax.all_to_all(sent.reshape(128, 2, 128), everyone, 0, 0, tiled=True)
    sent, image = call(
        first_kernel,
        [(256, 128), (32, 512)],
        [SM, SM, SM, VM, VM, ANY] + [VM] * 8,
        40,
        [
            pltpu.VMEM((128, 512), bf16),
            pltpu.VMEM((4, 32, 128), jnp.int32),
            pltpu.SemaphoreType.DMA,
        ],
    )(
        lat_at,
        frequency,
        slowness,
        got.reshape(256, 128),
        vel_index,
        const["own"],
        *const["ey"],
        *const["ex"],
        *const["back_y"],
        *const["forth_y"],
    )
    got = lax.all_to_all(sent.reshape(16, 16, 128), "lat", 0, 0, tiled=True)
    sent = call(column_kernel, (16, 2, 16, 128), [SM, SM, SM] + [VM] * 5, 24)(
        lat_at,
        frequency,
        slowness,
        got.reshape(256, 128),
        *const["forth_x"],
        *const["back_x"],
    )
    got = lax.all_to_all(sent.reshape(16, 32, 128), "lat", 0, 0, tiled=True)
    wave, sent = call(
        last_kernel, [(2, 32, 512), (8, 32, 128)],
        [SM, SM] + [VM] * 5,
        24,
        [pltpu.VMEM((4, 32, 128), jnp.int32), pltpu.VMEM((2, 4, 32, 128), f32)],
    )(
        frequency,
        slowness,
        got.reshape(16, 2, 16, 128),
        vel_index,
        image,
        *const["back_y"],
    )
    got = lax.all_to_all(sent, "freq", 0, 0, tiled=True)
    depth_image = call(sum_kernel, (2, 32, 64), [VM], 16, [pltpu.VMEM((32, 128), f32)])(got)
    return (wave.reshape(2, 1, 32, 512), depth_image)


def solution(mesh):
    return jax.shard_map(
        local,
        mesh=mesh,
        in_specs=(
            P(None, None, ("freq", "lat")),
            P(("freq", "lat"), None),
            P(("freq", "lat")),
            P(None, ("freq", "lat")),
            P(("freq", "lat")),
            P("freq"),
            P(),
            P(None, "lat", None),
        ),
        out_specs=(P(None, "freq", "lat", None), P(None, "lat", "freq")),
        check_vma=False,
    )
```

```python
import math

import jax
import jax.numpy as jnp
import ml_dtypes
import numpy as np
from jax import lax
from jax.experimental import pallas as pl
from jax.experimental.pallas import tpu as pltpu
from jax.sharding import PartitionSpec as P

NX = 512
NY = 512
TB = 32
MODES = 8
HALF = 256
SCALE = 1.0 / (NX * NY)
STEP = 2.0 * math.pi / 512

f32 = jnp.float32
bf16 = jnp.bfloat16
VM = pl.BlockSpec(memory_space=pltpu.VMEM)
SM = pl.BlockSpec(memory_space=pltpu.SMEM)
HBM = pl.BlockSpec(memory_space=pltpu.HBM)


def pair(table):
    table = np.asarray(table, np.float32)
    high = table.astype(ml_dtypes.bfloat16)
    low = (table - high.astype(np.float32)).astype(ml_dtypes.bfloat16)
    return high, low


def column_order():
    out = []
    for q in range(2):
        first = 2 * np.arange(128) + q
        mirror = (512 - first) % 512
        if q == 0:
            mirror[0] = 256
        out.append(np.concatenate([first, mirror]))
    return np.stack(out)


def row_order():
    first = np.arange(256)
    mirror = (512 - first) % 512
    mirror[0] = 256
    return np.concatenate([first, mirror])


def angle(left, right):
    return 2.0 * np.pi / 512 * ((left[:, None] * right[None, :]) % 512)


def mode_spectrum(order):
    cell = np.arange(TB)
    modes = np.cos(np.pi * np.arange(MODES)[:, None] * (cell[None, :] + 0.5) / TB)
    place = np.arange(16)[:, None] * TB + cell[None, :]
    wave = np.exp(-2j * np.pi / 512 * ((place[:, :, None] * order[None, None, :]) % 512))
    return np.einsum("aj,yjn->yan", modes, wave).reshape(16 * MODES, -1)


def tables():
    cols, rows = column_order(), row_order()
    every = cols.reshape(-1)
    ey = mode_spectrum(every)
    ey = np.concatenate([ey.real, ey.imag], 1)
    ex = mode_spectrum(rows).T
    ex = np.concatenate(
        [np.concatenate([ex.real, -ex.imag], 1), np.concatenate([ex.imag, ex.real], 1)], 0
    )
    own = []
    for slab in range(16):
        x_at = np.concatenate([32 * slab + 2 * np.arange(16) + h for h in range(2)])
        turn = angle(x_at, rows)
        own.append(np.concatenate([np.cos(turn), np.sin(turn)], 0))
    own_high, own_low = pair(np.stack(own))
    own = np.concatenate([own_high, own_low], 1)
    half = np.arange(HALF)
    back_y, forth_y = [], []
    for q in range(2):
        turn = angle(cols[q], half)
        back_y.append(np.concatenate([np.cos(turn), np.sin(turn)], 1))
        forth_y.append(np.concatenate([np.cos(turn.T), np.sin(turn.T)], 1))
    forth_x, back_x = [], []
    for h in range(2):
        turn = angle(half, 2 * half + h)
        forth_x.append(np.concatenate([np.cos(turn), np.sin(turn)], 0))
        back_x.append(np.concatenate([np.cos(turn.T), np.sin(turn.T)], 0))
    return dict(
        ey=pair(ey),
        ex=pair(ex),
        own=own,
        back_y=pair(np.stack(back_y)),
        forth_y=pair(np.stack(forth_y)),
        forth_x=pair(np.stack(forth_x)),
        back_x=pair(np.stack(back_x)),
    )


def split(value):
    high = value.astype(bf16)
    low = (value - high.astype(f32)).astype(bf16)
    return high, low


def mm(left, right):
    return jnp.dot(left, right, preferred_element_type=f32)


def dot3(left, right):
    return mm(left[0], right[0]) + (mm(left[0], right[1]) + mm(left[1], right[0]))


def lanes(shape):
    return lax.broadcasted_iota(jnp.int32, shape, len(shape) - 1)


def turned(value, shift, axis=1):
    size = value.shape[axis]
    shift = shift % size
    return value if shift == 0 else pltpu.roll(value, shift, axis)


def cos_sin(turn):
    half = 0.5 * turn
    sq = half * half
    cosine = 1.0 / 479001600
    for c in (-1.0 / 3628800, 1.0 / 40320, -1.0 / 720, 1.0 / 24, -0.5, 1.0):
        cosine = cosine * sq + c
    sine = 1.0 / 6227020800
    for c in (-1.0 / 39916800, 1.0 / 362880, -1.0 / 5040, 1.0 / 120, -1.0 / 6, 1.0):
        sine = sine * sq + c
    sine = sine * half
    return 1.0 - 2.0 * sine * sine, 2.0 * sine * cosine


def shift_factor(wave_sq, kx, ky):
    vertical = wave_sq - kx * kx - ky * ky
    root = jnp.sqrt(jnp.abs(vertical))
    cosine, sine = cos_sin(root)
    moving = vertical > 0.0
    return jnp.where(moving, cosine, jnp.exp(-root)), jnp.where(moving, sine, 0.0)


def references_of(slow_ref, step):
    values = [slow_ref[step, i] for i in range(8)]
    refs = [
        (values[4 * g] + values[4 * g + 1] + values[4 * g + 2] + values[4 * g + 3]) * 0.25
        for g in range(2)
    ]
    return values, refs


def velocity_rows(vel_ref, vel_tmp, step):
    for c in range(4):
        vel_tmp[c] = vel_ref[step, :, 128 * c : 128 * c + 128]
    return jnp.concatenate(
        [
            jnp.concatenate([vel_tmp[c, pl.ds(h, 16, stride=2), :] for c in range(4)], 1)
            for h in range(2)
        ],
        0,
    )


def rows_to_field(step, parts, back_high, back_low, vel_ref, vel_tmp, slow_ref, freq_ref):
    halves = []
    for q in range(2):
        both = dot3(split(parts[q]), (back_high[q], back_low[q]))
        with_cos, with_sin = both[:, :HALF], both[:, HALF:]
        halves.append(
            (with_cos[:64] - with_sin[64:], with_cos[64:] + with_sin[:64])
        )
    back = [
        jnp.concatenate([halves[0][p] + halves[1][p], halves[0][p] - halves[1][p]], 1)
        for p in range(2)
    ]
    velocity = velocity_rows(vel_ref, vel_tmp, step)
    values, refs = references_of(slow_ref, step)
    picked = [jnp.where(velocity >= 4, back[p][32:], back[p][:32]) for p in range(2)]
    turn = jnp.zeros(velocity.shape, f32)
    for i in range(8):
        turn = jnp.where(velocity == i, freq_ref[0] * (values[i] - refs[i // 4]), turn)
    cosine, sine = cos_sin(turn)
    cosine, sine = cosine * SCALE, sine * SCALE
    return (
        picked[0] * cosine - picked[1] * sine,
        picked[0] * sine + picked[1] * cosine,
    )


class Fetch:
    def __init__(self, sources, targets, sems):
        self.targets = targets
        self.copies = [
            pltpu.make_async_copy(s, t, sems.at[i]) for i, (s, t) in enumerate(zip(sources, targets))
        ]
        for copy in self.copies:
            copy.start()

    def take(self, *which):
        for i in which:
            self.copies[i].wait()
        out = [self.targets[i] for i in which]
        return out[0] if len(out) == 1 else out


def route_kernel(*refs):
    sources, out_ref, targets, sems = refs[:5], refs[5], refs[6:11], refs[11]
    fetch = Fetch(sources, targets, sems)
    tile = fetch.take(0)[...]
    tile_f = tile.astype(f32)
    below = lax.broadcasted_iota(jnp.int32, (128, 128), 0) < lanes((128, 128))
    columns = []
    ranks = []
    for j in range(8):
        here = tile_f[:, 128 * j : 128 * (j + 1)]
        here_all = jnp.broadcast_to(here, (128, 128))
        columns.append(here_all.T)
        found = jnp.where((columns[j] == here_all) & below, 1.0, 0.0)
        for i in range(j):
            found = found + jnp.where(columns[i] == here_all, 1.0, 0.0)
        ranks.append(jnp.sum(found, axis=0, keepdims=True))
    rank = jnp.concatenate(ranks, 1).astype(jnp.int32)
    row_at = (tile >> 1) * 4 + (rank & 3)
    group_at = (tile & 1) * 2 + (rank >> 2)
    bin_ref, offset_ref, weight_ref, spectra_ref = fetch.take(1, 2, 3, 4)
    place = bin_ref[...]
    cell_x = (place >> 5).astype(f32) + offset_ref[0:1, :]
    cell_y = (place & 31).astype(f32) + offset_ref[1:2, :]
    values = jnp.concatenate(
        [
            spectra_ref[...],
            jnp.concatenate([weight_ref[...], cell_x, cell_y, jnp.zeros((5, 1024), f32)], 0),
            jnp.zeros((8, 1024), f32),
        ],
        0,
    )
    spread = jnp.concatenate([jnp.where(group_at == s, values, 0.0) for s in range(4)], 0)
    high = spread.astype(bf16)
    rest = spread - high.astype(f32)
    mid = rest.astype(bf16)
    low = (rest - mid.astype(f32)).astype(bf16)
    wide = jnp.concatenate([high, mid, low], 0)
    rows = lax.broadcasted_iota(jnp.int32, (512, 1024), 0)
    chosen = jnp.where(rows == row_at, 1.0, 0.0).astype(bf16)
    moved = lax.dot_general(
        chosen, wide, (((1,), (1,)), ((), ())), preferred_element_type=f32
    )
    out_ref[...] = (moved[:, :128] + moved[:, 128:256]) + moved[:, 256:]


def solve_kernel(got_ref, out_ref):
    turned_in = got_ref[...].T
    blocks = []
    mode = lax.broadcasted_iota(jnp.int32, (8, 1024), 0).astype(f32)
    eye_rows = lax.broadcasted_iota(jnp.int32, (64, 128), 0)
    eye = jnp.where(eye_rows == lanes((64, 128)), 1.0, 0.0)
    for t in range(2):
        both = jnp.concatenate(
            [turned_in[64 * t : 64 * t + 24], turned_in[64 * t + 32 : 64 * t + 56]], 1
        )
        along_x = jnp.cos(math.pi * mode * (both[17:18] + 0.5) / TB)
        along_y = jnp.cos(math.pi * mode * (both[18:19] + 0.5) / TB)
        basis = jnp.concatenate([along_x[a : a + 1] * along_y for a in range(8)], 0)
        wide = jnp.concatenate([basis, both[0:16], jnp.zeros((48, 1024), f32)], 0)
        system = lax.dot_general(
            basis * both[16:17],
            wide,
            (((1,), (1,)), ((), ())),
            preferred_element_type=f32,
            precision=lax.Precision.HIGHEST,
        )
        system = system + eye
        blocks.append([system[8 * a : 8 * a + 8] for a in range(8)])
    sub = lax.broadcasted_iota(jnp.int32, (8, 128), 0)
    for j in range(64):
        at, inner = j // 8, j % 8
        for t in range(2):
            mine = blocks[t]
            row = mine[at][inner : inner + 1]
            row = row / row[:, j : j + 1]
            fresh = []
            for a in range(8):
                new = mine[a] - mine[a][:, j : j + 1] * row
                if a == at:
                    new = jnp.where(sub == inner, row, new)
                fresh.append(new)
            blocks[t] = fresh
    stacked = jnp.concatenate([blocks[t][a] for a in range(8) for t in range(2)], 0)
    final = stacked.T
    odd = (lax.broadcasted_iota(jnp.int32, (32, 128), 0) & 1) == 1
    for f in range(8):
        out_ref[32 * f : 32 * f + 32] = jnp.where(
            odd, final[72 + f : 73 + f], final[64 + f : 65 + f]
        )


def first_kernel(
    lat_ref,
    freq_ref,
    slow_ref,
    got_ref,
    *refs,
):
    sources, out_ref, image_ref = refs[:10], refs[10], refs[11]
    targets, vel_tmp, sems = refs[12:22], refs[22], refs[23]
    sources = (*sources[:4], sources[4].at[lat_ref[0]], *sources[5:])
    fetch = Fetch(sources, targets, sems)
    rows = lax.broadcasted_iota(jnp.int32, (128, 128), 0)
    groups = lanes((128, 128)) >> 4
    stacked = []
    for p in range(2):
        value = got_ref[pl.ds(p, 128, stride=2), :]
        for k in (1, 2, 4):
            s_bit, g_bit = (rows & k) != 0, (groups & k) != 0
            down = turned(turned(value, k, 0), -16 * k, 1)
            up = turned(turned(value, -k, 0), 16 * k, 1)
            value = jnp.where(
                s_bit & ~g_bit, down, jnp.where(~s_bit & g_bit, up, value)
            )
        stacked.append(value)
    ey_h, ey_l = fetch.take(0, 1)
    both = dot3(split(jnp.concatenate(stacked, 0)), (ey_h[...], ey_l[...]))
    along_y = jnp.concatenate(
        [both[:128, :512] - both[128:, 512:], both[:128, 512:] + both[128:, :512]], 0
    )
    along_y = split(along_y)
    ex_h, ex_l, own_ref = fetch.take(2, 3, 4)
    own_high, own_both = own_ref[:64], own_ref[...]
    values, refs = references_of(slow_ref, 0)
    row_at = lax.broadcasted_iota(jnp.int32, (HALF, 128), 0)
    kx = row_at.astype(f32) * STEP
    kx_edge = jnp.where(row_at[:8] == 0, 256, row_at[:8]).astype(f32) * STEP
    parts = []
    for q in range(2):
        here = tuple(a[:, 256 * q : 256 * q + 256] for a in along_y)
        spectrum = dot3((ex_h[...], ex_l[...]), here)
        at = 2 * lanes((1, 128)) + q
        at_mirror = jnp.where(at == 0, 256, at) if q == 0 else at
        per_ref = []
        for g in range(2):
            wave = freq_ref[0] * refs[g]
            wave_sq = wave * wave
            ky = at.astype(f32) * STEP
            straight = shift_factor(wave_sq, kx, ky)
            edge = shift_factor(wave_sq, kx_edge, ky)
            if q == 0:
                ky_mirror = at_mirror.astype(f32) * STEP
                straight_m = shift_factor(wave_sq, kx, ky_mirror)
                edge_m = shift_factor(wave_sq, kx_edge, ky_mirror)
            else:
                straight_m, edge_m = straight, edge
            factor = []
            for p in range(2):
                top = jnp.concatenate([straight[p], straight_m[p]], 1)
                border = jnp.concatenate([edge[p], edge_m[p]], 1)
                factor.append(jnp.concatenate([top, border, top[8:]], 0))
            re, im = spectrum[:512], spectrum[512:]
            moved = jnp.concatenate(
                [re * factor[0] - im * factor[1], re * factor[1] + im * factor[0]], 1
            )
            high, low = split(moved)
            with_high = mm(own_both, high)
            total = with_high[:64] + (with_high[64:] + mm(own_high, low))
            per_ref.append(
                (
                    total[:32, :256] - total[32:, 256:],
                    total[:32, 256:] + total[32:, :256],
                )
            )
        parts.append(
            jnp.concatenate([per_ref[g][p] for p in range(2) for g in range(2)], 0)
        )
    vel_ref, by_h, by_l = fetch.take(5, 6, 7)
    field = rows_to_field(0, parts, by_h, by_l, vel_ref, vel_tmp, slow_ref, freq_ref)
    image_ref[...] = field[0]
    stacked = jnp.concatenate(field, 0)
    fy_h, fy_l = fetch.take(8, 9)
    group = lanes((16, 128)) >> 5
    for q in range(2):
        lower, upper = stacked[:, :HALF], stacked[:, HALF:]
        mixed = lower + upper if q == 0 else lower - upper
        both = dot3(split(mixed), (fy_h[q], fy_l[q]))
        with_cos, with_sin = both[:, :HALF], both[:, HALF:]
        result = (with_cos[:32] + with_sin[32:], with_cos[32:] - with_sin[:32])
        for jj in range(8):
            col, pos = jj // 4, jj % 4
            packed = None
            for p in range(2):
                for h in range(2):
                    piece = result[p][16 * h : 16 * h + 16, 128 * col : 128 * col + 128]
                    piece = turned(piece, 32 * (2 * p + h - pos))
                    packed = piece if packed is None else jnp.where(group == 2 * p + h, piece, packed)
            dest = 2 * jj + q
            out_ref[16 * dest : 16 * dest + 16] = packed


def column_kernel(lat_ref, freq_ref, slow_ref, got_ref, fx_h, fx_l, bx_h, bx_l, out_ref):
    data = got_ref[...]
    lane = lanes((HALF, 128))
    group = lane >> 5
    rolled = [turned(data, 32 * d) for d in range(4)]

    def spread(source):
        out = rolled[(0 - source) % 4]
        for t in range(1, 4):
            out = jnp.where(group == t, rolled[(t - source) % 4], out)
        return out

    found = []
    for h in range(2):
        weights = split(jnp.concatenate([spread(h), spread(2 + h)], 1))
        both = dot3((fx_h[h], fx_l[h]), weights)
        found.append(
            (
                both[:256, :128] + both[256:, 128:],
                both[:256, 128:] - both[256:, :128],
            )
        )
    upper = lane >= 64
    re, im = [
        jnp.where(upper, found[0][p] - found[1][p], found[0][p] + found[1][p]) for p in range(2)
    ]
    values, refs = references_of(slow_ref, 1)
    band = lat_ref[0]
    q, jj = band & 1, band >> 1
    row_lane = lanes((1, 128))
    at = 2 * (32 * (jj & 3) + (row_lane & 31)) + q
    at = jnp.where((at == 0) & (jj >= 4), 256, at)
    ky = at.astype(f32) * STEP
    wave = freq_ref[0] * jnp.where(((row_lane >> 5) & 1) == 1, refs[1], refs[0])
    row_at = lax.broadcasted_iota(jnp.int32, (HALF, 128), 0)
    kx = jnp.where(upper, row_at - 256, row_at).astype(f32) * STEP
    fac_re, fac_im = shift_factor(wave * wave, kx, ky)
    moved_re, moved_im = re * fac_re - im * fac_im, re * fac_im + im * fac_re
    turned_re, turned_im = turned(moved_re, 64), turned(moved_im, 64)
    for h in range(2):
        if h == 0:
            mixed = jnp.where(upper, moved_im + turned_im, moved_re + turned_re)
        else:
            mixed = jnp.where(upper, turned_im - moved_im, moved_re - turned_re)
        both = dot3((bx_h[h], bx_l[h]), split(mixed))
        crossed = turned(both[256:], 64)
        result = both[:256] + jnp.where(upper, crossed, -crossed)
        out_ref[:, h] = result.reshape(16, 16, 128)


def last_kernel(
    freq_ref, slow_ref, got_ref, vel_ref, image_ref, by_h, by_l, wave_ref, out_ref, vel_tmp, wave_tmp
):
    group = lanes((16, 128)) >> 5
    parts = []
    for q in range(2):
        rows = []
        for p in range(2):
            for g in range(2):
                for h in range(2):
                    cols = []
                    for col in range(2):
                        packed = None
                        for pos in range(4):
                            piece = got_ref[2 * (4 * col + pos) + q, h]
                            piece = turned(piece, 32 * (pos - (2 * p + g)))
                            packed = piece if packed is None else jnp.where(group == pos, piece, packed)
                        cols.append(packed)
                    rows.append(jnp.concatenate(cols, 1))
        parts.append(jnp.concatenate(rows, 0))
    field = rows_to_field(1, parts, by_h, by_l, vel_ref, vel_tmp, slow_ref, freq_ref)
    for p in range(2):
        for h in range(2):
            for c in range(4):
                wave_tmp[p, c, pl.ds(h, 16, stride=2), :] = field[p][
                    16 * h : 16 * h + 16, 128 * c : 128 * c + 128
                ]
    for p in range(2):
        wave_ref[p] = jnp.concatenate([wave_tmp[p, c] for c in range(4)], 1)
    upper = lanes((32, 128)) >= 64
    for d in range(8):
        col, pos = d // 2, d % 2
        first = turned(image_ref[:, 128 * col : 128 * col + 128], -64 * pos)
        second = turned(field[0][:, 128 * col : 128 * col + 128], 64 - 64 * pos)
        out_ref[d] = jnp.where(upper, second, first)


def sum_kernel(got_ref, out_ref, image_tmp):
    total = got_ref[0]
    for d in range(1, 8):
        total = total + got_ref[d]
    for h in range(2):
        image_tmp[pl.ds(h, 16, stride=2), :] = total[16 * h : 16 * h + 16]
    total = image_tmp[...]
    out_ref[0] = total[:, :64]
    out_ref[1] = total[:, 64:]


def call(kernel, outs, in_specs, mega, scratch=()):
    many = isinstance(outs, list)
    shapes = [jax.ShapeDtypeStruct(s, f32) for s in (outs if many else [outs])]
    return pl.pallas_call(
        kernel,
        out_shape=shapes if many else shapes[0],
        in_specs=in_specs,
        out_specs=[VM] * len(shapes) if many else VM,
        scratch_shapes=list(scratch),
        compiler_params=pltpu.CompilerParams(vmem_limit_bytes=mega * 1024 * 1024),
    )


def local(spectra, tile_route, bin_in_tile, trace_offset, weights, frequency, slowness, vel_index):
    const = tables()
    lat_at = lax.axis_index("lat").astype(jnp.int32).reshape(1)
    everyone = ("freq", "lat")
    sent = call(
        route_kernel,
        (512, 128),
        [HBM] * 5,
        60,
        [
            pltpu.VMEM((1, 1024), jnp.int32),
            pltpu.VMEM((1, 1024), jnp.int32),
            pltpu.VMEM((2, 1024), f32),
            pltpu.VMEM((1, 1024), f32),
            pltpu.VMEM((16, 1024), f32),
            pltpu.SemaphoreType.DMA((5,)),
        ],
    )(
        tile_route.reshape(1, 1024),
        bin_in_tile.reshape(1, 1024),
        trace_offset,
        weights.reshape(1, 1024),
        spectra.reshape(16, 1024),
    )
    got = lax.all_to_all(sent.reshape(128, 4, 128), everyone, 0, 0, tiled=True)
    sent = call(solve_kernel, (256, 128), [VM], 24)(got.reshape(512, 128))
    got = lax.all_to_all(sent.reshape(128, 2, 128), everyone, 0, 0, tiled=True)
    sent, image = call(
        first_kernel,
        [(256, 128), (32, 512)],
        [SM, SM, SM, VM] + [HBM] * 10,
        59,
        [
            pltpu.VMEM((128, 1024), bf16),
            pltpu.VMEM((128, 1024), bf16),
            pltpu.VMEM((1024, 256), bf16),
            pltpu.VMEM((1024, 256), bf16),
            pltpu.VMEM((128, 512), bf16),
            pltpu.VMEM((2, 32, 512), jnp.int32),
            *[pltpu.VMEM((2, 256, 512), bf16)] * 4,
            pltpu.VMEM((4, 32, 128), jnp.int32),
            pltpu.SemaphoreType.DMA((10,)),
        ],
    )(
        lat_at,
        frequency,
        slowness,
        got.reshape(256, 128),
        *const["ey"],
        *const["ex"],
        const["own"],
        vel_index,
        *const["back_y"],
        *const["forth_y"],
    )
    got = lax.all_to_all(sent.reshape(16, 16, 128), "lat", 0, 0, tiled=True)
    sent = call(column_kernel, (16, 2, 16, 128), [SM, SM, SM] + [VM] * 5, 24)(
        lat_at,
        frequency,
        slowness,
        got.reshape(256, 128),
        *const["forth_x"],
        *const["back_x"],
    )
    got = lax.all_to_all(sent.reshape(16, 32, 128), "lat", 0, 0, tiled=True)
    wave, sent = call(
        last_kernel, [(2, 32, 512), (8, 32, 128)],
        [SM, SM] + [VM] * 5,
        24,
        [pltpu.VMEM((4, 32, 128), jnp.int32), pltpu.VMEM((2, 4, 32, 128), f32)],
    )(
        frequency,
        slowness,
        got.reshape(16, 2, 16, 128),
        vel_index,
        image,
        *const["back_y"],
    )
    got = lax.all_to_all(sent, "freq", 0, 0, tiled=True)
    depth_image = call(sum_kernel, (2, 32, 64), [VM], 16, [pltpu.VMEM((32, 128), f32)])(got)
    return (wave.reshape(2, 1, 32, 512), depth_image)


def solution(mesh):
    return jax.shard_map(
        local,
        mesh=mesh,
        in_specs=(
            P(None, None, ("freq", "lat")),
            P(("freq", "lat"), None),
            P(("freq", "lat")),
            P(None, ("freq", "lat")),
            P(("freq", "lat")),
            P("freq"),
            P(),
            P(None, "lat", None),
        ),
        out_specs=(P(None, "freq", "lat", None), P(None, "lat", "freq")),
        check_vma=False,
    )
```

```python
import math

import jax
import jax.numpy as jnp
import ml_dtypes
import numpy as np
from jax import lax
from jax.experimental import pallas as pl
from jax.experimental.pallas import tpu as pltpu
from jax.sharding import PartitionSpec as P

NX = 512
NY = 512
TB = 32
MODES = 8
HALF = 256
SCALE = 1.0 / (NX * NY)
STEP = 2.0 * math.pi / 512

f32 = jnp.float32
bf16 = jnp.bfloat16
VM = pl.BlockSpec(memory_space=pltpu.VMEM)
SM = pl.BlockSpec(memory_space=pltpu.SMEM)
HBM = pl.BlockSpec(memory_space=pltpu.HBM)


def pair(table):
    table = np.asarray(table, np.float32)
    high = table.astype(ml_dtypes.bfloat16)
    low = (table - high.astype(np.float32)).astype(ml_dtypes.bfloat16)
    return np.stack([high, low])


def waves(bins):
    twice = 2 * np.asarray(bins)[None, :] + 1
    index = np.arange(HALF)[:, None]
    sine_index = np.where(index == 0, HALF, index)
    return (
        np.cos(np.pi / 512 * (index * twice % 1024)),
        np.sin(np.pi / 512 * (sine_index * twice % 1024)),
    )


def tables():
    cell = np.arange(TB)
    modes = np.cos(np.pi * np.arange(MODES)[:, None] * (cell[None, :] + 0.5) / TB)
    cosine, sine = waves(np.arange(512))
    along = [
        np.einsum("aj,iyj->yai", modes, t.reshape(HALF, 16, TB)).reshape(16 * MODES, HALF)
        for t in (cosine, sine)
    ]
    along = np.concatenate(along, 1)
    own = np.concatenate(
        [pair(t.reshape(HALF, 16, 32).transpose(1, 2, 0)) for t in (cosine, sine)], 0
    )
    own = own.transpose(1, 0, 2, 3).reshape(16, 128, HALF)
    first = [cosine[:, :HALF], sine[:, :HALF]]
    late = [cosine[:, HALF:], sine[:, HALF:]]
    waves_all = pair(np.stack([*first, *[t.T for t in first], *late]))
    return dict(along_y=pair(along), along_x=pair(along.T), own=own, waves=waves_all)


def split(value):
    high = value.astype(bf16)
    low = (value - high.astype(f32)).astype(bf16)
    return high, low


def mm(left, right):
    return jnp.dot(left, right, preferred_element_type=f32)


def dot3(left, right):
    return mm(left[0], right[0]) + (mm(left[0], right[1]) + mm(left[1], right[0]))


def lanes(shape):
    return lax.broadcasted_iota(jnp.int32, shape, len(shape) - 1)


def turned(value, shift, axis=1):
    size = value.shape[axis]
    shift = shift % size
    return value if shift == 0 else pltpu.roll(value, shift, axis)


def cos_sin(turn):
    half = 0.5 * turn
    sq = half * half
    cosine = 1.0 / 479001600
    for c in (-1.0 / 3628800, 1.0 / 40320, -1.0 / 720, 1.0 / 24, -0.5, 1.0):
        cosine = cosine * sq + c
    sine = 1.0 / 6227020800
    for c in (-1.0 / 39916800, 1.0 / 362880, -1.0 / 5040, 1.0 / 120, -1.0 / 6, 1.0):
        sine = sine * sq + c
    sine = sine * half
    return 1.0 - 2.0 * sine * sine, 2.0 * sine * cosine


def shift_factor(wave_sq, kx, ky):
    vertical = wave_sq - kx * kx - ky * ky
    root = jnp.sqrt(jnp.abs(vertical))
    cosine, sine = cos_sin(root)
    moving = vertical > 0.0
    return jnp.where(moving, cosine, jnp.exp(-root)), jnp.where(moving, sine, 0.0)


def references_of(slow_ref, step):
    values = [slow_ref[step, i] for i in range(8)]
    refs = [
        (values[4 * g] + values[4 * g + 1] + values[4 * g + 2] + values[4 * g + 3]) * 0.25
        for g in range(2)
    ]
    return values, refs


def split_turns(velocity, step, slow_ref, freq_ref):
    values, refs = references_of(slow_ref, step)
    pairs = [cos_sin(freq_ref[0] * (values[i] - refs[i // 4])) for i in range(8)]
    low, mid, top = (velocity & 1) == 1, (velocity & 2) == 2, velocity >= 4
    out = []
    for p in range(2):
        level = [pairs[i][p] * SCALE for i in range(8)]
        level = [jnp.where(low, level[2 * i + 1], level[2 * i]) for i in range(4)]
        level = [jnp.where(mid, level[2 * i + 1], level[2 * i]) for i in range(2)]
        out.append(jnp.where(top, level[1], level[0]))
    return out[0], out[1], top


def no_first(value, axis):
    at = lax.broadcasted_iota(jnp.int32, value.shape, axis)
    return jnp.where(at > 0, value, 0.0)


def plus_i(u, v):
    return u[0] - v[1], u[1] + v[0]


def minus_i(u, v):
    return u[0] + v[1], u[1] - v[0]


def halves_of(value, axis, count):
    if axis == 0:
        return value[:count], value[count:]
    return value[:, :count], value[:, count:]


class Fetch:
    def __init__(self, sources, targets, sems):
        self.targets = targets
        self.copies = [
            pltpu.make_async_copy(s, t, sems.at[i]) for i, (s, t) in enumerate(zip(sources, targets))
        ]
        for copy in self.copies:
            copy.start()

    def take(self, *which):
        for i in which:
            self.copies[i].wait()
        out = [self.targets[i] for i in which]
        return out[0] if len(out) == 1 else out


def route_kernel(lat_ref, *refs):
    sources, out_ref, vel_ref = refs[:6], refs[6], refs[7]
    targets, sems = refs[8:14], refs[14]
    fetch = Fetch([*sources[:5], sources[5].at[0]], targets, sems)
    tile = fetch.take(0)[...]
    tile_f = tile.astype(f32)
    below = lax.broadcasted_iota(jnp.int32, (128, 128), 0) < lanes((128, 128))
    columns = []
    ranks = []
    for j in range(8):
        here = tile_f[:, 128 * j : 128 * (j + 1)]
        here_all = jnp.broadcast_to(here, (128, 128))
        columns.append(here_all.T)
        found = jnp.where((columns[j] == here_all) & below, 1.0, 0.0)
        for i in range(j):
            found = found + jnp.where(columns[i] == here_all, 1.0, 0.0)
        ranks.append(jnp.sum(found, axis=0, keepdims=True))
    rank = jnp.concatenate(ranks, 1).astype(jnp.int32)
    row_at = (tile >> 1) * 4 + (rank & 3)
    group_at = (tile & 1) * 2 + (rank >> 2)
    bin_ref, offset_ref, weight_ref, spectra_ref = fetch.take(1, 2, 3, 4)
    place = bin_ref[...]
    cell_x = (place >> 5).astype(f32) + offset_ref[0:1, :]
    cell_y = (place & 31).astype(f32) + offset_ref[1:2, :]
    values = jnp.concatenate(
        [
            spectra_ref[...],
            jnp.concatenate([weight_ref[...], cell_x, cell_y, jnp.zeros((5, 1024), f32)], 0),
            jnp.zeros((8, 1024), f32),
        ],
        0,
    )
    spread = jnp.concatenate([jnp.where(group_at == s, values, 0.0) for s in range(4)], 0)
    high = spread.astype(bf16)
    rest = spread - high.astype(f32)
    mid = rest.astype(bf16)
    low = (rest - mid.astype(f32)).astype(bf16)
    wide = jnp.concatenate([high, mid, low], 0)
    rows = lax.broadcasted_iota(jnp.int32, (512, 1024), 0)
    chosen = jnp.where(rows == row_at, 1.0, 0.0).astype(bf16)
    moved = lax.dot_general(
        chosen, wide, (((1,), (1,)), ((), ())), preferred_element_type=f32
    )
    out_ref[...] = (moved[:, :128] + moved[:, 128:256]) + moved[:, 256:]
    velocity = fetch.take(5)[...].astype(f32).astype(bf16)
    at = lax.broadcasted_iota(jnp.int32, (HALF, HALF), 0)
    flip = jnp.where(at + lanes((HALF, HALF)) == HALF - 1, 1.0, 0.0).astype(bf16)
    right = mm(velocity[:, HALF:], flip).astype(bf16)
    velocity = jnp.concatenate([velocity[:, :HALF], right], 1)
    at, along = lax.broadcasted_iota(jnp.int32, (32, 32), 0), lanes((32, 32))
    target = jnp.where(lat_ref[0] >= 8, 31 - at, at)
    vel_ref[...] = mm(jnp.where(along == target, 1.0, 0.0).astype(bf16), velocity)


def solve_kernel(lat_ref, got_ref, *refs):
    slabs, out_ref, four_ref, sems = refs[:4], refs[4], refs[5], refs[6]
    fetch = Fetch(slabs, [four_ref.at[(lat_ref[0] & 3) ^ d] for d in range(4)], sems)
    turned_in = got_ref[...].T
    blocks = []
    mode = lax.broadcasted_iota(jnp.int32, (8, 1024), 0).astype(f32)
    eye_rows = lax.broadcasted_iota(jnp.int32, (64, 128), 0)
    eye = jnp.where(eye_rows == lanes((64, 128)), 1.0, 0.0)
    for t in range(2):
        both = jnp.concatenate(
            [turned_in[64 * t : 64 * t + 24], turned_in[64 * t + 32 : 64 * t + 56]], 1
        )
        along_x = jnp.cos(math.pi * mode * (both[17:18] + 0.5) / TB)
        along_y = jnp.cos(math.pi * mode * (both[18:19] + 0.5) / TB)
        basis = jnp.concatenate([along_x[a : a + 1] * along_y for a in range(8)], 0)
        wide = jnp.concatenate([basis, both[0:16], jnp.zeros((48, 1024), f32)], 0)
        system = lax.dot_general(
            basis * both[16:17],
            wide,
            (((1,), (1,)), ((), ())),
            preferred_element_type=f32,
            precision=lax.Precision.HIGHEST,
        )
        system = system + eye
        blocks.append([system[8 * a : 8 * a + 8] for a in range(8)])
    sub = lax.broadcasted_iota(jnp.int32, (8, 128), 0)
    for j in range(64):
        at, inner = j // 8, j % 8
        for t in range(2):
            mine = blocks[t]
            row = mine[at][inner : inner + 1]
            row = row / row[:, j : j + 1]
            fresh = []
            for a in range(8):
                new = mine[a] - mine[a][:, j : j + 1] * row
                if a == at:
                    new = jnp.where(sub == inner, row, new)
                fresh.append(new)
            blocks[t] = fresh
    stacked = jnp.concatenate([blocks[t][a] for a in range(8) for t in range(2)], 0)
    final = stacked.T
    odd = (lax.broadcasted_iota(jnp.int32, (32, 128), 0) & 1) == 1
    for f in range(8):
        out_ref[32 * f : 32 * f + 32] = jnp.where(
            odd, final[72 + f : 73 + f], final[64 + f : 65 + f]
        )
    fetch.take(0, 1, 2, 3)


def factor_kernel(freq_ref, slow_ref, factor_ref, edge_ref):
    at = lanes((1, HALF))
    ky = at.astype(f32) * STEP
    ky_mirror = jnp.where(at[:, :128] == 0, 256, at[:, :128]).astype(f32) * STEP
    for step in range(2):
        values, refs = references_of(slow_ref, step)
        for g in range(2):
            wave = freq_ref[0] * refs[g]
            wave_sq = wave * wave

            def rows_of(kx):
                first = shift_factor(wave_sq, kx, ky)
                mirror = shift_factor(wave_sq, kx[:, :128], ky_mirror)
                return [
                    jnp.concatenate([first[p], mirror[p], first[p][:, 128:]], 1) for p in range(2)
                ]

            def some_rows(k, carry):
                start = pl.multiple_of(k * 32, 32)
                kx = (lax.broadcasted_iota(jnp.int32, (32, HALF), 0) + start).astype(f32) * STEP
                found = rows_of(kx)
                for p in range(2):
                    factor_ref[step, g, p, pl.ds(start, 32), :] = found[p]
                return carry

            lax.fori_loop(0, 8, some_rows, 0)
            at_row = lax.broadcasted_iota(jnp.int32, (8, HALF), 0)
            found = rows_of(jnp.where(at_row == 0, 256, at_row).astype(f32) * STEP)
            for p in range(2):
                edge_ref[step, g, p] = found[p]


def store_spectrum(spec_ref, u, v, cols):
    first = minus_i(u, [no_first(t, 0) for t in v])
    second = plus_i([no_first(t, 0) for t in u], v)
    for k, value in enumerate((*first, *second)):
        spec_ref[k, :, cols] = value


def wave_pair(waves_ref, which):
    return waves_ref[0, which], waves_ref[1, which]


def own_dot(own_ref, rows_at, value):
    with_high = mm(own_ref[rows_at : rows_at + 64], value[0])
    return with_high[:32] + (with_high[32:] + mm(own_ref[rows_at : rows_at + 32], value[1]))


def invert_x(spec_ref, factor_ref, edge_ref, own_ref, own_back, g, cols):
    fac = [factor_ref[g, p, :, cols] for p in range(2)]
    fac_edge = [jnp.concatenate([edge_ref[g, p, :, cols], fac[p][8:]], 0) for p in range(2)]
    s = [spec_ref[i, :, cols] for i in range(4)]
    up = (s[0] * fac[0] - s[1] * fac[1], s[0] * fac[1] + s[1] * fac[0])
    down = (s[2] * fac_edge[0] - s[3] * fac_edge[1], s[2] * fac_edge[1] + s[3] * fac_edge[0])
    even = split(jnp.concatenate([up[p] + no_first(down[p], 0) for p in range(2)], 1))
    odd = split(jnp.concatenate([no_first(up[p], 0) - down[p] for p in range(2)], 1))
    mine = plus_i(
        halves_of(own_dot(own_ref, 0, even), 1, HALF),
        halves_of(own_dot(own_ref, 64, odd), 1, HALF),
    )
    for p in range(2):
        own_back[g, 32 * p : 32 * p + 32, cols] = mine[p]
    return even, odd


def fold_columns(value):
    left, right = value[:, :HALF], value[:, HALF:]
    return split(left + no_first(right, 1)), split(no_first(left, 1) - right)


def own_field(step, own_back, waves_ref, velocity, slow_ref, freq_ref):
    even, odd = fold_columns(jnp.concatenate([own_back[0], own_back[1]], 0))
    sides = []
    for at in (0, 4):
        u, v = dot3(even, wave_pair(waves_ref, at)), dot3(odd, wave_pair(waves_ref, at + 1))
        sides.append(
            [
                plus_i(
                    halves_of(u[64 * g : 64 * g + 64], 0, 32),
                    halves_of(v[64 * g : 64 * g + 64], 0, 32),
                )
                for g in range(2)
            ]
        )
    back = [
        [jnp.concatenate([sides[0][g][p], sides[1][g][p]], 1) for p in range(2)] for g in range(2)
    ]
    cosine, sine, top = split_turns(velocity, step, slow_ref, freq_ref)
    picked = [jnp.where(top, back[1][p], back[0][p]) for p in range(2)]
    return (
        picked[0] * cosine - picked[1] * sine,
        picked[0] * sine + picked[1] * cosine,
    )


def first_kernel(lat_ref, freq_ref, slow_ref, got_ref, *refs):
    sources, image_ref, back_hbm = refs[:7], refs[7], refs[8]
    targets, sems, out_sems = refs[9:16], refs[16], refs[17]
    spec_ref, own_back, back_ref = refs[18:]
    fetch = Fetch(
        [
            *sources[:2],
            sources[2].at[lat_ref[0]],
            sources[3].at[0],
            sources[4].at[0],
            sources[5],
            sources[6].at[0],
        ],
        targets,
        sems,
    )
    rows = lax.broadcasted_iota(jnp.int32, (128, 128), 0)
    groups = lanes((128, 128)) >> 4
    stacked = []
    for p in range(2):
        value = got_ref[pl.ds(p, 128, stride=2), :]
        for k in (1, 2, 4):
            s_bit, g_bit = (rows & k) != 0, (groups & k) != 0
            down = turned(turned(value, k, 0), -16 * k, 1)
            up = turned(turned(value, -k, 0), 16 * k, 1)
            value = jnp.where(
                s_bit & ~g_bit, down, jnp.where(~s_bit & g_bit, up, value)
            )
        stacked.append(value)
    table = fetch.take(0)
    both = dot3(split(jnp.concatenate(stacked, 0)), (table[0], table[1]))
    u, v = (halves_of(t, 0, 128) for t in (both[:, :HALF], both[:, HALF:]))
    first = minus_i(u, [no_first(t, 1) for t in v])
    second = plus_i([no_first(t, 1) for t in u], v)
    table = fetch.take(1)
    for c, here in enumerate((first, second)):
        both = dot3((table[0], table[1]), split(jnp.concatenate(here, 1)))
        store_spectrum(
            spec_ref,
            halves_of(both[:HALF], 1, HALF),
            halves_of(both[HALF:], 1, HALF),
            pl.ds(HALF * c, HALF),
        )
    own_ref, factor_ref, edge_ref, waves_ref = fetch.take(2, 3, 4, 5)
    leaving = []
    for g in range(2):
        for c in range(2):
            cols = pl.ds(HALF * c, HALF)
            even, odd = invert_x(spec_ref, factor_ref, edge_ref, own_ref, own_back, g, cols)
            u = halves_of(dot3(wave_pair(waves_ref, 2), even), 1, HALF)
            v = halves_of(dot3(wave_pair(waves_ref, 3), odd), 1, HALF)
            first, second = plus_i(u, v), minus_i(u, v)
            for p in range(2):
                back_ref[g, p, :HALF, cols] = first[p]
                back_ref[g, p, HALF:, cols] = second[p]
            copy = pltpu.make_async_copy(
                back_ref.at[g, :, :, cols], back_hbm.at[g, :, :, cols], out_sems.at[2 * g + c]
            )
            copy.start()
            leaving.append(copy)
    vel_ref = fetch.take(6)
    image_ref[...] = own_field(0, own_back, waves_ref, vel_ref[...], slow_ref, freq_ref)[0]
    for copy in leaving:
        copy.wait()


def second_kernel(lat_ref, freq_ref, slow_ref, image_ref, *refs):
    slabs, refs = refs[:4], refs[4:]
    sources, wave_ref, out_ref = refs[:6], refs[6], refs[7]
    targets, slabs_ref, sems, back_sems = refs[8:13], refs[13], refs[14], refs[15]
    back_ref, spec_ref, own_back, half_ref = refs[16:]

    def arriving(k):
        at = pl.ds(pl.multiple_of(k * 128, 128), 128)
        return pltpu.make_async_copy(
            sources[0].at[:, :, at, :], back_ref.at[:, :, at, :], back_sems.at[k]
        )

    arriving(0).start()
    fetch = Fetch(
        [
            sources[1],
            *slabs,
            sources[2].at[1],
            sources[3].at[1],
            sources[4].at[lat_ref[0]],
            sources[5].at[1],
        ],
        [targets[0], *[slabs_ref.at[(lat_ref[0] >> 2) ^ d] for d in range(4)], *targets[1:]],
        sems,
    )
    for k in range(1, 4):
        arriving(k).start()
    waves_ref = fetch.take(*range(5))[0]

    def some_rows(k, carry):
        arriving(k).wait()
        at = pl.ds(pl.multiple_of(k * 128, 128), 128)
        back = []
        for g in range(2):
            even, odd = fold_columns(
                jnp.concatenate([back_ref[g, p, at, :] for p in range(2)], 0)
            )
            u = halves_of(dot3(even, wave_pair(waves_ref, 0)), 0, 128)
            v = halves_of(dot3(odd, wave_pair(waves_ref, 1)), 0, 128)
            back.append((plus_i(u, v), minus_i(u, v)))
        slabs = [
            slabs_ref[jnp.where(k < 2, k, 5 - k), jnp.where(k < 2, i, 3 - i)] for i in range(4)
        ]
        velocity = jnp.concatenate(slabs, 0).astype(jnp.int32)
        fields = []
        for side in range(2):
            cosine, sine, top = split_turns(
                velocity[:, HALF * side : HALF * side + HALF], 0, slow_ref, freq_ref
            )
            picked = [jnp.where(top, back[1][side][p], back[0][side][p]) for p in range(2)]
            fields.append(
                jnp.concatenate(
                    [
                        picked[0] * cosine - picked[1] * sine,
                        picked[0] * sine + picked[1] * cosine,
                    ],
                    0,
                )
            )
        u = halves_of(dot3(split(fields[0] + fields[1]), wave_pair(waves_ref, 2)), 0, 128)
        v = halves_of(dot3(split(fields[0] - fields[1]), wave_pair(waves_ref, 3)), 0, 128)
        first = minus_i(u, [no_first(t, 1) for t in v])
        second = plus_i([no_first(t, 1) for t in u], v)
        for p in range(2):
            half_ref[p, at, :HALF] = first[p]
            half_ref[p, at, HALF:] = second[p]
        return carry

    lax.fori_loop(0, 4, some_rows, 0)

    def some_columns(c, carry):
        cols = pl.ds(pl.multiple_of(c * HALF, HALF), HALF)
        top = jnp.concatenate([half_ref[p, :HALF, cols] for p in range(2)], 1)
        low = jnp.concatenate([half_ref[p, HALF:, cols] for p in range(2)], 1)
        u = halves_of(dot3(wave_pair(waves_ref, 0), split(top + low)), 1, HALF)
        v = halves_of(dot3(wave_pair(waves_ref, 1), split(top - low)), 1, HALF)
        store_spectrum(spec_ref, u, v, cols)
        return carry

    lax.fori_loop(0, 2, some_columns, 0)
    factor_ref, edge_ref, own_ref, vel_ref = fetch.take(5, 6, 7, 8)

    def invert(k, carry):
        cols = pl.ds(pl.multiple_of((k & 1) * HALF, HALF), HALF)
        invert_x(spec_ref, factor_ref, edge_ref, own_ref, own_back, k >> 1, cols)
        return carry

    lax.fori_loop(0, 4, invert, 0)
    field = own_field(1, own_back, waves_ref, vel_ref[...], slow_ref, freq_ref)
    for p in range(2):
        wave_ref[p] = field[p]
    upper = lanes((32, 128)) >= 64
    image = image_ref[...]
    for d in range(8):
        col, pos = d // 2, d % 2
        first = turned(image[:, 128 * col : 128 * col + 128], -64 * pos)
        second = turned(field[0][:, 128 * col : 128 * col + 128], 64 - 64 * pos)
        out_ref[d] = jnp.where(upper, second, first)


def sum_kernel(got_ref, out_ref):
    total = got_ref[0]
    for d in range(1, 8):
        total = total + got_ref[d]
    out_ref[0] = total[:, :64]
    out_ref[1] = total[:, 64:]


def call(kernel, outs, in_specs, mega, scratch=(), out_specs=None):
    many = isinstance(outs, list)
    shapes = [jax.ShapeDtypeStruct(s, f32) for s in (outs if many else [outs])]
    return pl.pallas_call(
        kernel,
        out_shape=shapes if many else shapes[0],
        in_specs=in_specs,
        out_specs=out_specs or ([VM] * len(shapes) if many else VM),
        scratch_shapes=list(scratch),
        compiler_params=pltpu.CompilerParams(vmem_limit_bytes=mega * 1024 * 1024),
    )


def local(spectra, tile_route, bin_in_tile, trace_offset, weights, frequency, slowness, vel_index):
    const = tables()
    lat_at = lax.axis_index("lat").astype(jnp.int32).reshape(1)
    everyone = ("freq", "lat")
    sent, velocity = call(
        route_kernel,
        [(512, 128), (32, 512)],
        [SM] + [HBM] * 6,
        60,
        [
            pltpu.VMEM((1, 1024), jnp.int32),
            pltpu.VMEM((1, 1024), jnp.int32),
            pltpu.VMEM((2, 1024), f32),
            pltpu.VMEM((1, 1024), f32),
            pltpu.VMEM((16, 1024), f32),
            pltpu.VMEM((32, 512), jnp.int32),
            pltpu.SemaphoreType.DMA((6,)),
        ],
    )(
        lat_at,
        tile_route.reshape(1, 1024),
        bin_in_tile.reshape(1, 1024),
        trace_offset,
        weights.reshape(1, 1024),
        spectra.reshape(16, 1024),
        vel_index,
    )
    got = lax.all_to_all(sent.reshape(128, 4, 128), everyone, 0, 0, tiled=True)
    slabs = [velocity] + [
        lax.ppermute(velocity, "lat", [(i, i ^ d) for i in range(16)]) for d in (1, 2, 3)
    ]
    sent, slabs = call(
        solve_kernel,
        [(256, 128), (4, 32, 512)],
        [SM, VM] + [HBM] * 4,
        24,
        [pltpu.SemaphoreType.DMA((4,))],
        [VM, HBM],
    )(lat_at, got.reshape(512, 128), *slabs)
    got = lax.all_to_all(sent.reshape(128, 2, 128), everyone, 0, 0, tiled=True)
    slabs = [slabs] + [
        lax.ppermute(slabs, "lat", [(i, i ^ d) for i in range(16)]) for d in (4, 8, 12)
    ]
    factor, edge = call(
        factor_kernel, [(2, 2, 2, 256, 512), (2, 2, 2, 8, 512)], [SM, SM], 59
    )(frequency, slowness)
    image, back = call(
        first_kernel,
        [(32, 512), (2, 2, 512, 512)],
        [SM, SM, SM, VM] + [HBM] * 7,
        59,
        [
            pltpu.VMEM((2, 128, 512), bf16),
            pltpu.VMEM((2, 512, 128), bf16),
            pltpu.VMEM((128, 256), bf16),
            pltpu.VMEM((2, 2, 256, 512), f32),
            pltpu.VMEM((2, 2, 8, 512), f32),
            pltpu.VMEM((2, 6, 256, 256), bf16),
            pltpu.VMEM((32, 512), jnp.int32),
            pltpu.SemaphoreType.DMA((7,)),
            pltpu.SemaphoreType.DMA((4,)),
            pltpu.VMEM((4, 256, 512), f32),
            pltpu.VMEM((2, 64, 512), f32),
            pltpu.VMEM((2, 2, 512, 512), f32),
        ],
        [VM, HBM],
    )(
        lat_at,
        frequency,
        slowness,
        got.reshape(256, 128),
        const["along_y"],
        const["along_x"],
        const["own"],
        factor,
        edge,
        const["waves"],
        vel_index,
    )
    wave, sent = call(
        second_kernel,
        [(2, 32, 512), (8, 32, 128)],
        [SM, SM, SM, VM] + [HBM] * 10,
        59,
        [
            pltpu.VMEM((2, 6, 256, 256), bf16),
            pltpu.VMEM((2, 2, 256, 512), f32),
            pltpu.VMEM((2, 2, 8, 512), f32),
            pltpu.VMEM((128, 256), bf16),
            pltpu.VMEM((32, 512), jnp.int32),
            pltpu.VMEM((4, 4, 32, 512), f32),
            pltpu.SemaphoreType.DMA((9,)),
            pltpu.SemaphoreType.DMA((4,)),
            pltpu.VMEM((2, 2, 512, 512), f32),
            pltpu.VMEM((4, 256, 512), f32),
            pltpu.VMEM((2, 64, 512), f32),
            pltpu.VMEM((2, 512, 512), f32),
        ],
    )(
        lat_at,
        frequency,
        slowness,
        image,
        *slabs,
        back,
        const["waves"],
        factor,
        edge,
        const["own"],
        vel_index,
    )
    got = lax.all_to_all(sent, "freq", 0, 0, tiled=True)
    depth_image = call(sum_kernel, (2, 32, 64), [VM], 16)(got)
    return (wave.reshape(2, 1, 32, 512), depth_image)


def solution(mesh):
    return jax.shard_map(
        local,
        mesh=mesh,
        in_specs=(
            P(None, None, ("freq", "lat")),
            P(("freq", "lat"), None),
            P(("freq", "lat")),
            P(None, ("freq", "lat")),
            P(("freq", "lat")),
            P("freq"),
            P(),
            P(None, "lat", None),
        ),
        out_specs=(P(None, "freq", "lat", None), P(None, "lat", "freq")),
        check_vma=False,
    )
```

```python
import math

import jax
import jax.numpy as jnp
import ml_dtypes
import numpy as np
from jax import lax
from jax.experimental import pallas as pl
from jax.experimental.pallas import tpu as pltpu
from jax.sharding import PartitionSpec as P

NX = 512
NY = 512
TB = 32
MODES = 8
HALF = 256
SCALE = 1.0 / (NX * NY)
STEP = 2.0 * math.pi / 512

f32 = jnp.float32
bf16 = jnp.bfloat16
VM = pl.BlockSpec(memory_space=pltpu.VMEM)
SM = pl.BlockSpec(memory_space=pltpu.SMEM)
HBM = pl.BlockSpec(memory_space=pltpu.HBM)


def pair(table):
    table = np.asarray(table, np.float32)
    high = table.astype(ml_dtypes.bfloat16)
    low = (table - high.astype(np.float32)).astype(ml_dtypes.bfloat16)
    return np.stack([high, low])


def waves(bins):
    twice = 2 * np.asarray(bins)[None, :] + 1
    index = np.arange(HALF)[:, None]
    sine_index = np.where(index == 0, HALF, index)
    return (
        np.cos(np.pi / 512 * (index * twice % 1024)),
        np.sin(np.pi / 512 * (sine_index * twice % 1024)),
    )


def tables():
    cell = np.arange(TB)
    modes = np.cos(np.pi * np.arange(MODES)[:, None] * (cell[None, :] + 0.5) / TB)
    cosine, sine = waves(np.arange(512))
    along = [
        np.einsum("aj,iyj->yai", modes, t.reshape(HALF, 16, TB)).reshape(16 * MODES, HALF)
        for t in (cosine, sine)
    ]
    along = np.concatenate(along, 1)
    own = np.concatenate(
        [pair(t.reshape(HALF, 16, 32).transpose(1, 2, 0)) for t in (cosine, sine)], 0
    )
    own = own.transpose(1, 0, 2, 3).reshape(16, 128, HALF)
    first = [cosine[:, :HALF], sine[:, :HALF]]
    late = [cosine[:, HALF:], sine[:, HALF:]]
    waves_all = pair(np.stack([*first, *[t.T for t in first], *late]))
    return dict(along_y=pair(along), along_x=pair(along.T), own=own, waves=waves_all)


def split(value):
    high = value.astype(bf16)
    low = (value - high.astype(f32)).astype(bf16)
    return high, low


def mm(left, right):
    return jnp.dot(left, right, preferred_element_type=f32)


def dot3(left, right):
    return mm(
        jnp.concatenate([left[0], left[1], left[0]], 1),
        jnp.concatenate([right[0], right[0], right[1]], 0),
    )


def lanes(shape):
    return lax.broadcasted_iota(jnp.int32, shape, len(shape) - 1)


def turned(value, shift, axis=1):
    size = value.shape[axis]
    shift = shift % size
    return value if shift == 0 else pltpu.roll(value, shift, axis)


def cos_sin(turn):
    half = 0.5 * turn
    sq = half * half
    cosine = 1.0 / 479001600
    for c in (-1.0 / 3628800, 1.0 / 40320, -1.0 / 720, 1.0 / 24, -0.5, 1.0):
        cosine = cosine * sq + c
    sine = 1.0 / 6227020800
    for c in (-1.0 / 39916800, 1.0 / 362880, -1.0 / 5040, 1.0 / 120, -1.0 / 6, 1.0):
        sine = sine * sq + c
    sine = sine * half
    return 1.0 - 2.0 * sine * sine, 2.0 * sine * cosine


def shift_factor(wave_sq, kx, ky):
    vertical = wave_sq - kx * kx - ky * ky
    root = jnp.sqrt(jnp.abs(vertical))
    cosine, sine = cos_sin(root)
    moving = vertical > 0.0
    return jnp.where(moving, cosine, jnp.exp(-root)), jnp.where(moving, sine, 0.0)


def references_of(slow_ref, step):
    values = [slow_ref[step, i] for i in range(8)]
    refs = [
        (values[4 * g] + values[4 * g + 1] + values[4 * g + 2] + values[4 * g + 3]) * 0.25
        for g in range(2)
    ]
    return values, refs


def split_turns(velocity, step, slow_ref, freq_ref):
    values, refs = references_of(slow_ref, step)
    pairs = [cos_sin(freq_ref[0] * (values[i] - refs[i // 4])) for i in range(8)]
    low, mid, top = (velocity & 1) == 1, (velocity & 2) == 2, velocity >= 4
    out = []
    for p in range(2):
        level = [pairs[i][p] * SCALE for i in range(8)]
        level = [jnp.where(low, level[2 * i + 1], level[2 * i]) for i in range(4)]
        level = [jnp.where(mid, level[2 * i + 1], level[2 * i]) for i in range(2)]
        out.append(jnp.where(top, level[1], level[0]))
    return out[0], out[1], top


def no_first(value, axis):
    at = lax.broadcasted_iota(jnp.int32, value.shape, axis)
    return jnp.where(at > 0, value, 0.0)


def plus_i(u, v):
    return u[0] - v[1], u[1] + v[0]


def minus_i(u, v):
    return u[0] + v[1], u[1] - v[0]


def halves_of(value, axis, count):
    if axis == 0:
        return value[:count], value[count:]
    return value[:, :count], value[:, count:]


class Fetch:
    def __init__(self, sources, targets, sems):
        self.targets = targets
        self.copies = [
            pltpu.make_async_copy(s, t, sems.at[i]) for i, (s, t) in enumerate(zip(sources, targets))
        ]
        for copy in self.copies:
            copy.start()

    def take(self, *which):
        for i in which:
            self.copies[i].wait()
        out = [self.targets[i] for i in which]
        return out[0] if len(out) == 1 else out


def route_kernel(lat_ref, *refs):
    sources, out_ref, vel_ref = refs[:6], refs[6], refs[7]
    targets, sems = refs[8:14], refs[14]
    fetch = Fetch([*sources[:5], sources[5].at[0]], targets, sems)
    tile = fetch.take(0)[...]
    tile_f = tile.astype(f32)
    below = lax.broadcasted_iota(jnp.int32, (128, 128), 0) < lanes((128, 128))
    columns = []
    ranks = []
    for j in range(8):
        here = tile_f[:, 128 * j : 128 * (j + 1)]
        here_all = jnp.broadcast_to(here, (128, 128))
        columns.append(here_all.T)
        found = jnp.where((columns[j] == here_all) & below, 1.0, 0.0)
        for i in range(j):
            found = found + jnp.where(columns[i] == here_all, 1.0, 0.0)
        ranks.append(jnp.sum(found, axis=0, keepdims=True))
    rank = jnp.concatenate(ranks, 1).astype(jnp.int32)
    row_at = (tile >> 1) * 4 + (rank & 3)
    group_at = (tile & 1) * 2 + (rank >> 2)
    bin_ref, offset_ref, weight_ref, spectra_ref = fetch.take(1, 2, 3, 4)
    place = bin_ref[...]
    cell_x = (place >> 5).astype(f32) + offset_ref[0:1, :]
    cell_y = (place & 31).astype(f32) + offset_ref[1:2, :]
    values = jnp.concatenate(
        [
            spectra_ref[...],
            jnp.concatenate([weight_ref[...], cell_x, cell_y, jnp.zeros((5, 1024), f32)], 0),
            jnp.zeros((8, 1024), f32),
        ],
        0,
    )
    spread = jnp.concatenate([jnp.where(group_at == s, values, 0.0) for s in range(4)], 0)
    high = spread.astype(bf16)
    rest = spread - high.astype(f32)
    mid = rest.astype(bf16)
    low = (rest - mid.astype(f32)).astype(bf16)
    wide = jnp.concatenate([high, mid, low], 0)
    rows = lax.broadcasted_iota(jnp.int32, (512, 1024), 0)
    chosen = jnp.where(rows == row_at, 1.0, 0.0).astype(bf16)
    moved = lax.dot_general(
        chosen, wide, (((1,), (1,)), ((), ())), preferred_element_type=f32
    )
    out_ref[...] = (moved[:, :128] + moved[:, 128:256]) + moved[:, 256:]
    velocity = fetch.take(5)[...].astype(f32).astype(bf16)
    at = lax.broadcasted_iota(jnp.int32, (HALF, HALF), 0)
    flip = jnp.where(at + lanes((HALF, HALF)) == HALF - 1, 1.0, 0.0).astype(bf16)
    right = mm(velocity[:, HALF:], flip).astype(bf16)
    velocity = jnp.concatenate([velocity[:, :HALF], right], 1)
    at, along = lax.broadcasted_iota(jnp.int32, (32, 32), 0), lanes((32, 32))
    target = jnp.where(lat_ref[0] >= 8, 31 - at, at)
    vel_ref[...] = mm(jnp.where(along == target, 1.0, 0.0).astype(bf16), velocity)


def mode_cosines(mode, place):
    turns = mode * place * (1.0 / 64)
    half = (turns - jnp.round(turns)) * math.pi
    sq = half * half
    sine = 1.0 / 6227020800
    for c in (-1.0 / 39916800, 1.0 / 362880, -1.0 / 5040, 1.0 / 120, -1.0 / 6, 1.0):
        sine = sine * sq + c
    sine = sine * half
    return 1.0 - 2.0 * sine * sine


def factor_rows(wave_sq, kx, ky, ky_mirror):
    first = shift_factor(wave_sq, kx, ky)
    mirror = shift_factor(wave_sq, kx[:, :128], ky_mirror)
    return [jnp.concatenate([first[p], mirror[p], first[p][:, 128:]], 1) for p in range(2)]


def factor_kernel(freq_ref, slow_ref, factor_ref, edge_ref):
    at = lanes((1, HALF))
    ky = at.astype(f32) * STEP
    ky_mirror = jnp.where(at[:, :128] == 0, 256, at[:, :128]).astype(f32) * STEP
    for step in range(2):
        values, refs = references_of(slow_ref, step)
        for g in range(2):
            wave = freq_ref[0] * refs[g]
            wave_sq = wave * wave

            def some_rows(k, carry):
                start = pl.multiple_of(k * 32, 32)
                row = lax.broadcasted_iota(jnp.int32, (32, HALF), 0) + start
                found = factor_rows(wave_sq, row.astype(f32) * STEP, ky, ky_mirror)
                for p in range(2):
                    factor_ref[step, g, p, pl.ds(start, 32), :] = found[p]
                return carry

            lax.fori_loop(0, 8, some_rows, 0)
            row = lax.broadcasted_iota(jnp.int32, (8, HALF), 0)
            row = jnp.where(row == 0, 256, row)
            found = factor_rows(wave_sq, row.astype(f32) * STEP, ky, ky_mirror)
            for p in range(2):
                edge_ref[step, g, p] = found[p]


def solve_kernel(lat_ref, got_ref, *refs):
    slabs, out_ref, four_ref, sems = refs[:4], refs[4], refs[5], refs[6]
    fetch = Fetch(slabs, [four_ref.at[(lat_ref[0] & 3) ^ d] for d in range(4)], sems)
    turned_in = got_ref[...].T
    blocks = []
    mode = lax.broadcasted_iota(jnp.int32, (8, 1024), 0).astype(f32)
    eye_rows = lax.broadcasted_iota(jnp.int32, (64, 128), 0)
    eye = jnp.where(eye_rows == lanes((64, 128)), 1.0, 0.0)
    for t in range(2):
        both = jnp.concatenate(
            [turned_in[64 * t : 64 * t + 24], turned_in[64 * t + 32 : 64 * t + 56]], 1
        )
        along_x = mode_cosines(mode, both[17:18] + 0.5)
        along_y = mode_cosines(mode, both[18:19] + 0.5)
        basis = jnp.concatenate([along_x[a : a + 1] * along_y for a in range(8)], 0)
        wide = jnp.concatenate([basis, both[0:16], jnp.zeros((48, 1024), f32)], 0)
        system = lax.dot_general(
            basis * both[16:17],
            wide,
            (((1,), (1,)), ((), ())),
            preferred_element_type=f32,
            precision=lax.Precision.HIGHEST,
        )
        system = system + eye
        blocks.append([system[8 * a : 8 * a + 8] for a in range(8)])
    sub = lax.broadcasted_iota(jnp.int32, (8, 128), 0)
    for at in range(8):
        for inner in range(0, 8, 4):
            picked = [(8 * at + inner + i, inner + i) for i in range(4)]
            for t in range(2):
                mine = blocks[t]
                rows = [
                    jnp.broadcast_to(mine[at][s : s + 1], (8, 128)) for _, s in picked
                ]
                small = [
                    [jnp.broadcast_to(row[:, j : j + 1], (8, 128)) for j, _ in picked]
                    for row in rows
                ]
                count = len(picked)
                for p in range(count):
                    scale = 1.0 / small[p][p]
                    rows[p] = rows[p] * scale
                    small[p] = [v * scale for v in small[p]]
                    for i in range(count):
                        if i != p:
                            by = small[i][p]
                            rows[i] = rows[i] - by * rows[p]
                            small[i] = [
                                v - by * w if k > p else v
                                for k, (v, w) in enumerate(zip(small[i], small[p]))
                            ]
                for k in range(0, 8):
                    new = mine[k]
                    for row, (j, s) in zip(rows, picked):
                        new = new - mine[k][:, j : j + 1] * row
                    if k == at:
                        for row, (j, s) in zip(rows, picked):
                            new = jnp.where(sub == s, row, new)
                    mine[k] = new
    stacked = jnp.concatenate([blocks[t][a] for a in range(8) for t in range(2)], 0)
    final = stacked.T
    odd = (lax.broadcasted_iota(jnp.int32, (32, 128), 0) & 1) == 1
    for f in range(8):
        out_ref[32 * f : 32 * f + 32] = jnp.where(
            odd, final[72 + f : 73 + f], final[64 + f : 65 + f]
        )
    fetch.take(0, 1, 2, 3)


def store_spectrum(spec_ref, u, v, cols):
    first = minus_i(u, [no_first(t, 0) for t in v])
    second = plus_i([no_first(t, 0) for t in u], v)
    for k, value in enumerate((*first, *second)):
        spec_ref[k, :, cols] = value


def wave_pair(waves_ref, which):
    return waves_ref[0, which], waves_ref[1, which]


def own_dot(own_ref, rows_at, value):
    with_high = mm(own_ref[rows_at : rows_at + 64], value[0])
    return with_high[:32] + (with_high[32:] + mm(own_ref[rows_at : rows_at + 32], value[1]))


def invert_x(spec_ref, factor_ref, edge_ref, own_ref, own_back, g, cols):
    fac = [factor_ref[g, p, :, cols] for p in range(2)]
    fac_edge = [jnp.concatenate([edge_ref[g, p, :, cols], fac[p][8:]], 0) for p in range(2)]
    s = [spec_ref[i, :, cols] for i in range(4)]
    up = (s[0] * fac[0] - s[1] * fac[1], s[0] * fac[1] + s[1] * fac[0])
    down = (s[2] * fac_edge[0] - s[3] * fac_edge[1], s[2] * fac_edge[1] + s[3] * fac_edge[0])
    even = split(jnp.concatenate([up[p] + no_first(down[p], 0) for p in range(2)], 1))
    odd = split(jnp.concatenate([no_first(up[p], 0) - down[p] for p in range(2)], 1))
    mine = plus_i(
        halves_of(own_dot(own_ref, 0, even), 1, HALF),
        halves_of(own_dot(own_ref, 64, odd), 1, HALF),
    )
    for p in range(2):
        own_back[g, 32 * p : 32 * p + 32, cols] = mine[p]
    return even, odd


def fold_columns(value):
    left, right = value[:, :HALF], value[:, HALF:]
    return split(left + no_first(right, 1)), split(no_first(left, 1) - right)


def own_field(step, own_back, waves_ref, velocity, slow_ref, freq_ref):
    even, odd = fold_columns(jnp.concatenate([own_back[0], own_back[1]], 0))
    sides = []
    for at in (0, 4):
        u, v = dot3(even, wave_pair(waves_ref, at)), dot3(odd, wave_pair(waves_ref, at + 1))
        sides.append(
            [
                plus_i(
                    halves_of(u[64 * g : 64 * g + 64], 0, 32),
                    halves_of(v[64 * g : 64 * g + 64], 0, 32),
                )
                for g in range(2)
            ]
        )
    back = [
        [jnp.concatenate([sides[0][g][p], sides[1][g][p]], 1) for p in range(2)] for g in range(2)
    ]
    cosine, sine, top = split_turns(velocity, step, slow_ref, freq_ref)
    picked = [jnp.where(top, back[1][p], back[0][p]) for p in range(2)]
    return (
        picked[0] * cosine - picked[1] * sine,
        picked[0] * sine + picked[1] * cosine,
    )


def first_kernel(lat_ref, freq_ref, slow_ref, got_ref, *refs):
    sources, image_ref, back_hbm = refs[:7], refs[7], refs[8]
    targets, sems, out_sems = refs[9:16], refs[16], refs[17]
    spec_ref, own_back, back_ref = refs[18:]
    fetch = Fetch(
        [
            *sources[:2],
            sources[2].at[lat_ref[0]],
            sources[3].at[0],
            sources[4].at[0],
            sources[5],
            sources[6].at[0],
        ],
        targets,
        sems,
    )
    rows = lax.broadcasted_iota(jnp.int32, (128, 128), 0)
    groups = lanes((128, 128)) >> 4
    stacked = []
    for p in range(2):
        value = got_ref[pl.ds(p, 128, stride=2), :]
        for k in (1, 2, 4):
            s_bit, g_bit = (rows & k) != 0, (groups & k) != 0
            down = turned(turned(value, k, 0), -16 * k, 1)
            up = turned(turned(value, -k, 0), 16 * k, 1)
            value = jnp.where(
                s_bit & ~g_bit, down, jnp.where(~s_bit & g_bit, up, value)
            )
        stacked.append(value)
    table = fetch.take(0)
    both = dot3(split(jnp.concatenate(stacked, 0)), (table[0], table[1]))
    u, v = (halves_of(t, 0, 128) for t in (both[:, :HALF], both[:, HALF:]))
    first = minus_i(u, [no_first(t, 1) for t in v])
    second = plus_i([no_first(t, 1) for t in u], v)
    table = fetch.take(1)
    for c, here in enumerate((first, second)):
        both = dot3((table[0], table[1]), split(jnp.concatenate(here, 1)))
        store_spectrum(
            spec_ref,
            halves_of(both[:HALF], 1, HALF),
            halves_of(both[HALF:], 1, HALF),
            pl.ds(HALF * c, HALF),
        )
    own_ref, factor_ref, edge_ref, waves_ref = fetch.take(2, 3, 4, 5)
    leaving = []
    for g in range(2):
        for c in range(2):
            cols = pl.ds(HALF * c, HALF)
            even, odd = invert_x(spec_ref, factor_ref, edge_ref, own_ref, own_back, g, cols)
            u = halves_of(dot3(wave_pair(waves_ref, 2), even), 1, HALF)
            v = halves_of(dot3(wave_pair(waves_ref, 3), odd), 1, HALF)
            first, second = plus_i(u, v), minus_i(u, v)
            for p in range(2):
                back_ref[g, p, :HALF, cols] = first[p]
                back_ref[g, p, HALF:, cols] = second[p]
            copy = pltpu.make_async_copy(
                back_ref.at[g, :, :, cols], back_hbm.at[g, :, :, cols], out_sems.at[2 * g + c]
            )
            copy.start()
            leaving.append(copy)
    vel_ref = fetch.take(6)
    image_ref[...] = own_field(0, own_back, waves_ref, vel_ref[...], slow_ref, freq_ref)[0]
    for copy in leaving:
        copy.wait()


def second_kernel(lat_ref, freq_ref, slow_ref, image_ref, *refs):
    slabs, refs = refs[:4], refs[4:]
    sources, wave_ref, out_ref = refs[:6], refs[6], refs[7]
    targets, slabs_ref, sems, back_sems = refs[8:13], refs[13], refs[14], refs[15]
    back_ref, spec_ref, own_back, half_ref = refs[16:]

    def arriving(k):
        at = pl.ds(pl.multiple_of(k * 128, 128), 128)
        return pltpu.make_async_copy(
            sources[0].at[:, :, at, :], back_ref.at[:, :, at, :], back_sems.at[k]
        )

    arriving(0).start()
    fetch = Fetch(
        [
            sources[1],
            *slabs,
            sources[2].at[1],
            sources[3].at[1],
            sources[4].at[lat_ref[0]],
            sources[5].at[1],
        ],
        [targets[0], *[slabs_ref.at[(lat_ref[0] >> 2) ^ d] for d in range(4)], *targets[1:]],
        sems,
    )
    for k in range(1, 4):
        arriving(k).start()
    waves_ref = fetch.take(*range(5))[0]

    def some_rows(k, carry):
        arriving(k).wait()
        at = pl.ds(pl.multiple_of(k * 128, 128), 128)
        back = []
        for g in range(2):
            even, odd = fold_columns(
                jnp.concatenate([back_ref[g, p, at, :] for p in range(2)], 0)
            )
            u = halves_of(dot3(even, wave_pair(waves_ref, 0)), 0, 128)
            v = halves_of(dot3(odd, wave_pair(waves_ref, 1)), 0, 128)
            back.append((plus_i(u, v), minus_i(u, v)))
        slabs = [
            slabs_ref[jnp.where(k < 2, k, 5 - k), jnp.where(k < 2, i, 3 - i)] for i in range(4)
        ]
        velocity = jnp.concatenate(slabs, 0).astype(jnp.int32)
        fields = []
        for side in range(2):
            cosine, sine, top = split_turns(
                velocity[:, HALF * side : HALF * side + HALF], 0, slow_ref, freq_ref
            )
            picked = [jnp.where(top, back[1][side][p], back[0][side][p]) for p in range(2)]
            fields.append(
                jnp.concatenate(
                    [
                        picked[0] * cosine - picked[1] * sine,
                        picked[0] * sine + picked[1] * cosine,
                    ],
                    0,
                )
            )
        u = halves_of(dot3(split(fields[0] + fields[1]), wave_pair(waves_ref, 2)), 0, 128)
        v = halves_of(dot3(split(fields[0] - fields[1]), wave_pair(waves_ref, 3)), 0, 128)
        first = minus_i(u, [no_first(t, 1) for t in v])
        second = plus_i([no_first(t, 1) for t in u], v)
        for p in range(2):
            half_ref[p, at, :HALF] = first[p]
            half_ref[p, at, HALF:] = second[p]
        return carry

    lax.fori_loop(0, 4, some_rows, 0)

    def some_columns(c, carry):
        cols = pl.ds(pl.multiple_of(c * HALF, HALF), HALF)
        top = jnp.concatenate([half_ref[p, :HALF, cols] for p in range(2)], 1)
        low = jnp.concatenate([half_ref[p, HALF:, cols] for p in range(2)], 1)
        u = halves_of(dot3(wave_pair(waves_ref, 0), split(top + low)), 1, HALF)
        v = halves_of(dot3(wave_pair(waves_ref, 1), split(top - low)), 1, HALF)
        store_spectrum(spec_ref, u, v, cols)
        return carry

    lax.fori_loop(0, 2, some_columns, 0)
    factor_ref, edge_ref, own_ref, vel_ref = fetch.take(5, 6, 7, 8)

    def invert(k, carry):
        cols = pl.ds(pl.multiple_of((k & 1) * HALF, HALF), HALF)
        invert_x(spec_ref, factor_ref, edge_ref, own_ref, own_back, k >> 1, cols)
        return carry

    lax.fori_loop(0, 4, invert, 0)
    field = own_field(1, own_back, waves_ref, vel_ref[...], slow_ref, freq_ref)
    for p in range(2):
        wave_ref[p] = field[p]
    upper = lanes((32, 128)) >= 64
    image = image_ref[...]
    for d in range(8):
        col, pos = d // 2, d % 2
        first = turned(image[:, 128 * col : 128 * col + 128], -64 * pos)
        second = turned(field[0][:, 128 * col : 128 * col + 128], 64 - 64 * pos)
        out_ref[d] = jnp.where(upper, second, first)


def sum_kernel(got_ref, out_ref):
    total = got_ref[0]
    for d in range(1, 8):
        total = total + got_ref[d]
    out_ref[0] = total[:, :64]
    out_ref[1] = total[:, 64:]


def call(kernel, outs, in_specs, mega, scratch=(), out_specs=None):
    many = isinstance(outs, list)
    shapes = [jax.ShapeDtypeStruct(s, f32) for s in (outs if many else [outs])]
    return pl.pallas_call(
        kernel,
        out_shape=shapes if many else shapes[0],
        in_specs=in_specs,
        out_specs=out_specs or ([VM] * len(shapes) if many else VM),
        scratch_shapes=list(scratch),
        compiler_params=pltpu.CompilerParams(vmem_limit_bytes=mega * 1024 * 1024),
    )


def local(spectra, tile_route, bin_in_tile, trace_offset, weights, frequency, slowness, vel_index):
    const = tables()
    lat_at = lax.axis_index("lat").astype(jnp.int32).reshape(1)
    everyone = ("freq", "lat")
    sent, velocity = call(
        route_kernel,
        [(512, 128), (32, 512)],
        [SM] + [HBM] * 6,
        60,
        [
            pltpu.VMEM((1, 1024), jnp.int32),
            pltpu.VMEM((1, 1024), jnp.int32),
            pltpu.VMEM((2, 1024), f32),
            pltpu.VMEM((1, 1024), f32),
            pltpu.VMEM((16, 1024), f32),
            pltpu.VMEM((32, 512), jnp.int32),
            pltpu.SemaphoreType.DMA((6,)),
        ],
    )(
        lat_at,
        tile_route.reshape(1, 1024),
        bin_in_tile.reshape(1, 1024),
        trace_offset,
        weights.reshape(1, 1024),
        spectra.reshape(16, 1024),
        vel_index,
    )
    got = lax.all_to_all(sent.reshape(128, 4, 128), everyone, 0, 0, tiled=True)
    slabs = [velocity] + [
        lax.ppermute(velocity, "lat", [(i, i ^ d) for i in range(16)]) for d in (1, 2, 3)
    ]
    sent, slabs = call(
        solve_kernel,
        [(256, 128), (4, 32, 512)],
        [SM, VM] + [HBM] * 4,
        24,
        [pltpu.SemaphoreType.DMA((4,))],
        [VM, HBM],
    )(lat_at, got.reshape(512, 128), *slabs)
    got = lax.all_to_all(sent.reshape(128, 2, 128), everyone, 0, 0, tiled=True)
    slabs = [slabs] + [
        lax.ppermute(slabs, "lat", [(i, i ^ d) for i in range(16)]) for d in (4, 8, 12)
    ]
    factor, edge = call(
        factor_kernel, [(2, 2, 2, 256, 512), (2, 2, 2, 8, 512)], [SM, SM], 59
    )(frequency, slowness)
    image, back = call(
        first_kernel,
        [(32, 512), (2, 2, 512, 512)],
        [SM, SM, SM, VM] + [HBM] * 7,
        59,
        [
            pltpu.VMEM((2, 128, 512), bf16),
            pltpu.VMEM((2, 512, 128), bf16),
            pltpu.VMEM((128, 256), bf16),
            pltpu.VMEM((2, 2, 256, 512), f32),
            pltpu.VMEM((2, 2, 8, 512), f32),
            pltpu.VMEM((2, 6, 256, 256), bf16),
            pltpu.VMEM((32, 512), jnp.int32),
            pltpu.SemaphoreType.DMA((7,)),
            pltpu.SemaphoreType.DMA((4,)),
            pltpu.VMEM((4, 256, 512), f32),
            pltpu.VMEM((2, 64, 512), f32),
            pltpu.VMEM((2, 2, 512, 512), f32),
        ],
        [VM, HBM],
    )(
        lat_at,
        frequency,
        slowness,
        got.reshape(256, 128),
        const["along_y"],
        const["along_x"],
        const["own"],
        factor,
        edge,
        const["waves"],
        vel_index,
    )
    wave, sent = call(
        second_kernel,
        [(2, 32, 512), (8, 32, 128)],
        [SM, SM, SM, VM] + [HBM] * 10,
        59,
        [
            pltpu.VMEM((2, 6, 256, 256), bf16),
            pltpu.VMEM((2, 2, 256, 512), f32),
            pltpu.VMEM((2, 2, 8, 512), f32),
            pltpu.VMEM((128, 256), bf16),
            pltpu.VMEM((32, 512), jnp.int32),
            pltpu.VMEM((4, 4, 32, 512), f32),
            pltpu.SemaphoreType.DMA((9,)),
            pltpu.SemaphoreType.DMA((4,)),
            pltpu.VMEM((2, 2, 512, 512), f32),
            pltpu.VMEM((4, 256, 512), f32),
            pltpu.VMEM((2, 64, 512), f32),
            pltpu.VMEM((2, 512, 512), f32),
        ],
    )(
        lat_at,
        frequency,
        slowness,
        image,
        *slabs,
        back,
        const["waves"],
        factor,
        edge,
        const["own"],
        vel_index,
    )
    got = lax.all_to_all(sent, "freq", 0, 0, tiled=True)
    depth_image = call(sum_kernel, (2, 32, 64), [VM], 16)(got)
    return (wave.reshape(2, 1, 32, 512), depth_image)


def solution(mesh):
    return jax.shard_map(
        local,
        mesh=mesh,
        in_specs=(
            P(None, None, ("freq", "lat")),
            P(("freq", "lat"), None),
            P(("freq", "lat")),
            P(None, ("freq", "lat")),
            P(("freq", "lat")),
            P("freq"),
            P(),
            P(None, "lat", None),
        ),
        out_specs=(P(None, "freq", "lat", None), P(None, "lat", "freq")),
        check_vma=False,
    )
```

```python
import math

import jax
import jax.numpy as jnp
import ml_dtypes
import numpy as np
from jax import lax
from jax.experimental import pallas as pl
from jax.experimental.pallas import tpu as pltpu
from jax.sharding import PartitionSpec as P

NX = 512
NY = 512
TB = 32
MODES = 8
HALF = 256
SCALE = 1.0 / (NX * NY)
STEP = 2.0 * math.pi / 512

f32 = jnp.float32
bf16 = jnp.bfloat16
VM = pl.BlockSpec(memory_space=pltpu.VMEM)
SM = pl.BlockSpec(memory_space=pltpu.SMEM)
HBM = pl.BlockSpec(memory_space=pltpu.HBM)


def pair(table):
    table = np.asarray(table, np.float32)
    high = table.astype(ml_dtypes.bfloat16)
    low = (table - high.astype(np.float32)).astype(ml_dtypes.bfloat16)
    return np.stack([high, low])


def waves(bins):
    twice = 2 * np.asarray(bins)[None, :] + 1
    index = np.arange(HALF)[:, None]
    sine_index = np.where(index == 0, HALF, index)
    return (
        np.cos(np.pi / 512 * (index * twice % 1024)),
        np.sin(np.pi / 512 * (sine_index * twice % 1024)),
    )


def tables():
    cell = np.arange(TB)
    modes = np.cos(np.pi * np.arange(MODES)[:, None] * (cell[None, :] + 0.5) / TB)
    cosine, sine = waves(np.arange(512))
    along = [
        np.einsum("aj,iyj->yai", modes, t.reshape(HALF, 16, TB)).reshape(16 * MODES, HALF)
        for t in (cosine, sine)
    ]
    along = np.concatenate(along, 1)
    own = np.concatenate(
        [pair(t.reshape(HALF, 16, 32).transpose(1, 2, 0)) for t in (cosine, sine)], 0
    )
    own = own.transpose(1, 0, 2, 3).reshape(16, 128, HALF)
    first = [cosine[:, :HALF], sine[:, :HALF]]
    late = [cosine[:, HALF:], sine[:, HALF:]]
    waves_all = pair(np.stack([*first, *[t.T for t in first], *late]))
    return dict(along_y=pair(along), along_x=pair(along.T), own=own, waves=waves_all)


def split(value):
    high = value.astype(bf16)
    low = (value - high.astype(f32)).astype(bf16)
    return high, low


def mm(left, right):
    return jnp.dot(left, right, preferred_element_type=f32)


def dot3(left, right):
    return mm(
        jnp.concatenate([left[0], left[1], left[0]], 1),
        jnp.concatenate([right[0], right[0], right[1]], 0),
    )


def lanes(shape):
    return lax.broadcasted_iota(jnp.int32, shape, len(shape) - 1)


def turned(value, shift, axis=1):
    size = value.shape[axis]
    shift = shift % size
    return value if shift == 0 else pltpu.roll(value, shift, axis)


def cos_sin(turn):
    half = 0.5 * turn
    sq = half * half
    cosine = 1.0 / 479001600
    for c in (-1.0 / 3628800, 1.0 / 40320, -1.0 / 720, 1.0 / 24, -0.5, 1.0):
        cosine = cosine * sq + c
    sine = 1.0 / 6227020800
    for c in (-1.0 / 39916800, 1.0 / 362880, -1.0 / 5040, 1.0 / 120, -1.0 / 6, 1.0):
        sine = sine * sq + c
    sine = sine * half
    return 1.0 - 2.0 * sine * sine, 2.0 * sine * cosine


def shift_factor(wave_sq, kx, ky):
    vertical = wave_sq - kx * kx - ky * ky
    root = jnp.sqrt(jnp.abs(vertical))
    cosine, sine = cos_sin(root)
    moving = vertical > 0.0
    return jnp.where(moving, cosine, jnp.exp(-root)), jnp.where(moving, sine, 0.0)


def references_of(slow_ref, step):
    values = [slow_ref[step, i] for i in range(8)]
    refs = [
        (values[4 * g] + values[4 * g + 1] + values[4 * g + 2] + values[4 * g + 3]) * 0.25
        for g in range(2)
    ]
    return values, refs


def split_turns(velocity, step, slow_ref, freq_ref):
    values, refs = references_of(slow_ref, step)
    pairs = [cos_sin(freq_ref[0] * (values[i] - refs[i // 4])) for i in range(8)]
    low, mid, top = (velocity & 1) == 1, (velocity & 2) == 2, velocity >= 4
    out = []
    for p in range(2):
        level = [pairs[i][p] * SCALE for i in range(8)]
        level = [jnp.where(low, level[2 * i + 1], level[2 * i]) for i in range(4)]
        level = [jnp.where(mid, level[2 * i + 1], level[2 * i]) for i in range(2)]
        out.append(jnp.where(top, level[1], level[0]))
    return out[0], out[1], top


def no_first(value, axis):
    at = lax.broadcasted_iota(jnp.int32, value.shape, axis)
    return jnp.where(at > 0, value, 0.0)


def plus_i(u, v):
    return u[0] - v[1], u[1] + v[0]


def minus_i(u, v):
    return u[0] + v[1], u[1] - v[0]


def halves_of(value, axis, count):
    if axis == 0:
        return value[:count], value[count:]
    return value[:, :count], value[:, count:]


class Fetch:
    def __init__(self, sources, targets, sems):
        self.targets = targets
        self.copies = [
            pltpu.make_async_copy(s, t, sems.at[i]) for i, (s, t) in enumerate(zip(sources, targets))
        ]
        for copy in self.copies:
            copy.start()

    def take(self, *which):
        for i in which:
            self.copies[i].wait()
        out = [self.targets[i] for i in which]
        return out[0] if len(out) == 1 else out


def route_kernel(lat_ref, *refs):
    sources, out_ref, vel_ref = refs[:6], refs[6], refs[7]
    targets, sems = refs[8:14], refs[14]
    fetch = Fetch([*sources[:5], sources[5].at[0]], targets, sems)
    tile = fetch.take(0)[...]
    tile_f = tile.astype(f32)
    below = lax.broadcasted_iota(jnp.int32, (128, 128), 0) < lanes((128, 128))
    columns = []
    ranks = []
    for j in range(8):
        here = tile_f[:, 128 * j : 128 * (j + 1)]
        here_all = jnp.broadcast_to(here, (128, 128))
        columns.append(here_all.T)
        found = jnp.where((columns[j] == here_all) & below, 1.0, 0.0)
        for i in range(j):
            found = found + jnp.where(columns[i] == here_all, 1.0, 0.0)
        ranks.append(jnp.sum(found, axis=0, keepdims=True))
    rank = jnp.concatenate(ranks, 1).astype(jnp.int32)
    row_at = (tile >> 1) * 4 + (rank & 3)
    group_at = (tile & 1) * 2 + (rank >> 2)
    bin_ref, offset_ref, weight_ref, spectra_ref = fetch.take(1, 2, 3, 4)
    place = bin_ref[...]
    cell_x = (place >> 5).astype(f32) + offset_ref[0:1, :]
    cell_y = (place & 31).astype(f32) + offset_ref[1:2, :]
    values = jnp.concatenate(
        [
            spectra_ref[...],
            jnp.concatenate([weight_ref[...], cell_x, cell_y, jnp.zeros((5, 1024), f32)], 0),
            jnp.zeros((8, 1024), f32),
        ],
        0,
    )
    spread = jnp.concatenate([jnp.where(group_at == s, values, 0.0) for s in range(4)], 0)
    high = spread.astype(bf16)
    rest = spread - high.astype(f32)
    mid = rest.astype(bf16)
    low = (rest - mid.astype(f32)).astype(bf16)
    wide = jnp.concatenate([high, mid, low], 0)
    rows = lax.broadcasted_iota(jnp.int32, (512, 1024), 0)
    chosen = jnp.where(rows == row_at, 1.0, 0.0).astype(bf16)
    moved = lax.dot_general(
        chosen, wide, (((1,), (1,)), ((), ())), preferred_element_type=f32
    )
    out_ref[...] = (moved[:, :128] + moved[:, 128:256]) + moved[:, 256:]
    velocity = fetch.take(5)[...].astype(f32).astype(bf16)
    at = lax.broadcasted_iota(jnp.int32, (HALF, HALF), 0)
    flip = jnp.where(at + lanes((HALF, HALF)) == HALF - 1, 1.0, 0.0).astype(bf16)
    right = mm(velocity[:, HALF:], flip).astype(bf16)
    velocity = jnp.concatenate([velocity[:, :HALF], right], 1)
    at, along = lax.broadcasted_iota(jnp.int32, (32, 32), 0), lanes((32, 32))
    target = jnp.where(lat_ref[0] >= 8, 31 - at, at)
    vel_ref[...] = mm(jnp.where(along == target, 1.0, 0.0).astype(bf16), velocity)


def mode_cosines(mode, place):
    turns = mode * place * (1.0 / 64)
    half = (turns - jnp.round(turns)) * math.pi
    sq = half * half
    sine = 1.0 / 6227020800
    for c in (-1.0 / 39916800, 1.0 / 362880, -1.0 / 5040, 1.0 / 120, -1.0 / 6, 1.0):
        sine = sine * sq + c
    sine = sine * half
    return 1.0 - 2.0 * sine * sine


def factor_rows(wave_sq, kx, ky, ky_mirror):
    first = shift_factor(wave_sq, kx, ky)
    mirror = shift_factor(wave_sq, kx[:, :128], ky_mirror)
    return [jnp.concatenate([first[p], mirror[p], first[p][:, 128:]], 1) for p in range(2)]


def factor_kernel(freq_ref, slow_ref, factor_hbm, edge_ref, factor_ref, sems):
    leaving = []
    at = lanes((1, HALF))
    ky = at.astype(f32) * STEP
    ky_mirror = jnp.where(at[:, :128] == 0, 256, at[:, :128]).astype(f32) * STEP
    for step in range(2):
        values, refs = references_of(slow_ref, step)
        for g in range(2):
            wave = freq_ref[0] * refs[g]
            wave_sq = wave * wave

            def some_rows(k, carry):
                start = pl.multiple_of(k * 32, 32)
                row = lax.broadcasted_iota(jnp.int32, (32, HALF), 0) + start
                found = factor_rows(wave_sq, row.astype(f32) * STEP, ky, ky_mirror)
                for p in range(2):
                    factor_ref[step, g, p, pl.ds(start, 32), :] = found[p]
                return carry

            lax.fori_loop(0, 8, some_rows, 0)
            row = lax.broadcasted_iota(jnp.int32, (8, HALF), 0)
            row = jnp.where(row == 0, 256, row)
            found = factor_rows(wave_sq, row.astype(f32) * STEP, ky, ky_mirror)
            for p in range(2):
                edge_ref[step, g, p] = found[p]
            copy = pltpu.make_async_copy(
                factor_ref.at[step, g], factor_hbm.at[step, g], sems.at[2 * step + g]
            )
            copy.start()
            leaving.append(copy)
    for copy in leaving:
        copy.wait()


def solve_kernel(lat_ref, got_ref, *refs):
    slabs, out_ref, four_ref, sems = refs[:4], refs[4], refs[5], refs[6]
    fetch = Fetch(slabs, [four_ref.at[(lat_ref[0] & 3) ^ d] for d in range(4)], sems)
    turned_in = got_ref[...].T
    blocks = []
    mode = lax.broadcasted_iota(jnp.int32, (8, 1024), 0).astype(f32)
    eye_rows = lax.broadcasted_iota(jnp.int32, (64, 128), 0)
    eye = jnp.where(eye_rows == lanes((64, 128)), 1.0, 0.0)
    for t in range(2):
        both = jnp.concatenate(
            [turned_in[64 * t : 64 * t + 24], turned_in[64 * t + 32 : 64 * t + 56]], 1
        )
        along_x = mode_cosines(mode, both[17:18] + 0.5)
        along_y = mode_cosines(mode, both[18:19] + 0.5)
        basis = jnp.concatenate([along_x[a : a + 1] * along_y for a in range(8)], 0)
        wide = jnp.concatenate([basis, both[0:16], jnp.zeros((48, 1024), f32)], 0)
        system = lax.dot_general(
            basis * both[16:17],
            wide,
            (((1,), (1,)), ((), ())),
            preferred_element_type=f32,
            precision=lax.Precision.HIGHEST,
        )
        system = system + eye
        blocks.append([system[8 * a : 8 * a + 8] for a in range(8)])
    sub = lax.broadcasted_iota(jnp.int32, (8, 128), 0)
    for at in range(8):
        for inner in range(0, 8, 4):
            picked = [(8 * at + inner + i, inner + i) for i in range(4)]
            for t in range(2):
                mine = blocks[t]
                rows = [
                    jnp.broadcast_to(mine[at][s : s + 1], (8, 128)) for _, s in picked
                ]
                small = [
                    [jnp.broadcast_to(row[:, j : j + 1], (8, 128)) for j, _ in picked]
                    for row in rows
                ]
                count = len(picked)
                for p in range(count):
                    scale = 1.0 / small[p][p]
                    rows[p] = rows[p] * scale
                    small[p] = [v * scale for v in small[p]]
                    for i in range(count):
                        if i != p:
                            by = small[i][p]
                            rows[i] = rows[i] - by * rows[p]
                            small[i] = [
                                v - by * w if k > p else v
                                for k, (v, w) in enumerate(zip(small[i], small[p]))
                            ]
                for k in range(0, 8):
                    new = mine[k]
                    for row, (j, s) in zip(rows, picked):
                        new = new - mine[k][:, j : j + 1] * row
                    if k == at:
                        for row, (j, s) in zip(rows, picked):
                            new = jnp.where(sub == s, row, new)
                    mine[k] = new
    stacked = jnp.concatenate([blocks[t][a] for a in range(8) for t in range(2)], 0)
    final = stacked.T
    odd = (lax.broadcasted_iota(jnp.int32, (32, 128), 0) & 1) == 1
    for f in range(8):
        out_ref[32 * f : 32 * f + 32] = jnp.where(
            odd, final[72 + f : 73 + f], final[64 + f : 65 + f]
        )
    fetch.take(0, 1, 2, 3)


def store_spectrum(spec_ref, u, v, cols):
    first = minus_i(u, [no_first(t, 0) for t in v])
    second = plus_i([no_first(t, 0) for t in u], v)
    for k, value in enumerate((*first, *second)):
        spec_ref[k, :, cols] = value


def wave_pair(waves_ref, which):
    return waves_ref[0, which], waves_ref[1, which]


def own_dot(own_ref, rows_at, value):
    with_high = mm(own_ref[rows_at : rows_at + 64], value[0])
    return with_high[:32] + (with_high[32:] + mm(own_ref[rows_at : rows_at + 32], value[1]))


def invert_x(spec_ref, factor_ref, edge_ref, own_ref, own_back, g, cols):
    fac = [factor_ref[g, p, :, cols] for p in range(2)]
    fac_edge = [jnp.concatenate([edge_ref[g, p, :, cols], fac[p][8:]], 0) for p in range(2)]
    s = [spec_ref[i, :, cols] for i in range(4)]
    up = (s[0] * fac[0] - s[1] * fac[1], s[0] * fac[1] + s[1] * fac[0])
    down = (s[2] * fac_edge[0] - s[3] * fac_edge[1], s[2] * fac_edge[1] + s[3] * fac_edge[0])
    even = split(jnp.concatenate([up[p] + no_first(down[p], 0) for p in range(2)], 1))
    odd = split(jnp.concatenate([no_first(up[p], 0) - down[p] for p in range(2)], 1))
    mine = plus_i(
        halves_of(own_dot(own_ref, 0, even), 1, HALF),
        halves_of(own_dot(own_ref, 64, odd), 1, HALF),
    )
    for p in range(2):
        own_back[g, 32 * p : 32 * p + 32, cols] = mine[p]
    return even, odd


def fold_columns(value):
    left, right = value[:, :HALF], value[:, HALF:]
    return split(left + no_first(right, 1)), split(no_first(left, 1) - right)


def own_field(step, own_back, waves_ref, velocity, slow_ref, freq_ref):
    even, odd = fold_columns(jnp.concatenate([own_back[0], own_back[1]], 0))
    sides = []
    for at in (0, 4):
        u, v = dot3(even, wave_pair(waves_ref, at)), dot3(odd, wave_pair(waves_ref, at + 1))
        sides.append(
            [
                plus_i(
                    halves_of(u[64 * g : 64 * g + 64], 0, 32),
                    halves_of(v[64 * g : 64 * g + 64], 0, 32),
                )
                for g in range(2)
            ]
        )
    back = [
        [jnp.concatenate([sides[0][g][p], sides[1][g][p]], 1) for p in range(2)] for g in range(2)
    ]
    cosine, sine, top = split_turns(velocity, step, slow_ref, freq_ref)
    picked = [jnp.where(top, back[1][p], back[0][p]) for p in range(2)]
    return (
        picked[0] * cosine - picked[1] * sine,
        picked[0] * sine + picked[1] * cosine,
    )


def grid_kernel(lat_ref, freq_ref, slow_ref, got_ref, *refs):
    slabs, refs = refs[:4], refs[4:]
    sources, wave_ref, out_ref = refs[:7], refs[7], refs[8]
    targets, slabs_ref, later_ref, sems = refs[9:16], *refs[16:19]
    spec_ref, own_back, back_ref, half_ref = refs[19:]
    fetch = Fetch(
        [
            *sources[:2],
            sources[2].at[lat_ref[0]],
            sources[3].at[0],
            *sources[4:],
            *slabs,
            sources[3].at[1],
        ],
        [*targets, *[slabs_ref.at[(lat_ref[0] >> 2) ^ d] for d in range(4)], later_ref],
        sems,
    )
    rows = lax.broadcasted_iota(jnp.int32, (128, 128), 0)
    groups = lanes((128, 128)) >> 4
    stacked = []
    for p in range(2):
        value = got_ref[pl.ds(p, 128, stride=2), :]
        for k in (1, 2, 4):
            s_bit, g_bit = (rows & k) != 0, (groups & k) != 0
            down = turned(turned(value, k, 0), -16 * k, 1)
            up = turned(turned(value, -k, 0), 16 * k, 1)
            value = jnp.where(
                s_bit & ~g_bit, down, jnp.where(~s_bit & g_bit, up, value)
            )
        stacked.append(value)
    table = fetch.take(0)
    both = dot3(split(jnp.concatenate(stacked, 0)), (table[0], table[1]))
    u, v = (halves_of(t, 0, 128) for t in (both[:, :HALF], both[:, HALF:]))
    first = minus_i(u, [no_first(t, 1) for t in v])
    second = plus_i([no_first(t, 1) for t in u], v)
    table = fetch.take(1)
    for c, here in enumerate((first, second)):
        both = dot3((table[0], table[1]), split(jnp.concatenate(here, 1)))
        store_spectrum(
            spec_ref,
            halves_of(both[:HALF], 1, HALF),
            halves_of(both[HALF:], 1, HALF),
            pl.ds(HALF * c, HALF),
        )
    own_ref, factor_ref, edge_ref, waves_ref = fetch.take(2, 3, 4, 5)
    for g in range(2):
        for c in range(2):
            cols = pl.ds(HALF * c, HALF)
            even, odd = invert_x(spec_ref, factor_ref, edge_ref.at[0], own_ref, own_back, g, cols)
            u = halves_of(dot3(wave_pair(waves_ref, 2), even), 1, HALF)
            v = halves_of(dot3(wave_pair(waves_ref, 3), odd), 1, HALF)
            first, second = plus_i(u, v), minus_i(u, v)
            for p in range(2):
                back_ref[g, p, :HALF, cols] = first[p]
                back_ref[g, p, HALF:, cols] = second[p]
    vel_ref = fetch.take(6)
    image = own_field(0, own_back, waves_ref, vel_ref[0], slow_ref, freq_ref)[0]
    fetch.take(7, 8, 9, 10)

    def some_rows(k, carry):
        at = pl.ds(pl.multiple_of(k * 128, 128), 128)
        back = []
        for g in range(2):
            even, odd = fold_columns(
                jnp.concatenate([back_ref[g, p, at, :] for p in range(2)], 0)
            )
            u = halves_of(dot3(even, wave_pair(waves_ref, 0)), 0, 128)
            v = halves_of(dot3(odd, wave_pair(waves_ref, 1)), 0, 128)
            back.append((plus_i(u, v), minus_i(u, v)))
        slabs = [
            slabs_ref[jnp.where(k < 2, k, 5 - k), jnp.where(k < 2, i, 3 - i)] for i in range(4)
        ]
        velocity = jnp.concatenate(slabs, 0).astype(jnp.int32)
        fields = []
        for side in range(2):
            cosine, sine, top = split_turns(
                velocity[:, HALF * side : HALF * side + HALF], 0, slow_ref, freq_ref
            )
            picked = [jnp.where(top, back[1][side][p], back[0][side][p]) for p in range(2)]
            fields.append(
                jnp.concatenate(
                    [
                        picked[0] * cosine - picked[1] * sine,
                        picked[0] * sine + picked[1] * cosine,
                    ],
                    0,
                )
            )
        u = halves_of(dot3(split(fields[0] + fields[1]), wave_pair(waves_ref, 2)), 0, 128)
        v = halves_of(dot3(split(fields[0] - fields[1]), wave_pair(waves_ref, 3)), 0, 128)
        first = minus_i(u, [no_first(t, 1) for t in v])
        second = plus_i([no_first(t, 1) for t in u], v)
        for p in range(2):
            half_ref[p, at, :HALF] = first[p]
            half_ref[p, at, HALF:] = second[p]
        return carry

    lax.fori_loop(0, 4, some_rows, 0)

    def some_columns(c, carry):
        cols = pl.ds(pl.multiple_of(c * HALF, HALF), HALF)
        top = jnp.concatenate([half_ref[p, :HALF, cols] for p in range(2)], 1)
        low = jnp.concatenate([half_ref[p, HALF:, cols] for p in range(2)], 1)
        u = halves_of(dot3(wave_pair(waves_ref, 0), split(top + low)), 1, HALF)
        v = halves_of(dot3(wave_pair(waves_ref, 1), split(top - low)), 1, HALF)
        store_spectrum(spec_ref, u, v, cols)
        return carry

    lax.fori_loop(0, 2, some_columns, 0)
    later_factor = fetch.take(11)

    def invert(k, carry):
        cols = pl.ds(pl.multiple_of((k & 1) * HALF, HALF), HALF)
        invert_x(spec_ref, later_factor, edge_ref.at[1], own_ref, own_back, k >> 1, cols)
        return carry

    lax.fori_loop(0, 4, invert, 0)
    field = own_field(1, own_back, waves_ref, vel_ref[1], slow_ref, freq_ref)
    for p in range(2):
        wave_ref[p] = field[p]
    upper = lanes((32, 128)) >= 64
    for d in range(8):
        col, pos = d // 2, d % 2
        first = turned(image[:, 128 * col : 128 * col + 128], -64 * pos)
        second = turned(field[0][:, 128 * col : 128 * col + 128], 64 - 64 * pos)
        out_ref[d] = jnp.where(upper, second, first)


def sum_kernel(got_ref, out_ref):
    total = got_ref[0]
    for d in range(1, 8):
        total = total + got_ref[d]
    out_ref[0] = total[:, :64]
    out_ref[1] = total[:, 64:]


def call(kernel, outs, in_specs, mega, scratch=(), out_specs=None):
    many = isinstance(outs, list)
    shapes = [jax.ShapeDtypeStruct(s, f32) for s in (outs if many else [outs])]
    return pl.pallas_call(
        kernel,
        out_shape=shapes if many else shapes[0],
        in_specs=in_specs,
        out_specs=out_specs or ([VM] * len(shapes) if many else VM),
        scratch_shapes=list(scratch),
        compiler_params=pltpu.CompilerParams(vmem_limit_bytes=mega * 1024 * 1024),
    )


def local(spectra, tile_route, bin_in_tile, trace_offset, weights, frequency, slowness, vel_index):
    const = tables()
    lat_at = lax.axis_index("lat").astype(jnp.int32).reshape(1)
    everyone = ("freq", "lat")
    sent, velocity = call(
        route_kernel,
        [(512, 128), (32, 512)],
        [SM] + [HBM] * 6,
        60,
        [
            pltpu.VMEM((1, 1024), jnp.int32),
            pltpu.VMEM((1, 1024), jnp.int32),
            pltpu.VMEM((2, 1024), f32),
            pltpu.VMEM((1, 1024), f32),
            pltpu.VMEM((16, 1024), f32),
            pltpu.VMEM((32, 512), jnp.int32),
            pltpu.SemaphoreType.DMA((6,)),
        ],
    )(
        lat_at,
        tile_route.reshape(1, 1024),
        bin_in_tile.reshape(1, 1024),
        trace_offset,
        weights.reshape(1, 1024),
        spectra.reshape(16, 1024),
        vel_index,
    )
    got = lax.all_to_all(sent.reshape(128, 4, 128), everyone, 0, 0, tiled=True)
    slabs = [velocity] + [
        lax.ppermute(velocity, "lat", [(i, i ^ d) for i in range(16)]) for d in (1, 2, 3)
    ]
    sent, slabs = call(
        solve_kernel,
        [(256, 128), (4, 32, 512)],
        [SM, VM] + [HBM] * 4,
        24,
        [pltpu.SemaphoreType.DMA((4,))],
        [VM, HBM],
    )(lat_at, got.reshape(512, 128), *slabs)
    got = lax.all_to_all(sent.reshape(128, 2, 128), everyone, 0, 0, tiled=True)
    slabs = [slabs] + [
        lax.ppermute(slabs, "lat", [(i, i ^ d) for i in range(16)]) for d in (4, 8, 12)
    ]
    factor, edge = call(
        factor_kernel,
        [(2, 2, 2, 256, 512), (2, 2, 2, 8, 512)],
        [SM, SM],
        59,
        [pltpu.VMEM((2, 2, 2, 256, 512), f32), pltpu.SemaphoreType.DMA((4,))],
        [HBM, VM],
    )(frequency, slowness)
    wave, sent = call(
        grid_kernel,
        [(2, 32, 512), (8, 32, 128)],
        [SM, SM, SM, VM] + [HBM] * 11,
        59,
        [
            pltpu.VMEM((2, 128, 512), bf16),
            pltpu.VMEM((2, 512, 128), bf16),
            pltpu.VMEM((128, 256), bf16),
            pltpu.VMEM((2, 2, 256, 512), f32),
            pltpu.VMEM((2, 2, 2, 8, 512), f32),
            pltpu.VMEM((2, 6, 256, 256), bf16),
            pltpu.VMEM((2, 32, 512), jnp.int32),
            pltpu.VMEM((4, 4, 32, 512), f32),
            pltpu.VMEM((2, 2, 256, 512), f32),
            pltpu.SemaphoreType.DMA((12,)),
            pltpu.VMEM((4, 256, 512), f32),
            pltpu.VMEM((2, 64, 512), f32),
            pltpu.VMEM((2, 2, 512, 512), f32),
            pltpu.VMEM((2, 512, 512), f32),
        ],
    )(
        lat_at,
        frequency,
        slowness,
        got.reshape(256, 128),
        *slabs,
        const["along_y"],
        const["along_x"],
        const["own"],
        factor,
        edge,
        const["waves"],
        vel_index,
    )
    got = lax.all_to_all(sent, "freq", 0, 0, tiled=True)
    depth_image = call(sum_kernel, (2, 32, 64), [VM], 16)(got)
    return (wave.reshape(2, 1, 32, 512), depth_image)


def solution(mesh):
    return jax.shard_map(
        local,
        mesh=mesh,
        in_specs=(
            P(None, None, ("freq", "lat")),
            P(("freq", "lat"), None),
            P(("freq", "lat")),
            P(None, ("freq", "lat")),
            P(("freq", "lat")),
            P("freq"),
            P(),
            P(None, "lat", None),
        ),
        out_specs=(P(None, "freq", "lat", None), P(None, "lat", "freq")),
        check_vma=False,
    )
```

```python
import math

import jax
import jax.numpy as jnp
import ml_dtypes
import numpy as np
from jax import lax
from jax.experimental import pallas as pl
from jax.experimental.pallas import tpu as pltpu
from jax.sharding import PartitionSpec as P

NX = 512
NY = 512
TB = 32
MODES = 8
HALF = 256
SCALE = 1.0 / (NX * NY)
STEP = 2.0 * math.pi / 512

f32 = jnp.float32
bf16 = jnp.bfloat16
VM = pl.BlockSpec(memory_space=pltpu.VMEM)
SM = pl.BlockSpec(memory_space=pltpu.SMEM)
HBM = pl.BlockSpec(memory_space=pltpu.HBM)


def pair(table):
    table = np.asarray(table, np.float32)
    high = table.astype(ml_dtypes.bfloat16)
    low = (table - high.astype(np.float32)).astype(ml_dtypes.bfloat16)
    return np.stack([high, low])


def waves(bins):
    twice = 2 * np.asarray(bins)[None, :] + 1
    index = np.arange(HALF)[:, None]
    sine_index = np.where(index == 0, HALF, index)
    return (
        np.cos(np.pi / 512 * (index * twice % 1024)),
        np.sin(np.pi / 512 * (sine_index * twice % 1024)),
    )


def tables():
    cell = np.arange(TB)
    modes = np.cos(np.pi * np.arange(MODES)[:, None] * (cell[None, :] + 0.5) / TB)
    cosine, sine = waves(np.arange(512))
    along = [
        np.einsum("aj,iyj->yai", modes, t.reshape(HALF, 16, TB)).reshape(16 * MODES, HALF)
        for t in (cosine, sine)
    ]
    along = np.concatenate(along, 1)
    own = np.concatenate(
        [pair(t.reshape(HALF, 16, 32).transpose(1, 2, 0)) for t in (cosine, sine)], 0
    )
    own = own.transpose(1, 0, 2, 3).reshape(16, 128, HALF)
    first = [cosine[:, :HALF], sine[:, :HALF]]
    late = [cosine[:, HALF:], sine[:, HALF:]]
    waves_all = pair(np.stack([*first, *[t.T for t in first], *late]))
    return dict(along_y=pair(along), along_x=pair(along.T), own=own, waves=waves_all)


def split(value):
    high = value.astype(bf16)
    low = (value - high.astype(f32)).astype(bf16)
    return high, low


def mm(left, right):
    return jnp.dot(left, right, preferred_element_type=f32)


def dot3(left, right):
    return mm(
        jnp.concatenate([left[0], left[1], left[0]], 1),
        jnp.concatenate([right[0], right[0], right[1]], 0),
    )


def lanes(shape):
    return lax.broadcasted_iota(jnp.int32, shape, len(shape) - 1)


def turned(value, shift, axis=1):
    size = value.shape[axis]
    shift = shift % size
    return value if shift == 0 else pltpu.roll(value, shift, axis)


def cos_sin(turn):
    half = 0.5 * turn
    sq = half * half
    cosine = 1.0 / 479001600
    for c in (-1.0 / 3628800, 1.0 / 40320, -1.0 / 720, 1.0 / 24, -0.5, 1.0):
        cosine = cosine * sq + c
    sine = 1.0 / 6227020800
    for c in (-1.0 / 39916800, 1.0 / 362880, -1.0 / 5040, 1.0 / 120, -1.0 / 6, 1.0):
        sine = sine * sq + c
    sine = sine * half
    return 1.0 - 2.0 * sine * sine, 2.0 * sine * cosine


def shift_factor(wave_sq, kx, ky):
    vertical = wave_sq - kx * kx - ky * ky
    root = jnp.sqrt(jnp.abs(vertical))
    cosine, sine = cos_sin(root)
    moving = vertical > 0.0
    return jnp.where(moving, cosine, jnp.exp(-root)), jnp.where(moving, sine, 0.0)


def references_of(slow_ref, step):
    values = [slow_ref[step, i] for i in range(8)]
    refs = [
        (values[4 * g] + values[4 * g + 1] + values[4 * g + 2] + values[4 * g + 3]) * 0.25
        for g in range(2)
    ]
    return values, refs


def split_turns(velocity, step, slow_ref, freq_ref):
    values, refs = references_of(slow_ref, step)
    pairs = [cos_sin(freq_ref[0] * (values[i] - refs[i // 4])) for i in range(8)]
    low, mid, top = (velocity & 1) == 1, (velocity & 2) == 2, velocity >= 4
    out = []
    for p in range(2):
        level = [pairs[i][p] * SCALE for i in range(8)]
        level = [jnp.where(low, level[2 * i + 1], level[2 * i]) for i in range(4)]
        level = [jnp.where(mid, level[2 * i + 1], level[2 * i]) for i in range(2)]
        out.append(jnp.where(top, level[1], level[0]))
    return out[0], out[1], top


def no_first(value, axis):
    at = lax.broadcasted_iota(jnp.int32, value.shape, axis)
    return jnp.where(at > 0, value, 0.0)


def plus_i(u, v):
    return u[0] - v[1], u[1] + v[0]


def minus_i(u, v):
    return u[0] + v[1], u[1] - v[0]


def halves_of(value, axis, count):
    if axis == 0:
        return value[:count], value[count:]
    return value[:, :count], value[:, count:]


class Fetch:
    def __init__(self, sources, targets, sems):
        self.targets = targets
        self.copies = [
            pltpu.make_async_copy(s, t, sems.at[i]) for i, (s, t) in enumerate(zip(sources, targets))
        ]
        for copy in self.copies:
            copy.start()

    def take(self, *which):
        for i in which:
            self.copies[i].wait()
        out = [self.targets[i] for i in which]
        return out[0] if len(out) == 1 else out


def route_kernel(lat_ref, *refs):
    sources, out_ref, vel_ref = refs[:6], refs[6], refs[7]
    targets, sems = refs[8:14], refs[14]
    fetch = Fetch([*sources[:5], sources[5].at[0]], targets, sems)
    tile = fetch.take(0)[...]
    tile_f = tile.astype(f32)
    below = lax.broadcasted_iota(jnp.int32, (128, 128), 0) < lanes((128, 128))
    columns = []
    ranks = []
    for j in range(8):
        here = tile_f[:, 128 * j : 128 * (j + 1)]
        here_all = jnp.broadcast_to(here, (128, 128))
        columns.append(here_all.T)
        found = jnp.where((columns[j] == here_all) & below, 1.0, 0.0)
        for i in range(j):
            found = found + jnp.where(columns[i] == here_all, 1.0, 0.0)
        ranks.append(jnp.sum(found, axis=0, keepdims=True))
    rank = jnp.concatenate(ranks, 1).astype(jnp.int32)
    row_at = (tile >> 1) * 4 + (rank & 3)
    group_at = (tile & 1) * 2 + (rank >> 2)
    bin_ref, offset_ref, weight_ref, spectra_ref = fetch.take(1, 2, 3, 4)
    place = bin_ref[...]
    cell_x = (place >> 5).astype(f32) + offset_ref[0:1, :]
    cell_y = (place & 31).astype(f32) + offset_ref[1:2, :]
    values = jnp.concatenate(
        [
            spectra_ref[...],
            jnp.concatenate([weight_ref[...], cell_x, cell_y, jnp.zeros((5, 1024), f32)], 0),
            jnp.zeros((8, 1024), f32),
        ],
        0,
    )
    spread = jnp.concatenate([jnp.where(group_at == s, values, 0.0) for s in range(4)], 0)
    high = spread.astype(bf16)
    rest = spread - high.astype(f32)
    mid = rest.astype(bf16)
    low = (rest - mid.astype(f32)).astype(bf16)
    wide = jnp.concatenate([high, mid, low], 0)
    rows = lax.broadcasted_iota(jnp.int32, (512, 1024), 0)
    chosen = jnp.where(rows == row_at, 1.0, 0.0).astype(bf16)
    moved = lax.dot_general(
        chosen, wide, (((1,), (1,)), ((), ())), preferred_element_type=f32
    )
    out_ref[...] = (moved[:, :128] + moved[:, 128:256]) + moved[:, 256:]
    velocity = fetch.take(5)[...].astype(f32).astype(bf16)
    at = lax.broadcasted_iota(jnp.int32, (HALF, HALF), 0)
    flip = jnp.where(at + lanes((HALF, HALF)) == HALF - 1, 1.0, 0.0).astype(bf16)
    right = mm(velocity[:, HALF:], flip).astype(bf16)
    velocity = jnp.concatenate([velocity[:, :HALF], right], 1)
    at, along = lax.broadcasted_iota(jnp.int32, (32, 32), 0), lanes((32, 32))
    target = jnp.where(lat_ref[0] >= 8, 31 - at, at)
    vel_ref[...] = mm(jnp.where(along == target, 1.0, 0.0).astype(bf16), velocity)


def mode_cosines(mode, place):
    turns = mode * place * (1.0 / 64)
    half = (turns - jnp.round(turns)) * math.pi
    sq = half * half
    sine = 1.0 / 6227020800
    for c in (-1.0 / 39916800, 1.0 / 362880, -1.0 / 5040, 1.0 / 120, -1.0 / 6, 1.0):
        sine = sine * sq + c
    sine = sine * half
    return 1.0 - 2.0 * sine * sine


def factor_rows(wave_sq, kx, ky, ky_mirror):
    first = shift_factor(wave_sq, kx, ky)
    mirror = shift_factor(wave_sq, kx[:, :128], ky_mirror)
    return [jnp.concatenate([first[p], mirror[p], first[p][:, 128:]], 1) for p in range(2)]


def factor_kernel(freq_ref, slow_ref, factor_hbm, edge_ref, factor_ref, sems):
    leaving = []
    at = lanes((1, HALF))
    ky = at.astype(f32) * STEP
    ky_mirror = jnp.where(at[:, :128] == 0, 256, at[:, :128]).astype(f32) * STEP
    for step in range(2):
        values, refs = references_of(slow_ref, step)
        for g in range(2):
            wave = freq_ref[0] * refs[g]
            wave_sq = wave * wave

            def some_rows(k, carry):
                start = pl.multiple_of(k * 32, 32)
                row = lax.broadcasted_iota(jnp.int32, (32, HALF), 0) + start
                found = factor_rows(wave_sq, row.astype(f32) * STEP, ky, ky_mirror)
                for p in range(2):
                    factor_ref[step, g, p, pl.ds(start, 32), :] = found[p]
                return carry

            lax.fori_loop(0, 8, some_rows, 0)
            row = lax.broadcasted_iota(jnp.int32, (8, HALF), 0)
            row = jnp.where(row == 0, 256, row)
            found = factor_rows(wave_sq, row.astype(f32) * STEP, ky, ky_mirror)
            for p in range(2):
                edge_ref[step, g, p] = found[p]
            copy = pltpu.make_async_copy(
                factor_ref.at[step, g], factor_hbm.at[step, g], sems.at[2 * step + g]
            )
            copy.start()
            leaving.append(copy)
    for copy in leaving:
        copy.wait()


def solve_kernel(lat_ref, got_ref, *refs):
    slabs, out_ref, four_ref, sems = refs[:4], refs[4], refs[5], refs[6]
    fetch = Fetch(slabs, [four_ref.at[(lat_ref[0] & 3) ^ d] for d in range(4)], sems)
    turned_in = got_ref[...].T
    blocks = []
    mode = lax.broadcasted_iota(jnp.int32, (8, 1024), 0).astype(f32)
    eye_rows = lax.broadcasted_iota(jnp.int32, (64, 128), 0)
    eye = jnp.where(eye_rows == lanes((64, 128)), 1.0, 0.0)
    for t in range(2):
        both = jnp.concatenate(
            [turned_in[64 * t : 64 * t + 24], turned_in[64 * t + 32 : 64 * t + 56]], 1
        )
        along_x = mode_cosines(mode, both[17:18] + 0.5)
        along_y = mode_cosines(mode, both[18:19] + 0.5)
        basis = jnp.concatenate([along_x[a : a + 1] * along_y for a in range(8)], 0)
        wide = jnp.concatenate([basis, both[0:16], jnp.zeros((48, 1024), f32)], 0)
        system = lax.dot_general(
            basis * both[16:17],
            wide,
            (((1,), (1,)), ((), ())),
            preferred_element_type=f32,
            precision=lax.Precision.HIGHEST,
        )
        system = system + eye
        blocks.append([system[8 * a : 8 * a + 8] for a in range(8)])
    sub = lax.broadcasted_iota(jnp.int32, (8, 128), 0)
    for at in range(8):
        for inner in range(0, 8, 4):
            picked = [(8 * at + inner + i, inner + i) for i in range(4)]
            for t in range(2):
                mine = blocks[t]
                rows = [
                    jnp.broadcast_to(mine[at][s : s + 1], (8, 128)) for _, s in picked
                ]
                small = [
                    [jnp.broadcast_to(row[:, j : j + 1], (8, 128)) for j, _ in picked]
                    for row in rows
                ]
                count = len(picked)
                for p in range(count):
                    scale = 1.0 / small[p][p]
                    rows[p] = rows[p] * scale
                    small[p] = [v * scale for v in small[p]]
                    for i in range(count):
                        if i != p:
                            by = small[i][p]
                            rows[i] = rows[i] - by * rows[p]
                            small[i] = [
                                v - by * w if k > p else v
                                for k, (v, w) in enumerate(zip(small[i], small[p]))
                            ]
                for k in range(0, 8):
                    new = mine[k]
                    for row, (j, s) in zip(rows, picked):
                        new = new - mine[k][:, j : j + 1] * row
                    if k == at:
                        for row, (j, s) in zip(rows, picked):
                            new = jnp.where(sub == s, row, new)
                    mine[k] = new
    stacked = jnp.concatenate([blocks[t][a] for a in range(8) for t in range(2)], 0)
    final = stacked.T
    odd = (lax.broadcasted_iota(jnp.int32, (32, 128), 0) & 1) == 1
    for f in range(8):
        out_ref[32 * f : 32 * f + 32] = jnp.where(
            odd, final[72 + f : 73 + f], final[64 + f : 65 + f]
        )
    fetch.take(0, 1, 2, 3)


def store_spectrum(spec_ref, u, v, cols):
    first = minus_i(u, [no_first(t, 0) for t in v])
    second = plus_i([no_first(t, 0) for t in u], v)
    for k, value in enumerate((*first, *second)):
        spec_ref[k, :, cols] = value


def wave_pair(waves_ref, which):
    return waves_ref[0, which], waves_ref[1, which]


def own_dot(own_ref, rows_at, value):
    with_high = mm(own_ref[rows_at : rows_at + 64], value[0])
    return with_high[:32] + (with_high[32:] + mm(own_ref[rows_at : rows_at + 32], value[1]))


def shifted(spec_ref, factor_ref, edge_ref, g, cols):
    fac = [factor_ref[g, p, :, cols] for p in range(2)]
    fac_edge = [jnp.concatenate([edge_ref[g, p, :, cols], fac[p][8:]], 0) for p in range(2)]
    s = [spec_ref[i, :, cols] for i in range(4)]
    up = (s[0] * fac[0] - s[1] * fac[1], s[0] * fac[1] + s[1] * fac[0])
    down = (s[2] * fac_edge[0] - s[3] * fac_edge[1], s[2] * fac_edge[1] + s[3] * fac_edge[0])
    even = split(jnp.concatenate([up[p] + no_first(down[p], 0) for p in range(2)], 1))
    odd = split(jnp.concatenate([no_first(up[p], 0) - down[p] for p in range(2)], 1))
    return even, odd


def fold_columns(value):
    left, right = value[:, :HALF], value[:, HALF:]
    return split(left + no_first(right, 1)), split(no_first(left, 1) - right)


def in_three(value):
    high = value.astype(bf16)
    rest = value - high.astype(f32)
    mid = rest.astype(bf16)
    return high, mid, (rest - mid.astype(f32)).astype(bf16)


def own_image(slab, real_ref):
    start = pl.multiple_of(32 * jnp.where(slab < 8, slab, 23 - slab), 32)
    value = real_ref[pl.ds(start, 32), :]
    at = lax.broadcasted_iota(jnp.int32, (32, 32), 0)
    target = jnp.where(slab >= 8, 31 - at, at)
    order = jnp.where(lanes((32, 32)) == target, 1.0, 0.0).astype(bf16)
    pieces = in_three(value)
    value = mm(order, pieces[0]) + mm(order, pieces[1]) + mm(order, pieces[2])
    at = lax.broadcasted_iota(jnp.int32, (HALF, HALF), 0)
    flip = jnp.where(at + lanes((HALF, HALF)) == HALF - 1, 1.0, 0.0).astype(bf16)
    right = mm(jnp.concatenate(in_three(value[:, HALF:]), 0), flip)
    right = right[:32] + right[32:64] + right[64:]
    return jnp.concatenate([value[:, :HALF], right], 1)


def own_field(step, own_back, waves_ref, velocity, slow_ref, freq_ref):
    even, odd = fold_columns(jnp.concatenate([own_back[0], own_back[1]], 0))
    sides = []
    for at in (0, 4):
        u, v = dot3(even, wave_pair(waves_ref, at)), dot3(odd, wave_pair(waves_ref, at + 1))
        sides.append(
            [
                plus_i(
                    halves_of(u[64 * g : 64 * g + 64], 0, 32),
                    halves_of(v[64 * g : 64 * g + 64], 0, 32),
                )
                for g in range(2)
            ]
        )
    back = [
        [jnp.concatenate([sides[0][g][p], sides[1][g][p]], 1) for p in range(2)] for g in range(2)
    ]
    cosine, sine, top = split_turns(velocity, step, slow_ref, freq_ref)
    picked = [jnp.where(top, back[1][p], back[0][p]) for p in range(2)]
    return (
        picked[0] * cosine - picked[1] * sine,
        picked[0] * sine + picked[1] * cosine,
    )


def grid_kernel(lat_ref, freq_ref, slow_ref, got_ref, *refs):
    slabs, refs = refs[:4], refs[4:]
    sources, wave_ref, out_ref = refs[:7], refs[7], refs[8]
    targets, slabs_ref, later_ref, sems = refs[9:16], *refs[16:19]
    spec_ref, own_back, back_ref, half_ref, real_ref = refs[19:]
    fetch = Fetch(
        [
            *sources[:2],
            sources[2].at[lat_ref[0]],
            sources[3].at[0],
            *sources[4:],
            *slabs,
            sources[3].at[1],
        ],
        [*targets, *[slabs_ref.at[(lat_ref[0] >> 2) ^ d] for d in range(4)], later_ref],
        sems,
    )
    rows = lax.broadcasted_iota(jnp.int32, (128, 128), 0)
    groups = lanes((128, 128)) >> 4
    stacked = []
    for p in range(2):
        value = got_ref[pl.ds(p, 128, stride=2), :]
        for k in (1, 2, 4):
            s_bit, g_bit = (rows & k) != 0, (groups & k) != 0
            down = turned(turned(value, k, 0), -16 * k, 1)
            up = turned(turned(value, -k, 0), 16 * k, 1)
            value = jnp.where(
                s_bit & ~g_bit, down, jnp.where(~s_bit & g_bit, up, value)
            )
        stacked.append(value)
    table = fetch.take(0)
    both = dot3(split(jnp.concatenate(stacked, 0)), (table[0], table[1]))
    u, v = (halves_of(t, 0, 128) for t in (both[:, :HALF], both[:, HALF:]))
    first = minus_i(u, [no_first(t, 1) for t in v])
    second = plus_i([no_first(t, 1) for t in u], v)
    table = fetch.take(1)
    for c, here in enumerate((first, second)):
        both = dot3((table[0], table[1]), split(jnp.concatenate(here, 1)))
        store_spectrum(
            spec_ref,
            halves_of(both[:HALF], 1, HALF),
            halves_of(both[HALF:], 1, HALF),
            pl.ds(HALF * c, HALF),
        )
    own_ref, factor_ref, edge_ref, waves_ref = fetch.take(2, 3, 4, 5)
    for g in range(2):
        for c in range(2):
            cols = pl.ds(HALF * c, HALF)
            even, odd = shifted(spec_ref, factor_ref, edge_ref.at[0], g, cols)
            u = halves_of(dot3(wave_pair(waves_ref, 2), even), 1, HALF)
            v = halves_of(dot3(wave_pair(waves_ref, 3), odd), 1, HALF)
            first, second = plus_i(u, v), minus_i(u, v)
            for p in range(2):
                back_ref[g, p, :HALF, cols] = first[p]
                back_ref[g, p, HALF:, cols] = second[p]
    vel_ref = fetch.take(6)
    fetch.take(7, 8, 9, 10)

    def some_rows(k, carry):
        at = pl.ds(pl.multiple_of(k * 128, 128), 128)
        back = []
        for g in range(2):
            even, odd = fold_columns(
                jnp.concatenate([back_ref[g, p, at, :] for p in range(2)], 0)
            )
            u = halves_of(dot3(even, wave_pair(waves_ref, 0)), 0, 128)
            v = halves_of(dot3(odd, wave_pair(waves_ref, 1)), 0, 128)
            back.append((plus_i(u, v), minus_i(u, v)))
        slabs = [
            slabs_ref[jnp.where(k < 2, k, 5 - k), jnp.where(k < 2, i, 3 - i)] for i in range(4)
        ]
        velocity = jnp.concatenate(slabs, 0).astype(jnp.int32)
        fields = []
        for side in range(2):
            cosine, sine, top = split_turns(
                velocity[:, HALF * side : HALF * side + HALF], 0, slow_ref, freq_ref
            )
            picked = [jnp.where(top, back[1][side][p], back[0][side][p]) for p in range(2)]
            fields.append(
                jnp.concatenate(
                    [
                        picked[0] * cosine - picked[1] * sine,
                        picked[0] * sine + picked[1] * cosine,
                    ],
                    0,
                )
            )
        for side in range(2):
            real_ref[at, HALF * side : HALF * side + HALF] = fields[side][:128]
        u = halves_of(dot3(split(fields[0] + fields[1]), wave_pair(waves_ref, 2)), 0, 128)
        v = halves_of(dot3(split(fields[0] - fields[1]), wave_pair(waves_ref, 3)), 0, 128)
        first = minus_i(u, [no_first(t, 1) for t in v])
        second = plus_i([no_first(t, 1) for t in u], v)
        for p in range(2):
            half_ref[p, at, :HALF] = first[p]
            half_ref[p, at, HALF:] = second[p]
        return carry

    lax.fori_loop(0, 4, some_rows, 0)

    def some_columns(c, carry):
        cols = pl.ds(pl.multiple_of(c * HALF, HALF), HALF)
        top = jnp.concatenate([half_ref[p, :HALF, cols] for p in range(2)], 1)
        low = jnp.concatenate([half_ref[p, HALF:, cols] for p in range(2)], 1)
        u = halves_of(dot3(wave_pair(waves_ref, 0), split(top + low)), 1, HALF)
        v = halves_of(dot3(wave_pair(waves_ref, 1), split(top - low)), 1, HALF)
        store_spectrum(spec_ref, u, v, cols)
        return carry

    lax.fori_loop(0, 2, some_columns, 0)
    later_factor = fetch.take(11)

    def invert(k, carry):
        cols = pl.ds(pl.multiple_of((k & 1) * HALF, HALF), HALF)
        even, odd = shifted(spec_ref, later_factor, edge_ref.at[1], k >> 1, cols)
        mine = plus_i(
            halves_of(own_dot(own_ref, 0, even), 1, HALF),
            halves_of(own_dot(own_ref, 64, odd), 1, HALF),
        )
        for p in range(2):
            own_back[k >> 1, 32 * p : 32 * p + 32, cols] = mine[p]
        return carry

    lax.fori_loop(0, 4, invert, 0)
    field = own_field(1, own_back, waves_ref, vel_ref[1], slow_ref, freq_ref)
    for p in range(2):
        wave_ref[p] = field[p]
    image = own_image(lat_ref[0], real_ref)
    upper = lanes((32, 128)) >= 64
    for d in range(8):
        col, pos = d // 2, d % 2
        first = turned(image[:, 128 * col : 128 * col + 128], -64 * pos)
        second = turned(field[0][:, 128 * col : 128 * col + 128], 64 - 64 * pos)
        out_ref[d] = jnp.where(upper, second, first)


def sum_kernel(got_ref, out_ref):
    total = got_ref[0]
    for d in range(1, 8):
        total = total + got_ref[d]
    out_ref[0] = total[:, :64]
    out_ref[1] = total[:, 64:]


def call(kernel, outs, in_specs, mega, scratch=(), out_specs=None):
    many = isinstance(outs, list)
    shapes = [jax.ShapeDtypeStruct(s, f32) for s in (outs if many else [outs])]
    return pl.pallas_call(
        kernel,
        out_shape=shapes if many else shapes[0],
        in_specs=in_specs,
        out_specs=out_specs or ([VM] * len(shapes) if many else VM),
        scratch_shapes=list(scratch),
        compiler_params=pltpu.CompilerParams(vmem_limit_bytes=mega * 1024 * 1024),
    )


def local(spectra, tile_route, bin_in_tile, trace_offset, weights, frequency, slowness, vel_index):
    const = tables()
    lat_at = lax.axis_index("lat").astype(jnp.int32).reshape(1)
    everyone = ("freq", "lat")
    sent, velocity = call(
        route_kernel,
        [(512, 128), (32, 512)],
        [SM] + [HBM] * 6,
        60,
        [
            pltpu.VMEM((1, 1024), jnp.int32),
            pltpu.VMEM((1, 1024), jnp.int32),
            pltpu.VMEM((2, 1024), f32),
            pltpu.VMEM((1, 1024), f32),
            pltpu.VMEM((16, 1024), f32),
            pltpu.VMEM((32, 512), jnp.int32),
            pltpu.SemaphoreType.DMA((6,)),
        ],
    )(
        lat_at,
        tile_route.reshape(1, 1024),
        bin_in_tile.reshape(1, 1024),
        trace_offset,
        weights.reshape(1, 1024),
        spectra.reshape(16, 1024),
        vel_index,
    )
    got = lax.all_to_all(sent.reshape(128, 4, 128), everyone, 0, 0, tiled=True)
    slabs = [velocity] + [
        lax.ppermute(velocity, "lat", [(i, i ^ d) for i in range(16)]) for d in (1, 2, 3)
    ]
    sent, slabs = call(
        solve_kernel,
        [(256, 128), (4, 32, 512)],
        [SM, VM] + [HBM] * 4,
        24,
        [pltpu.SemaphoreType.DMA((4,))],
        [VM, HBM],
    )(lat_at, got.reshape(512, 128), *slabs)
    got = lax.all_to_all(sent.reshape(128, 2, 128), everyone, 0, 0, tiled=True)
    slabs = [slabs] + [
        lax.ppermute(slabs, "lat", [(i, i ^ d) for i in range(16)]) for d in (4, 8, 12)
    ]
    factor, edge = call(
        factor_kernel,
        [(2, 2, 2, 256, 512), (2, 2, 2, 8, 512)],
        [SM, SM],
        59,
        [pltpu.VMEM((2, 2, 2, 256, 512), f32), pltpu.SemaphoreType.DMA((4,))],
        [HBM, VM],
    )(frequency, slowness)
    wave, sent = call(
        grid_kernel,
        [(2, 32, 512), (8, 32, 128)],
        [SM, SM, SM, VM] + [HBM] * 11,
        59,
        [
            pltpu.VMEM((2, 128, 512), bf16),
            pltpu.VMEM((2, 512, 128), bf16),
            pltpu.VMEM((128, 256), bf16),
            pltpu.VMEM((2, 2, 256, 512), f32),
            pltpu.VMEM((2, 2, 2, 8, 512), f32),
            pltpu.VMEM((2, 6, 256, 256), bf16),
            pltpu.VMEM((2, 32, 512), jnp.int32),
            pltpu.VMEM((4, 4, 32, 512), f32),
            pltpu.VMEM((2, 2, 256, 512), f32),
            pltpu.SemaphoreType.DMA((12,)),
            pltpu.VMEM((4, 256, 512), f32),
            pltpu.VMEM((2, 64, 512), f32),
            pltpu.VMEM((2, 2, 512, 512), f32),
            pltpu.VMEM((2, 512, 512), f32),
            pltpu.VMEM((512, 512), f32),
        ],
    )(
        lat_at,
        frequency,
        slowness,
        got.reshape(256, 128),
        *slabs,
        const["along_y"],
        const["along_x"],
        const["own"],
        factor,
        edge,
        const["waves"],
        vel_index,
    )
    got = lax.all_to_all(sent, "freq", 0, 0, tiled=True)
    depth_image = call(sum_kernel, (2, 32, 64), [VM], 16)(got)
    return (wave.reshape(2, 1, 32, 512), depth_image)


def solution(mesh):
    return jax.shard_map(
        local,
        mesh=mesh,
        in_specs=(
            P(None, None, ("freq", "lat")),
            P(("freq", "lat"), None),
            P(("freq", "lat")),
            P(None, ("freq", "lat")),
            P(("freq", "lat")),
            P("freq"),
            P(),
            P(None, "lat", None),
        ),
        out_specs=(P(None, "freq", "lat", None), P(None, "lat", "freq")),
        check_vma=False,
    )
```

```python
import math

import jax
import jax.numpy as jnp
import ml_dtypes
import numpy as np
from jax import lax
from jax.experimental import pallas as pl
from jax.experimental.pallas import tpu as pltpu
from jax.sharding import PartitionSpec as P

NX = 512
NY = 512
TB = 32
MODES = 8
HALF = 256
SCALE = 1.0 / (NX * NY)
STEP = 2.0 * math.pi / 512

f32 = jnp.float32
bf16 = jnp.bfloat16
VM = pl.BlockSpec(memory_space=pltpu.VMEM)
SM = pl.BlockSpec(memory_space=pltpu.SMEM)
HBM = pl.BlockSpec(memory_space=pltpu.HBM)


def pair(table):
    table = np.asarray(table, np.float32)
    high = table.astype(ml_dtypes.bfloat16)
    low = (table - high.astype(np.float32)).astype(ml_dtypes.bfloat16)
    return np.stack([high, low])


def waves(bins):
    twice = 2 * np.asarray(bins)[None, :] + 1
    index = np.arange(HALF)[:, None]
    sine_index = np.where(index == 0, HALF, index)
    return (
        np.cos(np.pi / 512 * (index * twice % 1024)),
        np.sin(np.pi / 512 * (sine_index * twice % 1024)),
    )


def tables():
    cell = np.arange(TB)
    modes = np.cos(np.pi * np.arange(MODES)[:, None] * (cell[None, :] + 0.5) / TB)
    cosine, sine = waves(np.arange(512))
    along = [
        np.einsum("aj,iyj->yai", modes, t.reshape(HALF, 16, TB)).reshape(16 * MODES, HALF)
        for t in (cosine, sine)
    ]
    along = np.concatenate(along, 1)
    own = np.concatenate(
        [pair(t.reshape(HALF, 16, 32).transpose(1, 2, 0)) for t in (cosine, sine)], 0
    )
    own = own.transpose(1, 0, 2, 3).reshape(16, 128, HALF)
    first = [cosine[:, :HALF], sine[:, :HALF]]
    late = [cosine[:, HALF:], sine[:, HALF:]]
    waves_all = pair(np.stack([*first, *[t.T for t in first], *late]))
    return dict(along_y=pair(along), along_x=pair(along.T), own=own, waves=waves_all)


def split(value):
    high = value.astype(bf16)
    low = (value - high.astype(f32)).astype(bf16)
    return high, low


def mm(left, right):
    return jnp.dot(left, right, preferred_element_type=f32)


def dot3(left, right):
    return mm(
        jnp.concatenate([left[0], left[1], left[0]], 1),
        jnp.concatenate([right[0], right[0], right[1]], 0),
    )


def lanes(shape):
    return lax.broadcasted_iota(jnp.int32, shape, len(shape) - 1)


def turned(value, shift, axis=1):
    size = value.shape[axis]
    shift = shift % size
    return value if shift == 0 else pltpu.roll(value, shift, axis)


def cos_sin(turn):
    half = 0.5 * turn
    sq = half * half
    cosine = 1.0 / 479001600
    for c in (-1.0 / 3628800, 1.0 / 40320, -1.0 / 720, 1.0 / 24, -0.5, 1.0):
        cosine = cosine * sq + c
    sine = 1.0 / 6227020800
    for c in (-1.0 / 39916800, 1.0 / 362880, -1.0 / 5040, 1.0 / 120, -1.0 / 6, 1.0):
        sine = sine * sq + c
    sine = sine * half
    return 1.0 - 2.0 * sine * sine, 2.0 * sine * cosine


def shift_factor(wave_sq, kx, ky):
    vertical = wave_sq - kx * kx - ky * ky
    root = jnp.sqrt(jnp.abs(vertical))
    cosine, sine = cos_sin(root)
    moving = vertical > 0.0
    return jnp.where(moving, cosine, jnp.exp(-root)), jnp.where(moving, sine, 0.0)


def references_of(slow_ref, step):
    values = [slow_ref[step, i] for i in range(8)]
    refs = [
        (values[4 * g] + values[4 * g + 1] + values[4 * g + 2] + values[4 * g + 3]) * 0.25
        for g in range(2)
    ]
    return values, refs


def split_turns(velocity, step, slow_ref, freq_ref):
    values, refs = references_of(slow_ref, step)
    pairs = [cos_sin(freq_ref[0] * (values[i] - refs[i // 4])) for i in range(8)]
    low, mid, top = (velocity & 1) == 1, (velocity & 2) == 2, velocity >= 4
    out = []
    for p in range(2):
        level = [pairs[i][p] * SCALE for i in range(8)]
        level = [jnp.where(low, level[2 * i + 1], level[2 * i]) for i in range(4)]
        level = [jnp.where(mid, level[2 * i + 1], level[2 * i]) for i in range(2)]
        out.append(jnp.where(top, level[1], level[0]))
    return out[0], out[1], top


def no_first(value, axis):
    at = lax.broadcasted_iota(jnp.int32, value.shape, axis)
    return jnp.where(at > 0, value, 0.0)


def plus_i(u, v):
    return u[0] - v[1], u[1] + v[0]


def minus_i(u, v):
    return u[0] + v[1], u[1] - v[0]


def halves_of(value, axis, count):
    if axis == 0:
        return value[:count], value[count:]
    return value[:, :count], value[:, count:]


class Fetch:
    def __init__(self, sources, targets, sems):
        self.targets = targets
        self.copies = [
            pltpu.make_async_copy(s, t, sems.at[i]) for i, (s, t) in enumerate(zip(sources, targets))
        ]
        for copy in self.copies:
            copy.start()

    def take(self, *which):
        for i in which:
            self.copies[i].wait()
        out = [self.targets[i] for i in which]
        return out[0] if len(out) == 1 else out


def route_kernel(lat_ref, *refs):
    sources, out_ref, vel_ref = refs[:6], refs[6], refs[7]
    targets, sems = refs[8:14], refs[14]
    fetch = Fetch([*sources[:5], sources[5].at[0]], targets, sems)
    tile = fetch.take(0)[...]
    tile_f = tile.astype(f32)
    below = lax.broadcasted_iota(jnp.int32, (128, 128), 0) < lanes((128, 128))
    columns = []
    ranks = []
    for j in range(8):
        here = tile_f[:, 128 * j : 128 * (j + 1)]
        here_all = jnp.broadcast_to(here, (128, 128))
        columns.append(here_all.T)
        found = jnp.where((columns[j] == here_all) & below, 1.0, 0.0)
        for i in range(j):
            found = found + jnp.where(columns[i] == here_all, 1.0, 0.0)
        ranks.append(jnp.sum(found, axis=0, keepdims=True))
    rank = jnp.concatenate(ranks, 1).astype(jnp.int32)
    row_at = (tile >> 1) * 4 + (rank & 3)
    group_at = (tile & 1) * 2 + (rank >> 2)
    bin_ref, offset_ref, weight_ref, spectra_ref = fetch.take(1, 2, 3, 4)
    place = bin_ref[...]
    cell_x = (place >> 5).astype(f32) + offset_ref[0:1, :]
    cell_y = (place & 31).astype(f32) + offset_ref[1:2, :]
    values = jnp.concatenate(
        [
            spectra_ref[...],
            jnp.concatenate([weight_ref[...], cell_x, cell_y, jnp.zeros((5, 1024), f32)], 0),
            jnp.zeros((8, 1024), f32),
        ],
        0,
    )
    spread = jnp.concatenate([jnp.where(group_at == s, values, 0.0) for s in range(4)], 0)
    high = spread.astype(bf16)
    rest = spread - high.astype(f32)
    mid = rest.astype(bf16)
    low = (rest - mid.astype(f32)).astype(bf16)
    wide = jnp.concatenate([high, mid, low], 0)
    rows = lax.broadcasted_iota(jnp.int32, (512, 1024), 0)
    chosen = jnp.where(rows == row_at, 1.0, 0.0).astype(bf16)
    moved = lax.dot_general(
        chosen, wide, (((1,), (1,)), ((), ())), preferred_element_type=f32
    )
    out_ref[...] = (moved[:, :128] + moved[:, 128:256]) + moved[:, 256:]
    velocity = fetch.take(5)[...].astype(f32).astype(bf16)
    at = lax.broadcasted_iota(jnp.int32, (HALF, HALF), 0)
    flip = jnp.where(at + lanes((HALF, HALF)) == HALF - 1, 1.0, 0.0).astype(bf16)
    right = mm(velocity[:, HALF:], flip).astype(bf16)
    velocity = jnp.concatenate([velocity[:, :HALF], right], 1)
    at, along = lax.broadcasted_iota(jnp.int32, (32, 32), 0), lanes((32, 32))
    target = jnp.where(lat_ref[0] >= 8, 31 - at, at)
    vel_ref[...] = mm(jnp.where(along == target, 1.0, 0.0).astype(bf16), velocity)


def mode_cosines(mode, place):
    turns = mode * place * (1.0 / 64)
    half = (turns - jnp.round(turns)) * math.pi
    sq = half * half
    sine = 1.0 / 6227020800
    for c in (-1.0 / 39916800, 1.0 / 362880, -1.0 / 5040, 1.0 / 120, -1.0 / 6, 1.0):
        sine = sine * sq + c
    sine = sine * half
    return 1.0 - 2.0 * sine * sine


def factor_rows(wave_sq, kx, ky, ky_mirror):
    first = shift_factor(wave_sq, kx, ky)
    mirror = shift_factor(wave_sq, kx[:, :128], ky_mirror)
    return [jnp.concatenate([first[p], mirror[p]], 1) for p in range(2)]


def factor_kernel(freq_ref, slow_ref, factor_hbm, edge_ref, factor_ref, sems):
    leaving = []
    at = lanes((1, HALF))
    ky = at.astype(f32) * STEP
    ky_mirror = jnp.where(at[:, :128] == 0, 256, at[:, :128]).astype(f32) * STEP
    for step in range(2):
        values, refs = references_of(slow_ref, step)
        for g in range(2):
            wave = freq_ref[0] * refs[g]
            wave_sq = wave * wave

            def some_rows(k, carry):
                start = pl.multiple_of(k * 32, 32)
                row = lax.broadcasted_iota(jnp.int32, (32, HALF), 0) + start
                found = factor_rows(wave_sq, row.astype(f32) * STEP, ky, ky_mirror)
                for p in range(2):
                    factor_ref[step, g, p, pl.ds(start, 32), :] = found[p]
                return carry

            lax.fori_loop(0, 8, some_rows, 0)
            row = lax.broadcasted_iota(jnp.int32, (8, HALF), 0)
            row = jnp.where(row == 0, 256, row)
            found = factor_rows(wave_sq, row.astype(f32) * STEP, ky, ky_mirror)
            for p in range(2):
                edge_ref[step, g, p] = found[p]
            copy = pltpu.make_async_copy(
                factor_ref.at[step, g], factor_hbm.at[step, g], sems.at[2 * step + g]
            )
            copy.start()
            leaving.append(copy)
    for copy in leaving:
        copy.wait()


def solve_kernel(lat_ref, got_ref, *refs):
    slabs, out_ref, four_ref, sems = refs[:4], refs[4], refs[5], refs[6]
    fetch = Fetch(slabs, [four_ref.at[(lat_ref[0] & 3) ^ d] for d in range(4)], sems)
    turned_in = got_ref[...].T
    blocks = []
    mode = lax.broadcasted_iota(jnp.int32, (8, 1024), 0).astype(f32)
    eye_rows = lax.broadcasted_iota(jnp.int32, (64, 128), 0)
    eye = jnp.where(eye_rows == lanes((64, 128)), 1.0, 0.0)
    for t in range(2):
        both = jnp.concatenate(
            [turned_in[64 * t : 64 * t + 24], turned_in[64 * t + 32 : 64 * t + 56]], 1
        )
        along_x = mode_cosines(mode, both[17:18] + 0.5)
        along_y = mode_cosines(mode, both[18:19] + 0.5)
        basis = jnp.concatenate([along_x[a : a + 1] * along_y for a in range(8)], 0)
        wide = jnp.concatenate([basis, both[0:16], jnp.zeros((48, 1024), f32)], 0)
        system = lax.dot_general(
            basis * both[16:17],
            wide,
            (((1,), (1,)), ((), ())),
            preferred_element_type=f32,
            precision=lax.Precision.HIGHEST,
        )
        system = system + eye
        blocks.append([system[8 * a : 8 * a + 8] for a in range(8)])
    sub = lax.broadcasted_iota(jnp.int32, (8, 128), 0)
    for at in range(8):
        for inner in range(0, 8, 4):
            picked = [(8 * at + inner + i, inner + i) for i in range(4)]
            for t in range(2):
                mine = blocks[t]
                rows = [
                    jnp.broadcast_to(mine[at][s : s + 1], (8, 128)) for _, s in picked
                ]
                small = [
                    [jnp.broadcast_to(row[:, j : j + 1], (8, 128)) for j, _ in picked]
                    for row in rows
                ]
                count = len(picked)
                for p in range(count):
                    scale = 1.0 / small[p][p]
                    rows[p] = rows[p] * scale
                    small[p] = [v * scale for v in small[p]]
                    for i in range(count):
                        if i != p:
                            by = small[i][p]
                            rows[i] = rows[i] - by * rows[p]
                            small[i] = [
                                v - by * w if k > p else v
                                for k, (v, w) in enumerate(zip(small[i], small[p]))
                            ]
                for k in range(0, 8):
                    new = mine[k]
                    for row, (j, s) in zip(rows, picked):
                        new = new - mine[k][:, j : j + 1] * row
                    if k == at:
                        for row, (j, s) in zip(rows, picked):
                            new = jnp.where(sub == s, row, new)
                    mine[k] = new
    stacked = jnp.concatenate([blocks[t][a] for a in range(8) for t in range(2)], 0)
    final = stacked.T
    odd = (lax.broadcasted_iota(jnp.int32, (32, 128), 0) & 1) == 1
    for f in range(8):
        out_ref[32 * f : 32 * f + 32] = jnp.where(
            odd, final[72 + f : 73 + f], final[64 + f : 65 + f]
        )
    fetch.take(0, 1, 2, 3)


def store_spectrum(spec_ref, u, v, cols):
    first = minus_i(u, [no_first(t, 0) for t in v])
    second = plus_i([no_first(t, 0) for t in u], v)
    for k, value in enumerate((*first, *second)):
        spec_ref[k, :, cols] = value


def wave_pair(waves_ref, which):
    return waves_ref[0, which], waves_ref[1, which]


def own_dot(own_ref, rows_at, value):
    with_high = mm(own_ref[rows_at : rows_at + 64], value[0])
    return with_high[:32] + (with_high[32:] + mm(own_ref[rows_at : rows_at + 32], value[1]))


def shifted(spec_ref, factor_ref, edge_ref, g, start):
    cols, side = pl.ds(start, HALF), pl.ds(start, 128)

    def both_sides(ref, p):
        return jnp.concatenate([ref[g, p, :, side], ref[g, p, :, 128:HALF]], 1)

    fac = [both_sides(factor_ref, p) for p in range(2)]
    fac_edge = [jnp.concatenate([both_sides(edge_ref, p), fac[p][8:]], 0) for p in range(2)]
    s = [spec_ref[i, :, cols] for i in range(4)]
    up = (s[0] * fac[0] - s[1] * fac[1], s[0] * fac[1] + s[1] * fac[0])
    down = (s[2] * fac_edge[0] - s[3] * fac_edge[1], s[2] * fac_edge[1] + s[3] * fac_edge[0])
    even = split(jnp.concatenate([up[p] + no_first(down[p], 0) for p in range(2)], 1))
    odd = split(jnp.concatenate([no_first(up[p], 0) - down[p] for p in range(2)], 1))
    return even, odd


def fold_columns(value):
    left, right = value[:, :HALF], value[:, HALF:]
    return split(left + no_first(right, 1)), split(no_first(left, 1) - right)


def in_three(value):
    high = value.astype(bf16)
    rest = value - high.astype(f32)
    mid = rest.astype(bf16)
    return high, mid, (rest - mid.astype(f32)).astype(bf16)


def own_image(slab, real_ref):
    start = pl.multiple_of(32 * jnp.where(slab < 8, slab, 23 - slab), 32)
    value = real_ref[pl.ds(start, 32), :]
    at = lax.broadcasted_iota(jnp.int32, (32, 32), 0)
    target = jnp.where(slab >= 8, 31 - at, at)
    order = jnp.where(lanes((32, 32)) == target, 1.0, 0.0).astype(bf16)
    pieces = in_three(value)
    value = mm(order, pieces[0]) + mm(order, pieces[1]) + mm(order, pieces[2])
    at = lax.broadcasted_iota(jnp.int32, (HALF, HALF), 0)
    flip = jnp.where(at + lanes((HALF, HALF)) == HALF - 1, 1.0, 0.0).astype(bf16)
    right = mm(jnp.concatenate(in_three(value[:, HALF:]), 0), flip)
    right = right[:32] + right[32:64] + right[64:]
    return jnp.concatenate([value[:, :HALF], right], 1)


def own_field(step, own_back, waves_ref, velocity, slow_ref, freq_ref):
    even, odd = fold_columns(jnp.concatenate([own_back[0], own_back[1]], 0))
    sides = []
    for at in (0, 4):
        u, v = dot3(even, wave_pair(waves_ref, at)), dot3(odd, wave_pair(waves_ref, at + 1))
        sides.append(
            [
                plus_i(
                    halves_of(u[64 * g : 64 * g + 64], 0, 32),
                    halves_of(v[64 * g : 64 * g + 64], 0, 32),
                )
                for g in range(2)
            ]
        )
    back = [
        [jnp.concatenate([sides[0][g][p], sides[1][g][p]], 1) for p in range(2)] for g in range(2)
    ]
    cosine, sine, top = split_turns(velocity, step, slow_ref, freq_ref)
    picked = [jnp.where(top, back[1][p], back[0][p]) for p in range(2)]
    return (
        picked[0] * cosine - picked[1] * sine,
        picked[0] * sine + picked[1] * cosine,
    )


def grid_kernel(lat_ref, freq_ref, slow_ref, got_ref, *refs):
    slabs, refs = refs[:4], refs[4:]
    sources, wave_ref, out_ref = refs[:7], refs[7], refs[8]
    targets, slabs_ref, later_ref, sems = refs[9:16], *refs[16:19]
    spec_ref, own_back, back_ref, half_ref, real_ref = refs[19:]
    fetch = Fetch(
        [
            *sources[:2],
            sources[2].at[lat_ref[0]],
            sources[3].at[0],
            *sources[4:],
            *slabs,
            sources[3].at[1],
        ],
        [*targets, *[slabs_ref.at[(lat_ref[0] >> 2) ^ d] for d in range(4)], later_ref],
        sems,
    )
    rows = lax.broadcasted_iota(jnp.int32, (128, 128), 0)
    groups = lanes((128, 128)) >> 4
    stacked = []
    for p in range(2):
        value = got_ref[pl.ds(p, 128, stride=2), :]
        for k in (1, 2, 4):
            s_bit, g_bit = (rows & k) != 0, (groups & k) != 0
            down = turned(turned(value, k, 0), -16 * k, 1)
            up = turned(turned(value, -k, 0), 16 * k, 1)
            value = jnp.where(
                s_bit & ~g_bit, down, jnp.where(~s_bit & g_bit, up, value)
            )
        stacked.append(value)
    table = fetch.take(0)
    both = dot3(split(jnp.concatenate(stacked, 0)), (table[0], table[1]))
    u, v = (halves_of(t, 0, 128) for t in (both[:, :HALF], both[:, HALF:]))
    first = minus_i(u, [no_first(t, 1) for t in v])
    second = plus_i([no_first(t, 1) for t in u], v)
    table = fetch.take(1)
    for c, here in enumerate((first, second)):
        both = dot3((table[0], table[1]), split(jnp.concatenate(here, 1)))
        store_spectrum(
            spec_ref,
            halves_of(both[:HALF], 1, HALF),
            halves_of(both[HALF:], 1, HALF),
            pl.ds(HALF * c, HALF),
        )
    own_ref, factor_ref, edge_ref, waves_ref = fetch.take(2, 3, 4, 5)
    for g in range(2):
        for c in range(2):
            cols = pl.ds(HALF * c, HALF)
            even, odd = shifted(spec_ref, factor_ref, edge_ref.at[0], g, HALF * c)
            u = halves_of(dot3(wave_pair(waves_ref, 2), even), 1, HALF)
            v = halves_of(dot3(wave_pair(waves_ref, 3), odd), 1, HALF)
            first, second = plus_i(u, v), minus_i(u, v)
            for p in range(2):
                back_ref[g, p, :HALF, cols] = first[p]
                back_ref[g, p, HALF:, cols] = second[p]
    vel_ref = fetch.take(6)
    fetch.take(7, 8, 9, 10)

    def some_rows(k, carry):
        at = pl.ds(pl.multiple_of(k * 128, 128), 128)
        back = []
        for g in range(2):
            even, odd = fold_columns(
                jnp.concatenate([back_ref[g, p, at, :] for p in range(2)], 0)
            )
            u = halves_of(dot3(even, wave_pair(waves_ref, 0)), 0, 128)
            v = halves_of(dot3(odd, wave_pair(waves_ref, 1)), 0, 128)
            back.append((plus_i(u, v), minus_i(u, v)))
        slabs = [
            slabs_ref[jnp.where(k < 2, k, 5 - k), jnp.where(k < 2, i, 3 - i)] for i in range(4)
        ]
        velocity = jnp.concatenate(slabs, 0).astype(jnp.int32)
        fields = []
        for side in range(2):
            cosine, sine, top = split_turns(
                velocity[:, HALF * side : HALF * side + HALF], 0, slow_ref, freq_ref
            )
            picked = [jnp.where(top, back[1][side][p], back[0][side][p]) for p in range(2)]
            fields.append(
                jnp.concatenate(
                    [
                        picked[0] * cosine - picked[1] * sine,
                        picked[0] * sine + picked[1] * cosine,
                    ],
                    0,
                )
            )
        for side in range(2):
            real_ref[at, HALF * side : HALF * side + HALF] = fields[side][:128]
        u = halves_of(dot3(split(fields[0] + fields[1]), wave_pair(waves_ref, 2)), 0, 128)
        v = halves_of(dot3(split(fields[0] - fields[1]), wave_pair(waves_ref, 3)), 0, 128)
        first = minus_i(u, [no_first(t, 1) for t in v])
        second = plus_i([no_first(t, 1) for t in u], v)
        for p in range(2):
            half_ref[p, at, :HALF] = first[p]
            half_ref[p, at, HALF:] = second[p]
        return carry

    lax.fori_loop(0, 4, some_rows, 0)

    def some_columns(c, carry):
        cols = pl.ds(pl.multiple_of(c * HALF, HALF), HALF)
        top = jnp.concatenate([half_ref[p, :HALF, cols] for p in range(2)], 1)
        low = jnp.concatenate([half_ref[p, HALF:, cols] for p in range(2)], 1)
        u = halves_of(dot3(wave_pair(waves_ref, 0), split(top + low)), 1, HALF)
        v = halves_of(dot3(wave_pair(waves_ref, 1), split(top - low)), 1, HALF)
        store_spectrum(spec_ref, u, v, cols)
        return carry

    lax.fori_loop(0, 2, some_columns, 0)
    later_factor = fetch.take(11)

    def invert(k, carry):
        start = pl.multiple_of((k & 1) * HALF, HALF)
        cols = pl.ds(start, HALF)
        even, odd = shifted(spec_ref, later_factor, edge_ref.at[1], k >> 1, start)
        mine = plus_i(
            halves_of(own_dot(own_ref, 0, even), 1, HALF),
            halves_of(own_dot(own_ref, 64, odd), 1, HALF),
        )
        for p in range(2):
            own_back[k >> 1, 32 * p : 32 * p + 32, cols] = mine[p]
        return carry

    lax.fori_loop(0, 4, invert, 0)
    field = own_field(1, own_back, waves_ref, vel_ref[1], slow_ref, freq_ref)
    for p in range(2):
        wave_ref[p] = field[p]
    image = own_image(lat_ref[0], real_ref)
    upper = lanes((32, 128)) >= 64
    for d in range(8):
        col, pos = d // 2, d % 2
        first = turned(image[:, 128 * col : 128 * col + 128], -64 * pos)
        second = turned(field[0][:, 128 * col : 128 * col + 128], 64 - 64 * pos)
        out_ref[d] = jnp.where(upper, second, first)


def sum_kernel(got_ref, out_ref):
    total = got_ref[0]
    for d in range(1, 8):
        total = total + got_ref[d]
    out_ref[0] = total[:, :64]
    out_ref[1] = total[:, 64:]


def call(kernel, outs, in_specs, mega, scratch=(), out_specs=None):
    many = isinstance(outs, list)
    shapes = [jax.ShapeDtypeStruct(s, f32) for s in (outs if many else [outs])]
    return pl.pallas_call(
        kernel,
        out_shape=shapes if many else shapes[0],
        in_specs=in_specs,
        out_specs=out_specs or ([VM] * len(shapes) if many else VM),
        scratch_shapes=list(scratch),
        compiler_params=pltpu.CompilerParams(vmem_limit_bytes=mega * 1024 * 1024),
    )


def local(spectra, tile_route, bin_in_tile, trace_offset, weights, frequency, slowness, vel_index):
    const = tables()
    lat_at = lax.axis_index("lat").astype(jnp.int32).reshape(1)
    everyone = ("freq", "lat")
    sent, velocity = call(
        route_kernel,
        [(512, 128), (32, 512)],
        [SM] + [HBM] * 6,
        60,
        [
            pltpu.VMEM((1, 1024), jnp.int32),
            pltpu.VMEM((1, 1024), jnp.int32),
            pltpu.VMEM((2, 1024), f32),
            pltpu.VMEM((1, 1024), f32),
            pltpu.VMEM((16, 1024), f32),
            pltpu.VMEM((32, 512), jnp.int32),
            pltpu.SemaphoreType.DMA((6,)),
        ],
    )(
        lat_at,
        tile_route.reshape(1, 1024),
        bin_in_tile.reshape(1, 1024),
        trace_offset,
        weights.reshape(1, 1024),
        spectra.reshape(16, 1024),
        vel_index,
    )
    got = lax.all_to_all(sent.reshape(128, 4, 128), everyone, 0, 0, tiled=True)
    slabs = [velocity] + [
        lax.ppermute(velocity, "lat", [(i, i ^ d) for i in range(16)]) for d in (1, 2, 3)
    ]
    sent, slabs = call(
        solve_kernel,
        [(256, 128), (4, 32, 512)],
        [SM, VM] + [HBM] * 4,
        24,
        [pltpu.SemaphoreType.DMA((4,))],
        [VM, HBM],
    )(lat_at, got.reshape(512, 128), *slabs)
    got = lax.all_to_all(sent.reshape(128, 2, 128), everyone, 0, 0, tiled=True)
    slabs = [slabs] + [
        lax.ppermute(slabs, "lat", [(i, i ^ d) for i in range(16)]) for d in (4, 8, 12)
    ]
    factor, edge = call(
        factor_kernel,
        [(2, 2, 2, 256, 384), (2, 2, 2, 8, 384)],
        [SM, SM],
        59,
        [pltpu.VMEM((2, 2, 2, 256, 384), f32), pltpu.SemaphoreType.DMA((4,))],
        [HBM, VM],
    )(frequency, slowness)
    wave, sent = call(
        grid_kernel,
        [(2, 32, 512), (8, 32, 128)],
        [SM, SM, SM, VM] + [HBM] * 11,
        59,
        [
            pltpu.VMEM((2, 128, 512), bf16),
            pltpu.VMEM((2, 512, 128), bf16),
            pltpu.VMEM((128, 256), bf16),
            pltpu.VMEM((2, 2, 256, 384), f32),
            pltpu.VMEM((2, 2, 2, 8, 384), f32),
            pltpu.VMEM((2, 6, 256, 256), bf16),
            pltpu.VMEM((2, 32, 512), jnp.int32),
            pltpu.VMEM((4, 4, 32, 512), f32),
            pltpu.VMEM((2, 2, 256, 384), f32),
            pltpu.SemaphoreType.DMA((12,)),
            pltpu.VMEM((4, 256, 512), f32),
            pltpu.VMEM((2, 64, 512), f32),
            pltpu.VMEM((2, 2, 512, 512), f32),
            pltpu.VMEM((2, 512, 512), f32),
            pltpu.VMEM((512, 512), f32),
        ],
    )(
        lat_at,
        frequency,
        slowness,
        got.reshape(256, 128),
        *slabs,
        const["along_y"],
        const["along_x"],
        const["own"],
        factor,
        edge,
        const["waves"],
        vel_index,
    )
    got = lax.all_to_all(sent, "freq", 0, 0, tiled=True)
    depth_image = call(sum_kernel, (2, 32, 64), [VM], 16)(got)
    return (wave.reshape(2, 1, 32, 512), depth_image)


def solution(mesh):
    return jax.shard_map(
        local,
        mesh=mesh,
        in_specs=(
            P(None, None, ("freq", "lat")),
            P(("freq", "lat"), None),
            P(("freq", "lat")),
            P(None, ("freq", "lat")),
            P(("freq", "lat")),
            P("freq"),
            P(),
            P(None, "lat", None),
        ),
        out_specs=(P(None, "freq", "lat", None), P(None, "lat", "freq")),
        check_vma=False,
    )
```

```python
import math

import jax
import jax.numpy as jnp
import ml_dtypes
import numpy as np
from jax import lax
from jax.experimental import pallas as pl
from jax.experimental.pallas import tpu as pltpu
from jax.sharding import PartitionSpec as P

NX = 512
NY = 512
TB = 32
MODES = 8
HALF = 256
SCALE = 1.0 / (NX * NY)
STEP = 2.0 * math.pi / 512

f32 = jnp.float32
bf16 = jnp.bfloat16
VM = pl.BlockSpec(memory_space=pltpu.VMEM)
SM = pl.BlockSpec(memory_space=pltpu.SMEM)
HBM = pl.BlockSpec(memory_space=pltpu.HBM)


def pair(table):
    table = np.asarray(table, np.float32)
    high = table.astype(ml_dtypes.bfloat16)
    low = (table - high.astype(np.float32)).astype(ml_dtypes.bfloat16)
    return np.stack([high, low])


def waves(bins):
    twice = 2 * np.asarray(bins)[None, :] + 1
    index = np.arange(HALF)[:, None]
    sine_index = np.where(index == 0, HALF, index)
    return (
        np.cos(np.pi / 512 * (index * twice % 1024)),
        np.sin(np.pi / 512 * (sine_index * twice % 1024)),
    )


def tables():
    cell = np.arange(TB)
    modes = np.cos(np.pi * np.arange(MODES)[:, None] * (cell[None, :] + 0.5) / TB)
    cosine, sine = waves(np.arange(512))
    along = [
        np.einsum("aj,iyj->yai", modes, t.reshape(HALF, 16, TB)).reshape(16 * MODES, HALF)
        for t in (cosine, sine)
    ]
    along = np.concatenate(along, 1)
    own = np.concatenate(
        [pair(t.reshape(HALF, 16, 32).transpose(1, 2, 0)) for t in (cosine, sine)], 0
    )
    own = own.transpose(1, 0, 2, 3).reshape(16, 128, HALF)
    first = [cosine[:, :HALF], sine[:, :HALF]]
    late = [cosine[:, HALF:], sine[:, HALF:]]
    waves_all = pair(np.stack([*first, *[t.T for t in first], *late]))
    return dict(along_y=pair(along), along_x=pair(along.T), own=own, waves=waves_all)


def split(value):
    high = value.astype(bf16)
    low = (value - high.astype(f32)).astype(bf16)
    return high, low


def mm(left, right):
    return jnp.dot(left, right, preferred_element_type=f32)


def dot3(left, right):
    return mm(
        jnp.concatenate([left[0], left[1], left[0]], 1),
        jnp.concatenate([right[0], right[0], right[1]], 0),
    )


def lanes(shape):
    return lax.broadcasted_iota(jnp.int32, shape, len(shape) - 1)


def turned(value, shift, axis=1):
    size = value.shape[axis]
    shift = shift % size
    return value if shift == 0 else pltpu.roll(value, shift, axis)


def cos_sin(turn):
    half = 0.5 * turn
    sq = half * half
    cosine = 1.0 / 479001600
    for c in (-1.0 / 3628800, 1.0 / 40320, -1.0 / 720, 1.0 / 24, -0.5, 1.0):
        cosine = cosine * sq + c
    sine = 1.0 / 6227020800
    for c in (-1.0 / 39916800, 1.0 / 362880, -1.0 / 5040, 1.0 / 120, -1.0 / 6, 1.0):
        sine = sine * sq + c
    sine = sine * half
    return 1.0 - 2.0 * sine * sine, 2.0 * sine * cosine


def shift_factor(wave_sq, kx, ky):
    vertical = wave_sq - kx * kx - ky * ky
    root = jnp.sqrt(jnp.abs(vertical))
    cosine, sine = cos_sin(root)
    moving = vertical > 0.0
    return jnp.where(moving, cosine, jnp.exp(-root)), jnp.where(moving, sine, 0.0)


def references_of(slow_ref, step):
    values = [slow_ref[step, i] for i in range(8)]
    refs = [
        (values[4 * g] + values[4 * g + 1] + values[4 * g + 2] + values[4 * g + 3]) * 0.25
        for g in range(2)
    ]
    return values, refs


def split_turns(velocity, step, slow_ref, freq_ref):
    values, refs = references_of(slow_ref, step)
    pairs = [cos_sin(freq_ref[0] * (values[i] - refs[i // 4])) for i in range(8)]
    low, mid, top = (velocity & 1) == 1, (velocity & 2) == 2, velocity >= 4
    out = []
    for p in range(2):
        level = [pairs[i][p] * SCALE for i in range(8)]
        level = [jnp.where(low, level[2 * i + 1], level[2 * i]) for i in range(4)]
        level = [jnp.where(mid, level[2 * i + 1], level[2 * i]) for i in range(2)]
        out.append(jnp.where(top, level[1], level[0]))
    return out[0], out[1], top


def no_first(value, axis):
    at = lax.broadcasted_iota(jnp.int32, value.shape, axis)
    return jnp.where(at > 0, value, 0.0)


def plus_i(u, v):
    return u[0] - v[1], u[1] + v[0]


def minus_i(u, v):
    return u[0] + v[1], u[1] - v[0]


def halves_of(value, axis, count):
    if axis == 0:
        return value[:count], value[count:]
    return value[:, :count], value[:, count:]


class Fetch:
    def __init__(self, sources, targets, sems):
        self.targets = targets
        self.copies = [
            pltpu.make_async_copy(s, t, sems.at[i]) for i, (s, t) in enumerate(zip(sources, targets))
        ]
        for copy in self.copies:
            copy.start()

    def take(self, *which):
        for i in which:
            self.copies[i].wait()
        out = [self.targets[i] for i in which]
        return out[0] if len(out) == 1 else out


def route_kernel(lat_ref, *refs):
    sources, out_ref, vel_ref = refs[:6], refs[6], refs[7]
    targets, sems = refs[8:14], refs[14]
    fetch = Fetch([*sources[:5], sources[5].at[0]], targets, sems)
    tile = fetch.take(0)[...]
    tile_f = tile.astype(f32)
    below = lax.broadcasted_iota(jnp.int32, (128, 128), 0) < lanes((128, 128))
    columns = []
    ranks = []
    for j in range(8):
        here = tile_f[:, 128 * j : 128 * (j + 1)]
        here_all = jnp.broadcast_to(here, (128, 128))
        columns.append(here_all.T)
        found = jnp.where((columns[j] == here_all) & below, 1.0, 0.0)
        for i in range(j):
            found = found + jnp.where(columns[i] == here_all, 1.0, 0.0)
        ranks.append(jnp.sum(found, axis=0, keepdims=True))
    rank = jnp.concatenate(ranks, 1).astype(jnp.int32)
    row_at = (tile >> 1) * 4 + (rank & 3)
    group_at = (tile & 1) * 2 + (rank >> 2)
    bin_ref, offset_ref, weight_ref, spectra_ref = fetch.take(1, 2, 3, 4)
    place = bin_ref[...]
    cell_x = (place >> 5).astype(f32) + offset_ref[0:1, :]
    cell_y = (place & 31).astype(f32) + offset_ref[1:2, :]
    values = jnp.concatenate(
        [
            spectra_ref[...],
            jnp.concatenate([weight_ref[...], cell_x, cell_y, jnp.zeros((5, 1024), f32)], 0),
            jnp.zeros((8, 1024), f32),
        ],
        0,
    )
    spread = jnp.concatenate([jnp.where(group_at == s, values, 0.0) for s in range(4)], 0)
    high = spread.astype(bf16)
    rest = spread - high.astype(f32)
    mid = rest.astype(bf16)
    low = (rest - mid.astype(f32)).astype(bf16)
    wide = jnp.concatenate([high, mid, low], 0)
    rows = lax.broadcasted_iota(jnp.int32, (512, 1024), 0)
    chosen = jnp.where(rows == row_at, 1.0, 0.0).astype(bf16)
    moved = lax.dot_general(
        chosen, wide, (((1,), (1,)), ((), ())), preferred_element_type=f32
    )
    out_ref[...] = (moved[:, :128] + moved[:, 128:256]) + moved[:, 256:]
    velocity = fetch.take(5)[...].astype(f32).astype(bf16)
    at = lax.broadcasted_iota(jnp.int32, (HALF, HALF), 0)
    flip = jnp.where(at + lanes((HALF, HALF)) == HALF - 1, 1.0, 0.0).astype(bf16)
    right = mm(velocity[:, HALF:], flip).astype(bf16)
    velocity = jnp.concatenate([velocity[:, :HALF], right], 1)
    at, along = lax.broadcasted_iota(jnp.int32, (32, 32), 0), lanes((32, 32))
    target = jnp.where(lat_ref[0] >= 8, 31 - at, at)
    vel_ref[...] = mm(jnp.where(along == target, 1.0, 0.0).astype(bf16), velocity)


def mode_cosines(mode, place):
    turns = mode * place * (1.0 / 64)
    half = (turns - jnp.round(turns)) * math.pi
    sq = half * half
    sine = 1.0 / 6227020800
    for c in (-1.0 / 39916800, 1.0 / 362880, -1.0 / 5040, 1.0 / 120, -1.0 / 6, 1.0):
        sine = sine * sq + c
    sine = sine * half
    return 1.0 - 2.0 * sine * sine


def factor_rows(wave_sq, kx, ky, ky_mirror):
    first = shift_factor(wave_sq, kx, ky)
    mirror = shift_factor(wave_sq, kx[:, :128], ky_mirror)
    return [jnp.concatenate([first[p], mirror[p]], 1) for p in range(2)]


def factor_kernel(freq_ref, slow_ref, factor_hbm, edge_ref, factor_ref, sems):
    leaving = []
    at = lanes((1, HALF))
    ky = at.astype(f32) * STEP
    ky_mirror = jnp.where(at[:, :128] == 0, 256, at[:, :128]).astype(f32) * STEP
    for step in range(2):
        values, refs = references_of(slow_ref, step)
        for g in range(2):
            wave = freq_ref[0] * refs[g]
            wave_sq = wave * wave

            def some_rows(k, carry):
                start = pl.multiple_of(k * 32, 32)
                row = lax.broadcasted_iota(jnp.int32, (32, HALF), 0) + start
                found = factor_rows(wave_sq, row.astype(f32) * STEP, ky, ky_mirror)
                for p in range(2):
                    factor_ref[step, g, p, pl.ds(start, 32), :] = found[p]
                return carry

            lax.fori_loop(0, 8, some_rows, 0)
            row = lax.broadcasted_iota(jnp.int32, (8, HALF), 0)
            row = jnp.where(row == 0, 256, row)
            found = factor_rows(wave_sq, row.astype(f32) * STEP, ky, ky_mirror)
            for p in range(2):
                edge_ref[step, g, p] = found[p]
            copy = pltpu.make_async_copy(
                factor_ref.at[step, g], factor_hbm.at[step, g], sems.at[2 * step + g]
            )
            copy.start()
            leaving.append(copy)
    for copy in leaving:
        copy.wait()


def solve_kernel(lat_ref, got_ref, *refs):
    slabs, out_ref, four_ref, sems = refs[:4], refs[4], refs[5], refs[6]
    fetch = Fetch(slabs, [four_ref.at[(lat_ref[0] & 3) ^ d] for d in range(4)], sems)
    turned_in = got_ref[...].T
    blocks = []
    mode = lax.broadcasted_iota(jnp.int32, (8, 1024), 0).astype(f32)
    eye_rows = lax.broadcasted_iota(jnp.int32, (64, 128), 0)
    eye = jnp.where(eye_rows == lanes((64, 128)), 1.0, 0.0)
    for t in range(2):
        both = jnp.concatenate(
            [turned_in[64 * t : 64 * t + 24], turned_in[64 * t + 32 : 64 * t + 56]], 1
        )
        along_x = mode_cosines(mode, both[17:18] + 0.5)
        along_y = mode_cosines(mode, both[18:19] + 0.5)
        basis = jnp.concatenate([along_x[a : a + 1] * along_y for a in range(8)], 0)
        wide = jnp.concatenate([basis, both[0:16], jnp.zeros((48, 1024), f32)], 0)
        system = lax.dot_general(
            basis * both[16:17],
            wide,
            (((1,), (1,)), ((), ())),
            preferred_element_type=f32,
            precision=lax.Precision.HIGHEST,
        )
        system = system + eye
        blocks.append([system[8 * a : 8 * a + 8] for a in range(8)])
    sub = lax.broadcasted_iota(jnp.int32, (8, 128), 0)
    for at in range(8):
        for inner in range(0, 8, 4):
            picked = [(8 * at + inner + i, inner + i) for i in range(4)]
            for t in range(2):
                mine = blocks[t]
                rows = [
                    jnp.broadcast_to(mine[at][s : s + 1], (8, 128)) for _, s in picked
                ]
                small = [
                    [jnp.broadcast_to(row[:, j : j + 1], (8, 128)) for j, _ in picked]
                    for row in rows
                ]
                count = len(picked)
                for p in range(count):
                    scale = 1.0 / small[p][p]
                    rows[p] = rows[p] * scale
                    small[p] = [v * scale for v in small[p]]
                    for i in range(count):
                        if i != p:
                            by = small[i][p]
                            rows[i] = rows[i] - by * rows[p]
                            small[i] = [
                                v - by * w if k > p else v
                                for k, (v, w) in enumerate(zip(small[i], small[p]))
                            ]
                for k in range(0, 8):
                    new = mine[k]
                    for row, (j, s) in zip(rows, picked):
                        new = new - mine[k][:, j : j + 1] * row
                    if k == at:
                        for row, (j, s) in zip(rows, picked):
                            new = jnp.where(sub == s, row, new)
                    mine[k] = new
    stacked = jnp.concatenate([blocks[t][a] for a in range(8) for t in range(2)], 0)
    final = stacked.T
    odd = (lax.broadcasted_iota(jnp.int32, (32, 128), 0) & 1) == 1
    for f in range(8):
        out_ref[32 * f : 32 * f + 32] = jnp.where(
            odd, final[72 + f : 73 + f], final[64 + f : 65 + f]
        )
    fetch.take(0, 1, 2, 3)


def store_spectrum(spec_ref, u, v, cols):
    first = minus_i(u, [no_first(t, 0) for t in v])
    second = plus_i([no_first(t, 0) for t in u], v)
    for k, value in enumerate((*first, *second)):
        spec_ref[k, :, cols] = value


def wave_pair(waves_ref, which):
    return waves_ref[0, which], waves_ref[1, which]


def own_dot(own_ref, rows_at, value):
    with_high = mm(own_ref[rows_at : rows_at + 64], value[0])
    return with_high[:32] + (with_high[32:] + mm(own_ref[rows_at : rows_at + 32], value[1]))


def shifted(spec_ref, factor_ref, edge_ref, g, start):
    cols, side = pl.ds(start, HALF), pl.ds(start, 128)

    def both_sides(ref, p):
        return jnp.concatenate([ref[g, p, :, side], ref[g, p, :, 128:HALF]], 1)

    fac = [both_sides(factor_ref, p) for p in range(2)]
    fac_edge = [jnp.concatenate([both_sides(edge_ref, p), fac[p][8:]], 0) for p in range(2)]
    s = [spec_ref[i, :, cols] for i in range(4)]
    up = (s[0] * fac[0] - s[1] * fac[1], s[0] * fac[1] + s[1] * fac[0])
    down = (s[2] * fac_edge[0] - s[3] * fac_edge[1], s[2] * fac_edge[1] + s[3] * fac_edge[0])
    even = split(jnp.concatenate([up[p] + no_first(down[p], 0) for p in range(2)], 1))
    odd = split(jnp.concatenate([no_first(up[p], 0) - down[p] for p in range(2)], 1))
    return even, odd


def fold_columns(value):
    left, right = value[:, :HALF], value[:, HALF:]
    return split(left + no_first(right, 1)), split(no_first(left, 1) - right)


def in_three(value):
    high = value.astype(bf16)
    rest = value - high.astype(f32)
    mid = rest.astype(bf16)
    return high, mid, (rest - mid.astype(f32)).astype(bf16)


def own_image(slab, real_ref):
    start = pl.multiple_of(32 * jnp.where(slab < 8, slab, 23 - slab), 32)
    value = real_ref[pl.ds(start, 32), :]
    at = lax.broadcasted_iota(jnp.int32, (32, 32), 0)
    target = jnp.where(slab >= 8, 31 - at, at)
    order = jnp.where(lanes((32, 32)) == target, 1.0, 0.0).astype(bf16)
    pieces = in_three(value)
    value = mm(order, pieces[0]) + mm(order, pieces[1]) + mm(order, pieces[2])
    at = lax.broadcasted_iota(jnp.int32, (HALF, HALF), 0)
    flip = jnp.where(at + lanes((HALF, HALF)) == HALF - 1, 1.0, 0.0).astype(bf16)
    right = mm(jnp.concatenate(in_three(value[:, HALF:]), 0), flip)
    right = right[:32] + right[32:64] + right[64:]
    return jnp.concatenate([value[:, :HALF], right], 1)


def own_field(step, own_back, waves_ref, velocity, slow_ref, freq_ref):
    even, odd = fold_columns(jnp.concatenate([own_back[0], own_back[1]], 0))
    sides = []
    for at in (0, 4):
        u, v = dot3(even, wave_pair(waves_ref, at)), dot3(odd, wave_pair(waves_ref, at + 1))
        sides.append(
            [
                plus_i(
                    halves_of(u[64 * g : 64 * g + 64], 0, 32),
                    halves_of(v[64 * g : 64 * g + 64], 0, 32),
                )
                for g in range(2)
            ]
        )
    back = [
        [jnp.concatenate([sides[0][g][p], sides[1][g][p]], 1) for p in range(2)] for g in range(2)
    ]
    cosine, sine, top = split_turns(velocity, step, slow_ref, freq_ref)
    picked = [jnp.where(top, back[1][p], back[0][p]) for p in range(2)]
    return (
        picked[0] * cosine - picked[1] * sine,
        picked[0] * sine + picked[1] * cosine,
    )


def grid_kernel(lat_ref, freq_ref, slow_ref, got_ref, *refs):
    slabs, refs = refs[:4], refs[4:]
    sources, wave_ref, out_ref = refs[:7], refs[7], refs[8]
    targets, slabs_ref, later_ref, sems = refs[9:16], *refs[16:19]
    spec_ref, own_back, back_ref, half_ref, real_ref = refs[19:]
    fetch = Fetch(
        [
            *sources[:2],
            sources[2].at[lat_ref[0]],
            sources[3].at[0],
            *sources[4:],
            *slabs,
            sources[3].at[1],
        ],
        [*targets, *[slabs_ref.at[(lat_ref[0] >> 2) ^ d] for d in range(4)], later_ref],
        sems,
    )
    rows = lax.broadcasted_iota(jnp.int32, (128, 128), 0)
    groups = lanes((128, 128)) >> 4
    stacked = []
    for p in range(2):
        value = got_ref[pl.ds(p, 128, stride=2), :]
        for k in (1, 2, 4):
            s_bit, g_bit = (rows & k) != 0, (groups & k) != 0
            down = turned(turned(value, k, 0), -16 * k, 1)
            up = turned(turned(value, -k, 0), 16 * k, 1)
            value = jnp.where(
                s_bit & ~g_bit, down, jnp.where(~s_bit & g_bit, up, value)
            )
        stacked.append(value)
    table = fetch.take(0)
    both = dot3(split(jnp.concatenate(stacked, 0)), (table[0], table[1]))
    u, v = (halves_of(t, 0, 128) for t in (both[:, :HALF], both[:, HALF:]))
    first = minus_i(u, [no_first(t, 1) for t in v])
    second = plus_i([no_first(t, 1) for t in u], v)
    table = fetch.take(1)
    for c, here in enumerate((first, second)):
        both = dot3((table[0], table[1]), split(jnp.concatenate(here, 1)))
        store_spectrum(
            spec_ref,
            halves_of(both[:HALF], 1, HALF),
            halves_of(both[HALF:], 1, HALF),
            pl.ds(HALF * c, HALF),
        )
    own_ref, factor_ref, edge_ref, waves_ref = fetch.take(2, 3, 4, 5)
    for g in range(2):
        for c in range(2):
            cols = pl.ds(HALF * c, HALF)
            even, odd = shifted(spec_ref, factor_ref, edge_ref.at[0], g, HALF * c)
            u = halves_of(dot3(wave_pair(waves_ref, 2), even), 1, HALF)
            v = halves_of(dot3(wave_pair(waves_ref, 3), odd), 1, HALF)
            first, second = plus_i(u, v), minus_i(u, v)
            for p in range(2):
                back_ref[g, p, :HALF, cols] = first[p]
                back_ref[g, p, HALF:, cols] = second[p]
    vel_ref = fetch.take(6)
    fetch.take(7, 8, 9, 10)

    def some_rows(k, carry):
        at = pl.ds(pl.multiple_of(k * 128, 128), 128)
        back = []
        for g in range(2):
            even, odd = fold_columns(
                jnp.concatenate([back_ref[g, p, at, :] for p in range(2)], 0)
            )
            u = halves_of(dot3(even, wave_pair(waves_ref, 0)), 0, 128)
            v = halves_of(dot3(odd, wave_pair(waves_ref, 1)), 0, 128)
            back.append((plus_i(u, v), minus_i(u, v)))
        slabs = [
            slabs_ref[jnp.where(k < 2, k, 5 - k), jnp.where(k < 2, i, 3 - i)] for i in range(4)
        ]
        velocity = jnp.concatenate(slabs, 0).astype(jnp.int32)
        fields = []
        for side in range(2):
            cosine, sine, top = split_turns(
                velocity[:, HALF * side : HALF * side + HALF], 0, slow_ref, freq_ref
            )
            picked = [jnp.where(top, back[1][side][p], back[0][side][p]) for p in range(2)]
            fields.append(
                jnp.concatenate(
                    [
                        picked[0] * cosine - picked[1] * sine,
                        picked[0] * sine + picked[1] * cosine,
                    ],
                    0,
                )
            )
        for side in range(2):
            real_ref[at, HALF * side : HALF * side + HALF] = fields[side][:128]
        u = halves_of(dot3(split(fields[0] + fields[1]), wave_pair(waves_ref, 2)), 0, 128)
        v = halves_of(dot3(split(fields[0] - fields[1]), wave_pair(waves_ref, 3)), 0, 128)
        first = minus_i(u, [no_first(t, 1) for t in v])
        second = plus_i([no_first(t, 1) for t in u], v)
        for p in range(2):
            half_ref[p, at, :HALF] = first[p]
            half_ref[p, at, HALF:] = second[p]
        return carry

    lax.fori_loop(0, 4, some_rows, 0, unroll=True)

    def some_columns(c, carry):
        cols = pl.ds(pl.multiple_of(c * HALF, HALF), HALF)
        top = jnp.concatenate([half_ref[p, :HALF, cols] for p in range(2)], 1)
        low = jnp.concatenate([half_ref[p, HALF:, cols] for p in range(2)], 1)
        u = halves_of(dot3(wave_pair(waves_ref, 0), split(top + low)), 1, HALF)
        v = halves_of(dot3(wave_pair(waves_ref, 1), split(top - low)), 1, HALF)
        store_spectrum(spec_ref, u, v, cols)
        return carry

    lax.fori_loop(0, 2, some_columns, 0, unroll=True)
    later_factor = fetch.take(11)

    def invert(k, carry):
        start = pl.multiple_of((k & 1) * HALF, HALF)
        cols = pl.ds(start, HALF)
        even, odd = shifted(spec_ref, later_factor, edge_ref.at[1], k >> 1, start)
        mine = plus_i(
            halves_of(own_dot(own_ref, 0, even), 1, HALF),
            halves_of(own_dot(own_ref, 64, odd), 1, HALF),
        )
        for p in range(2):
            own_back[k >> 1, 32 * p : 32 * p + 32, cols] = mine[p]
        return carry

    lax.fori_loop(0, 4, invert, 0, unroll=True)
    field = own_field(1, own_back, waves_ref, vel_ref[1], slow_ref, freq_ref)
    for p in range(2):
        wave_ref[p] = field[p]
    image = own_image(lat_ref[0], real_ref)
    upper = lanes((32, 128)) >= 64
    for d in range(8):
        col, pos = d // 2, d % 2
        first = turned(image[:, 128 * col : 128 * col + 128], -64 * pos)
        second = turned(field[0][:, 128 * col : 128 * col + 128], 64 - 64 * pos)
        out_ref[d] = jnp.where(upper, second, first)


def sum_kernel(got_ref, out_ref):
    total = got_ref[0]
    for d in range(1, 8):
        total = total + got_ref[d]
    out_ref[0] = total[:, :64]
    out_ref[1] = total[:, 64:]


def call(kernel, outs, in_specs, mega, scratch=(), out_specs=None):
    many = isinstance(outs, list)
    shapes = [jax.ShapeDtypeStruct(s, f32) for s in (outs if many else [outs])]
    return pl.pallas_call(
        kernel,
        out_shape=shapes if many else shapes[0],
        in_specs=in_specs,
        out_specs=out_specs or ([VM] * len(shapes) if many else VM),
        scratch_shapes=list(scratch),
        compiler_params=pltpu.CompilerParams(vmem_limit_bytes=mega * 1024 * 1024),
    )


def local(spectra, tile_route, bin_in_tile, trace_offset, weights, frequency, slowness, vel_index):
    const = tables()
    lat_at = lax.axis_index("lat").astype(jnp.int32).reshape(1)
    everyone = ("freq", "lat")
    sent, velocity = call(
        route_kernel,
        [(512, 128), (32, 512)],
        [SM] + [HBM] * 6,
        60,
        [
            pltpu.VMEM((1, 1024), jnp.int32),
            pltpu.VMEM((1, 1024), jnp.int32),
            pltpu.VMEM((2, 1024), f32),
            pltpu.VMEM((1, 1024), f32),
            pltpu.VMEM((16, 1024), f32),
            pltpu.VMEM((32, 512), jnp.int32),
            pltpu.SemaphoreType.DMA((6,)),
        ],
    )(
        lat_at,
        tile_route.reshape(1, 1024),
        bin_in_tile.reshape(1, 1024),
        trace_offset,
        weights.reshape(1, 1024),
        spectra.reshape(16, 1024),
        vel_index,
    )
    got = lax.all_to_all(sent.reshape(128, 4, 128), everyone, 0, 0, tiled=True)
    slabs = [velocity] + [
        lax.ppermute(velocity, "lat", [(i, i ^ d) for i in range(16)]) for d in (1, 2, 3)
    ]
    sent, slabs = call(
        solve_kernel,
        [(256, 128), (4, 32, 512)],
        [SM, VM] + [HBM] * 4,
        24,
        [pltpu.SemaphoreType.DMA((4,))],
        [VM, HBM],
    )(lat_at, got.reshape(512, 128), *slabs)
    got = lax.all_to_all(sent.reshape(128, 2, 128), everyone, 0, 0, tiled=True)
    slabs = [slabs] + [
        lax.ppermute(slabs, "lat", [(i, i ^ d) for i in range(16)]) for d in (4, 8, 12)
    ]
    factor, edge = call(
        factor_kernel,
        [(2, 2, 2, 256, 384), (2, 2, 2, 8, 384)],
        [SM, SM],
        59,
        [pltpu.VMEM((2, 2, 2, 256, 384), f32), pltpu.SemaphoreType.DMA((4,))],
        [HBM, VM],
    )(frequency, slowness)
    wave, sent = call(
        grid_kernel,
        [(2, 32, 512), (8, 32, 128)],
        [SM, SM, SM, VM] + [HBM] * 11,
        59,
        [
            pltpu.VMEM((2, 128, 512), bf16),
            pltpu.VMEM((2, 512, 128), bf16),
            pltpu.VMEM((128, 256), bf16),
            pltpu.VMEM((2, 2, 256, 384), f32),
            pltpu.VMEM((2, 2, 2, 8, 384), f32),
            pltpu.VMEM((2, 6, 256, 256), bf16),
            pltpu.VMEM((2, 32, 512), jnp.int32),
            pltpu.VMEM((4, 4, 32, 512), f32),
            pltpu.VMEM((2, 2, 256, 384), f32),
            pltpu.SemaphoreType.DMA((12,)),
            pltpu.VMEM((4, 256, 512), f32),
            pltpu.VMEM((2, 64, 512), f32),
            pltpu.VMEM((2, 2, 512, 512), f32),
            pltpu.VMEM((2, 512, 512), f32),
            pltpu.VMEM((512, 512), f32),
        ],
    )(
        lat_at,
        frequency,
        slowness,
        got.reshape(256, 128),
        *slabs,
        const["along_y"],
        const["along_x"],
        const["own"],
        factor,
        edge,
        const["waves"],
        vel_index,
    )
    got = lax.all_to_all(sent, "freq", 0, 0, tiled=True)
    depth_image = call(sum_kernel, (2, 32, 64), [VM], 16)(got)
    return (wave.reshape(2, 1, 32, 512), depth_image)


def solution(mesh):
    return jax.shard_map(
        local,
        mesh=mesh,
        in_specs=(
            P(None, None, ("freq", "lat")),
            P(("freq", "lat"), None),
            P(("freq", "lat")),
            P(None, ("freq", "lat")),
            P(("freq", "lat")),
            P("freq"),
            P(),
            P(None, "lat", None),
        ),
        out_specs=(P(None, "freq", "lat", None), P(None, "lat", "freq")),
        check_vma=False,
    )
```

```python
import math

import jax
import jax.numpy as jnp
import ml_dtypes
import numpy as np
from jax import lax
from jax.experimental import pallas as pl
from jax.experimental.pallas import tpu as pltpu
from jax.sharding import PartitionSpec as P

NX = 512
NY = 512
TB = 32
MODES = 8
HALF = 256
SCALE = 1.0 / (NX * NY)
STEP = 2.0 * math.pi / 512

f32 = jnp.float32
bf16 = jnp.bfloat16
VM = pl.BlockSpec(memory_space=pltpu.VMEM)
SM = pl.BlockSpec(memory_space=pltpu.SMEM)
HBM = pl.BlockSpec(memory_space=pltpu.HBM)


def pair(table):
    table = np.asarray(table, np.float32)
    high = table.astype(ml_dtypes.bfloat16)
    low = (table - high.astype(np.float32)).astype(ml_dtypes.bfloat16)
    return np.stack([high, low])


def waves(bins):
    twice = 2 * np.asarray(bins)[None, :] + 1
    index = np.arange(HALF)[:, None]
    sine_index = np.where(index == 0, HALF, index)
    return (
        np.cos(np.pi / 512 * (index * twice % 1024)),
        np.sin(np.pi / 512 * (sine_index * twice % 1024)),
    )


def tables():
    cell = np.arange(TB)
    modes = np.cos(np.pi * np.arange(MODES)[:, None] * (cell[None, :] + 0.5) / TB)
    cosine, sine = waves(np.arange(512))
    along = [
        np.einsum("aj,iyj->yai", modes, t.reshape(HALF, 16, TB)).reshape(16 * MODES, HALF)
        for t in (cosine, sine)
    ]
    along = np.concatenate(along, 1)
    own = np.concatenate(
        [pair(t.reshape(HALF, 16, 32).transpose(1, 2, 0)) for t in (cosine, sine)], 0
    )
    own = own.transpose(1, 0, 2, 3).reshape(16, 128, HALF)
    first = [cosine[:, :HALF], sine[:, :HALF]]
    late = [cosine[:, HALF:], sine[:, HALF:]]
    waves_all = pair(np.stack([*first, *[t.T for t in first], *late]))
    return dict(along_y=pair(along), along_x=pair(along.T), own=own, waves=waves_all)


def split(value):
    high = value.astype(bf16)
    low = (value - high.astype(f32)).astype(bf16)
    return high, low


def mm(left, right):
    return jnp.dot(left, right, preferred_element_type=f32)


def dot3(left, right):
    return mm(
        jnp.concatenate([left[0], left[1], left[0]], 1),
        jnp.concatenate([right[0], right[0], right[1]], 0),
    )


def lanes(shape):
    return lax.broadcasted_iota(jnp.int32, shape, len(shape) - 1)


def turned(value, shift, axis=1):
    size = value.shape[axis]
    shift = shift % size
    return value if shift == 0 else pltpu.roll(value, shift, axis)


def cos_sin(turn):
    half = 0.5 * turn
    sq = half * half
    cosine = -1.0 / 3628800
    for c in (1.0 / 40320, -1.0 / 720, 1.0 / 24, -0.5, 1.0):
        cosine = cosine * sq + c
    sine = -1.0 / 39916800
    for c in (1.0 / 362880, -1.0 / 5040, 1.0 / 120, -1.0 / 6, 1.0):
        sine = sine * sq + c
    sine = sine * half
    return 1.0 - 2.0 * sine * sine, 2.0 * sine * cosine


def shift_factor(wave_sq, kx, ky):
    vertical = wave_sq - kx * kx - ky * ky
    size = jnp.maximum(jnp.abs(vertical), 1e-30)
    root = size * lax.rsqrt(size)
    cosine, sine = cos_sin(root)
    moving = vertical > 0.0
    return jnp.where(moving, cosine, jnp.exp(-root)), jnp.where(moving, sine, 0.0)


def references_of(slow_ref, step):
    values = [slow_ref[step, i] for i in range(8)]
    refs = [
        (values[4 * g] + values[4 * g + 1] + values[4 * g + 2] + values[4 * g + 3]) * 0.25
        for g in range(2)
    ]
    return values, refs


def split_turns(velocity, step, slow_ref, freq_ref):
    values, refs = references_of(slow_ref, step)
    pairs = [cos_sin(freq_ref[0] * (values[i] - refs[i // 4])) for i in range(8)]
    low, mid, top = (velocity & 1) == 1, (velocity & 2) == 2, velocity >= 4
    out = []
    for p in range(2):
        level = [pairs[i][p] * SCALE for i in range(8)]
        level = [jnp.where(low, level[2 * i + 1], level[2 * i]) for i in range(4)]
        level = [jnp.where(mid, level[2 * i + 1], level[2 * i]) for i in range(2)]
        out.append(jnp.where(top, level[1], level[0]))
    return out[0], out[1], top


def no_first(value, axis):
    at = lax.broadcasted_iota(jnp.int32, value.shape, axis)
    return jnp.where(at > 0, value, 0.0)


def plus_i(u, v):
    return u[0] - v[1], u[1] + v[0]


def minus_i(u, v):
    return u[0] + v[1], u[1] - v[0]


def halves_of(value, axis, count):
    if axis == 0:
        return value[:count], value[count:]
    return value[:, :count], value[:, count:]


class Fetch:
    def __init__(self, sources, targets, sems):
        self.targets = targets
        self.copies = [
            pltpu.make_async_copy(s, t, sems.at[i]) for i, (s, t) in enumerate(zip(sources, targets))
        ]
        for copy in self.copies:
            copy.start()

    def take(self, *which):
        for i in which:
            self.copies[i].wait()
        out = [self.targets[i] for i in which]
        return out[0] if len(out) == 1 else out


def route_kernel(lat_ref, *refs):
    sources, out_ref, vel_ref = refs[:6], refs[6], refs[7]
    targets, sems = refs[8:14], refs[14]
    fetch = Fetch([*sources[:5], sources[5].at[0]], targets, sems)
    tile = fetch.take(0)[...]
    tile_f = tile.astype(f32)
    below = lax.broadcasted_iota(jnp.int32, (128, 128), 0) < lanes((128, 128))
    columns = []
    ranks = []
    for j in range(8):
        here = tile_f[:, 128 * j : 128 * (j + 1)]
        here_all = jnp.broadcast_to(here, (128, 128))
        columns.append(here_all.T)
        found = jnp.where((columns[j] == here_all) & below, 1.0, 0.0)
        for i in range(j):
            found = found + jnp.where(columns[i] == here_all, 1.0, 0.0)
        ranks.append(jnp.sum(found, axis=0, keepdims=True))
    rank = jnp.concatenate(ranks, 1).astype(jnp.int32)
    row_at = (tile >> 1) * 4 + (rank & 3)
    group_at = (tile & 1) * 2 + (rank >> 2)
    bin_ref, offset_ref, weight_ref, spectra_ref = fetch.take(1, 2, 3, 4)
    place = bin_ref[...]
    cell_x = (place >> 5).astype(f32) + offset_ref[0:1, :]
    cell_y = (place & 31).astype(f32) + offset_ref[1:2, :]
    values = jnp.concatenate(
        [
            spectra_ref[...],
            jnp.concatenate([weight_ref[...], cell_x, cell_y, jnp.zeros((5, 1024), f32)], 0),
            jnp.zeros((8, 1024), f32),
        ],
        0,
    )
    spread = jnp.concatenate([jnp.where(group_at == s, values, 0.0) for s in range(4)], 0)
    high = spread.astype(bf16)
    rest = spread - high.astype(f32)
    mid = rest.astype(bf16)
    low = (rest - mid.astype(f32)).astype(bf16)
    wide = jnp.concatenate([high, mid, low], 0)
    rows = lax.broadcasted_iota(jnp.int32, (512, 1024), 0)
    chosen = jnp.where(rows == row_at, 1.0, 0.0).astype(bf16)
    moved = lax.dot_general(
        chosen, wide, (((1,), (1,)), ((), ())), preferred_element_type=f32
    )
    out_ref[...] = (moved[:, :128] + moved[:, 128:256]) + moved[:, 256:]
    velocity = fetch.take(5)[...].astype(f32).astype(bf16)
    at = lax.broadcasted_iota(jnp.int32, (HALF, HALF), 0)
    flip = jnp.where(at + lanes((HALF, HALF)) == HALF - 1, 1.0, 0.0).astype(bf16)
    right = mm(velocity[:, HALF:], flip).astype(bf16)
    velocity = jnp.concatenate([velocity[:, :HALF], right], 1)
    at, along = lax.broadcasted_iota(jnp.int32, (32, 32), 0), lanes((32, 32))
    target = jnp.where(lat_ref[0] >= 8, 31 - at, at)
    vel_ref[...] = mm(jnp.where(along == target, 1.0, 0.0).astype(bf16), velocity)


def mode_cosines(mode, place):
    turns = mode * place * (1.0 / 64)
    half = (turns - jnp.round(turns)) * math.pi
    sq = half * half
    sine = 1.0 / 6227020800
    for c in (-1.0 / 39916800, 1.0 / 362880, -1.0 / 5040, 1.0 / 120, -1.0 / 6, 1.0):
        sine = sine * sq + c
    sine = sine * half
    return 1.0 - 2.0 * sine * sine


def factor_rows(wave_sq, kx, ky, ky_mirror):
    first = shift_factor(wave_sq, kx, ky)
    mirror = shift_factor(wave_sq, kx[:, :128], ky_mirror)
    return [jnp.concatenate([first[p], mirror[p]], 1) for p in range(2)]


def factor_kernel(freq_ref, slow_ref, factor_hbm, edge_ref, factor_ref, sems):
    leaving = []
    at = lanes((1, HALF))
    ky = at.astype(f32) * STEP
    ky_mirror = jnp.where(at[:, :128] == 0, 256, at[:, :128]).astype(f32) * STEP
    for step in range(2):
        values, refs = references_of(slow_ref, step)
        for g in range(2):
            wave = freq_ref[0] * refs[g]
            wave_sq = wave * wave

            def some_rows(k, carry):
                start = pl.multiple_of(k * 32, 32)
                row = lax.broadcasted_iota(jnp.int32, (32, HALF), 0) + start
                found = factor_rows(wave_sq, row.astype(f32) * STEP, ky, ky_mirror)
                for p in range(2):
                    factor_ref[step, g, p, pl.ds(start, 32), :] = found[p]
                return carry

            lax.fori_loop(0, 8, some_rows, 0, unroll=4)
            row = lax.broadcasted_iota(jnp.int32, (8, HALF), 0)
            row = jnp.where(row == 0, 256, row)
            found = factor_rows(wave_sq, row.astype(f32) * STEP, ky, ky_mirror)
            for p in range(2):
                edge_ref[step, g, p] = found[p]
            copy = pltpu.make_async_copy(
                factor_ref.at[step, g], factor_hbm.at[step, g], sems.at[2 * step + g]
            )
            copy.start()
            leaving.append(copy)
    for copy in leaving:
        copy.wait()


def solve_kernel(lat_ref, got_ref, *refs):
    slabs, out_ref, four_ref, sems = refs[:4], refs[4], refs[5], refs[6]
    fetch = Fetch(slabs, [four_ref.at[(lat_ref[0] & 3) ^ d] for d in range(4)], sems)
    turned_in = got_ref[...].T
    blocks = []
    mode = lax.broadcasted_iota(jnp.int32, (8, 1024), 0).astype(f32)
    eye_rows = lax.broadcasted_iota(jnp.int32, (64, 128), 0)
    eye = jnp.where(eye_rows == lanes((64, 128)), 1.0, 0.0)
    for t in range(2):
        both = jnp.concatenate(
            [turned_in[64 * t : 64 * t + 24], turned_in[64 * t + 32 : 64 * t + 56]], 1
        )
        along_x = mode_cosines(mode, both[17:18] + 0.5)
        along_y = mode_cosines(mode, both[18:19] + 0.5)
        basis = jnp.concatenate([along_x[a : a + 1] * along_y for a in range(8)], 0)
        wide = jnp.concatenate([basis, both[0:16], jnp.zeros((48, 1024), f32)], 0)
        system = lax.dot_general(
            basis * both[16:17],
            wide,
            (((1,), (1,)), ((), ())),
            preferred_element_type=f32,
            precision=lax.Precision.HIGHEST,
        )
        system = system + eye
        blocks.append([system[8 * a : 8 * a + 8] for a in range(8)])
    sub = lax.broadcasted_iota(jnp.int32, (8, 128), 0)
    for at in range(8):
        for inner in range(0, 8, 4):
            picked = [(8 * at + inner + i, inner + i) for i in range(4)]
            for t in range(2):
                mine = blocks[t]
                rows = [
                    jnp.broadcast_to(mine[at][s : s + 1], (8, 128)) for _, s in picked
                ]
                small = [
                    [jnp.broadcast_to(row[:, j : j + 1], (8, 128)) for j, _ in picked]
                    for row in rows
                ]
                count = len(picked)
                for p in range(count):
                    scale = 1.0 / small[p][p]
                    rows[p] = rows[p] * scale
                    small[p] = [v * scale for v in small[p]]
                    for i in range(count):
                        if i != p:
                            by = small[i][p]
                            rows[i] = rows[i] - by * rows[p]
                            small[i] = [
                                v - by * w if k > p else v
                                for k, (v, w) in enumerate(zip(small[i], small[p]))
                            ]
                for k in range(0, 8):
                    new = mine[k]
                    for row, (j, s) in zip(rows, picked):
                        new = new - mine[k][:, j : j + 1] * row
                    if k == at:
                        for row, (j, s) in zip(rows, picked):
                            new = jnp.where(sub == s, row, new)
                    mine[k] = new
    stacked = jnp.concatenate([blocks[t][a] for a in range(8) for t in range(2)], 0)
    final = stacked.T
    odd = (lax.broadcasted_iota(jnp.int32, (32, 128), 0) & 1) == 1
    for f in range(8):
        out_ref[32 * f : 32 * f + 32] = jnp.where(
            odd, final[72 + f : 73 + f], final[64 + f : 65 + f]
        )
    fetch.take(0, 1, 2, 3)


def store_spectrum(spec_ref, u, v, cols):
    first = minus_i(u, [no_first(t, 0) for t in v])
    second = plus_i([no_first(t, 0) for t in u], v)
    for k, value in enumerate((*first, *second)):
        spec_ref[k, :, cols] = value


def wave_pair(waves_ref, which):
    return waves_ref[0, which], waves_ref[1, which]


def own_dot(own_ref, rows_at, value):
    with_high = mm(own_ref[rows_at : rows_at + 64], value[0])
    return with_high[:32] + (with_high[32:] + mm(own_ref[rows_at : rows_at + 32], value[1]))


def shifted(spec_ref, factor_ref, edge_ref, g, start):
    cols, side = pl.ds(start, HALF), pl.ds(start, 128)

    def both_sides(ref, p):
        return jnp.concatenate([ref[g, p, :, side], ref[g, p, :, 128:HALF]], 1)

    fac = [both_sides(factor_ref, p) for p in range(2)]
    fac_edge = [jnp.concatenate([both_sides(edge_ref, p), fac[p][8:]], 0) for p in range(2)]
    s = [spec_ref[i, :, cols] for i in range(4)]
    up = (s[0] * fac[0] - s[1] * fac[1], s[0] * fac[1] + s[1] * fac[0])
    down = (s[2] * fac_edge[0] - s[3] * fac_edge[1], s[2] * fac_edge[1] + s[3] * fac_edge[0])
    even = split(jnp.concatenate([up[p] + no_first(down[p], 0) for p in range(2)], 1))
    odd = split(jnp.concatenate([no_first(up[p], 0) - down[p] for p in range(2)], 1))
    return even, odd


def fold_columns(value):
    left, right = value[:, :HALF], value[:, HALF:]
    return split(left + no_first(right, 1)), split(no_first(left, 1) - right)


def in_three(value):
    high = value.astype(bf16)
    rest = value - high.astype(f32)
    mid = rest.astype(bf16)
    return high, mid, (rest - mid.astype(f32)).astype(bf16)


def own_image(slab, real_ref):
    start = pl.multiple_of(32 * jnp.where(slab < 8, slab, 23 - slab), 32)
    value = real_ref[pl.ds(start, 32), :]
    at = lax.broadcasted_iota(jnp.int32, (32, 32), 0)
    target = jnp.where(slab >= 8, 31 - at, at)
    order = jnp.where(lanes((32, 32)) == target, 1.0, 0.0).astype(bf16)
    pieces = in_three(value)
    value = mm(order, pieces[0]) + mm(order, pieces[1]) + mm(order, pieces[2])
    at = lax.broadcasted_iota(jnp.int32, (HALF, HALF), 0)
    flip = jnp.where(at + lanes((HALF, HALF)) == HALF - 1, 1.0, 0.0).astype(bf16)
    right = mm(jnp.concatenate(in_three(value[:, HALF:]), 0), flip)
    right = right[:32] + right[32:64] + right[64:]
    return jnp.concatenate([value[:, :HALF], right], 1)


def own_field(step, own_back, waves_ref, velocity, slow_ref, freq_ref):
    even, odd = fold_columns(jnp.concatenate([own_back[0], own_back[1]], 0))
    sides = []
    for at in (0, 4):
        u, v = dot3(even, wave_pair(waves_ref, at)), dot3(odd, wave_pair(waves_ref, at + 1))
        sides.append(
            [
                plus_i(
                    halves_of(u[64 * g : 64 * g + 64], 0, 32),
                    halves_of(v[64 * g : 64 * g + 64], 0, 32),
                )
                for g in range(2)
            ]
        )
    back = [
        [jnp.concatenate([sides[0][g][p], sides[1][g][p]], 1) for p in range(2)] for g in range(2)
    ]
    cosine, sine, top = split_turns(velocity, step, slow_ref, freq_ref)
    picked = [jnp.where(top, back[1][p], back[0][p]) for p in range(2)]
    return (
        picked[0] * cosine - picked[1] * sine,
        picked[0] * sine + picked[1] * cosine,
    )


def grid_kernel(lat_ref, freq_ref, slow_ref, got_ref, *refs):
    slabs, refs = refs[:4], refs[4:]
    sources, wave_ref, out_ref = refs[:7], refs[7], refs[8]
    targets, slabs_ref, later_ref, sems = refs[9:16], *refs[16:19]
    spec_ref, own_back, back_ref, half_ref, real_ref = refs[19:]
    fetch = Fetch(
        [
            *sources[:2],
            sources[2].at[lat_ref[0]],
            sources[3].at[0],
            *sources[4:],
            *slabs,
            sources[3].at[1],
        ],
        [*targets, *[slabs_ref.at[(lat_ref[0] >> 2) ^ d] for d in range(4)], later_ref],
        sems,
    )
    rows = lax.broadcasted_iota(jnp.int32, (128, 128), 0)
    groups = lanes((128, 128)) >> 4
    stacked = []
    for p in range(2):
        value = got_ref[pl.ds(p, 128, stride=2), :]
        for k in (1, 2, 4):
            s_bit, g_bit = (rows & k) != 0, (groups & k) != 0
            down = turned(turned(value, k, 0), -16 * k, 1)
            up = turned(turned(value, -k, 0), 16 * k, 1)
            value = jnp.where(
                s_bit & ~g_bit, down, jnp.where(~s_bit & g_bit, up, value)
            )
        stacked.append(value)
    table = fetch.take(0)
    both = dot3(split(jnp.concatenate(stacked, 0)), (table[0], table[1]))
    u, v = (halves_of(t, 0, 128) for t in (both[:, :HALF], both[:, HALF:]))
    first = minus_i(u, [no_first(t, 1) for t in v])
    second = plus_i([no_first(t, 1) for t in u], v)
    table = fetch.take(1)
    for c, here in enumerate((first, second)):
        both = dot3((table[0], table[1]), split(jnp.concatenate(here, 1)))
        store_spectrum(
            spec_ref,
            halves_of(both[:HALF], 1, HALF),
            halves_of(both[HALF:], 1, HALF),
            pl.ds(HALF * c, HALF),
        )
    own_ref, factor_ref, edge_ref, waves_ref = fetch.take(2, 3, 4, 5)
    for g in range(2):
        for c in range(2):
            cols = pl.ds(HALF * c, HALF)
            even, odd = shifted(spec_ref, factor_ref, edge_ref.at[0], g, HALF * c)
            u = halves_of(dot3(wave_pair(waves_ref, 2), even), 1, HALF)
            v = halves_of(dot3(wave_pair(waves_ref, 3), odd), 1, HALF)
            first, second = plus_i(u, v), minus_i(u, v)
            for p in range(2):
                back_ref[g, p, :HALF, cols] = first[p]
                back_ref[g, p, HALF:, cols] = second[p]
    vel_ref = fetch.take(6)
    fetch.take(7, 8, 9, 10)

    def some_rows(k, carry):
        at = pl.ds(pl.multiple_of(k * 128, 128), 128)
        back = []
        for g in range(2):
            even, odd = fold_columns(
                jnp.concatenate([back_ref[g, p, at, :] for p in range(2)], 0)
            )
            u = halves_of(dot3(even, wave_pair(waves_ref, 0)), 0, 128)
            v = halves_of(dot3(odd, wave_pair(waves_ref, 1)), 0, 128)
            back.append((plus_i(u, v), minus_i(u, v)))
        slabs = [
            slabs_ref[jnp.where(k < 2, k, 5 - k), jnp.where(k < 2, i, 3 - i)] for i in range(4)
        ]
        velocity = jnp.concatenate(slabs, 0).astype(jnp.int32)
        fields = []
        for side in range(2):
            cosine, sine, top = split_turns(
                velocity[:, HALF * side : HALF * side + HALF], 0, slow_ref, freq_ref
            )
            picked = [jnp.where(top, back[1][side][p], back[0][side][p]) for p in range(2)]
            fields.append(
                jnp.concatenate(
                    [
                        picked[0] * cosine - picked[1] * sine,
                        picked[0] * sine + picked[1] * cosine,
                    ],
                    0,
                )
            )
        for side in range(2):
            real_ref[at, HALF * side : HALF * side + HALF] = fields[side][:128]
        u = halves_of(dot3(split(fields[0] + fields[1]), wave_pair(waves_ref, 2)), 0, 128)
        v = halves_of(dot3(split(fields[0] - fields[1]), wave_pair(waves_ref, 3)), 0, 128)
        first = minus_i(u, [no_first(t, 1) for t in v])
        second = plus_i([no_first(t, 1) for t in u], v)
        for p in range(2):
            half_ref[p, at, :HALF] = first[p]
            half_ref[p, at, HALF:] = second[p]
        return carry

    lax.fori_loop(0, 4, some_rows, 0, unroll=True)

    def some_columns(c, carry):
        cols = pl.ds(pl.multiple_of(c * HALF, HALF), HALF)
        top = jnp.concatenate([half_ref[p, :HALF, cols] for p in range(2)], 1)
        low = jnp.concatenate([half_ref[p, HALF:, cols] for p in range(2)], 1)
        u = halves_of(dot3(wave_pair(waves_ref, 0), split(top + low)), 1, HALF)
        v = halves_of(dot3(wave_pair(waves_ref, 1), split(top - low)), 1, HALF)
        store_spectrum(spec_ref, u, v, cols)
        return carry

    lax.fori_loop(0, 2, some_columns, 0, unroll=True)
    later_factor = fetch.take(11)

    def invert(k, carry):
        start = pl.multiple_of((k & 1) * HALF, HALF)
        cols = pl.ds(start, HALF)
        even, odd = shifted(spec_ref, later_factor, edge_ref.at[1], k >> 1, start)
        mine = plus_i(
            halves_of(own_dot(own_ref, 0, even), 1, HALF),
            halves_of(own_dot(own_ref, 64, odd), 1, HALF),
        )
        for p in range(2):
            own_back[k >> 1, 32 * p : 32 * p + 32, cols] = mine[p]
        return carry

    lax.fori_loop(0, 4, invert, 0, unroll=True)
    field = own_field(1, own_back, waves_ref, vel_ref[1], slow_ref, freq_ref)
    for p in range(2):
        wave_ref[p] = field[p]
    image = own_image(lat_ref[0], real_ref)
    upper = lanes((32, 128)) >= 64
    for d in range(8):
        col, pos = d // 2, d % 2
        first = turned(image[:, 128 * col : 128 * col + 128], -64 * pos)
        second = turned(field[0][:, 128 * col : 128 * col + 128], 64 - 64 * pos)
        out_ref[d] = jnp.where(upper, second, first)


def sum_kernel(got_ref, out_ref):
    total = got_ref[0]
    for d in range(1, 8):
        total = total + got_ref[d]
    out_ref[0] = total[:, :64]
    out_ref[1] = total[:, 64:]


def call(kernel, outs, in_specs, mega, scratch=(), out_specs=None):
    many = isinstance(outs, list)
    shapes = [jax.ShapeDtypeStruct(s, f32) for s in (outs if many else [outs])]
    return pl.pallas_call(
        kernel,
        out_shape=shapes if many else shapes[0],
        in_specs=in_specs,
        out_specs=out_specs or ([VM] * len(shapes) if many else VM),
        scratch_shapes=list(scratch),
        compiler_params=pltpu.CompilerParams(vmem_limit_bytes=mega * 1024 * 1024),
    )


def local(spectra, tile_route, bin_in_tile, trace_offset, weights, frequency, slowness, vel_index):
    const = tables()
    lat_at = lax.axis_index("lat").astype(jnp.int32).reshape(1)
    everyone = ("freq", "lat")
    sent, velocity = call(
        route_kernel,
        [(512, 128), (32, 512)],
        [SM] + [HBM] * 6,
        60,
        [
            pltpu.VMEM((1, 1024), jnp.int32),
            pltpu.VMEM((1, 1024), jnp.int32),
            pltpu.VMEM((2, 1024), f32),
            pltpu.VMEM((1, 1024), f32),
            pltpu.VMEM((16, 1024), f32),
            pltpu.VMEM((32, 512), jnp.int32),
            pltpu.SemaphoreType.DMA((6,)),
        ],
    )(
        lat_at,
        tile_route.reshape(1, 1024),
        bin_in_tile.reshape(1, 1024),
        trace_offset,
        weights.reshape(1, 1024),
        spectra.reshape(16, 1024),
        vel_index,
    )
    got = lax.all_to_all(sent.reshape(128, 4, 128), everyone, 0, 0, tiled=True)
    slabs = [velocity] + [
        lax.ppermute(velocity, "lat", [(i, i ^ d) for i in range(16)]) for d in (1, 2, 3)
    ]
    sent, slabs = call(
        solve_kernel,
        [(256, 128), (4, 32, 512)],
        [SM, VM] + [HBM] * 4,
        24,
        [pltpu.SemaphoreType.DMA((4,))],
        [VM, HBM],
    )(lat_at, got.reshape(512, 128), *slabs)
    got = lax.all_to_all(sent.reshape(128, 2, 128), everyone, 0, 0, tiled=True)
    slabs = [slabs] + [
        lax.ppermute(slabs, "lat", [(i, i ^ d) for i in range(16)]) for d in (4, 8, 12)
    ]
    factor, edge = call(
        factor_kernel,
        [(2, 2, 2, 256, 384), (2, 2, 2, 8, 384)],
        [SM, SM],
        59,
        [pltpu.VMEM((2, 2, 2, 256, 384), f32), pltpu.SemaphoreType.DMA((4,))],
        [HBM, VM],
    )(frequency, slowness)
    wave, sent = call(
        grid_kernel,
        [(2, 32, 512), (8, 32, 128)],
        [SM, SM, SM, VM] + [HBM] * 11,
        59,
        [
            pltpu.VMEM((2, 128, 512), bf16),
            pltpu.VMEM((2, 512, 128), bf16),
            pltpu.VMEM((128, 256), bf16),
            pltpu.VMEM((2, 2, 256, 384), f32),
            pltpu.VMEM((2, 2, 2, 8, 384), f32),
            pltpu.VMEM((2, 6, 256, 256), bf16),
            pltpu.VMEM((2, 32, 512), jnp.int32),
            pltpu.VMEM((4, 4, 32, 512), f32),
            pltpu.VMEM((2, 2, 256, 384), f32),
            pltpu.SemaphoreType.DMA((12,)),
            pltpu.VMEM((4, 256, 512), f32),
            pltpu.VMEM((2, 64, 512), f32),
            pltpu.VMEM((2, 2, 512, 512), f32),
            pltpu.VMEM((2, 512, 512), f32),
            pltpu.VMEM((512, 512), f32),
        ],
    )(
        lat_at,
        frequency,
        slowness,
        got.reshape(256, 128),
        *slabs,
        const["along_y"],
        const["along_x"],
        const["own"],
        factor,
        edge,
        const["waves"],
        vel_index,
    )
    got = lax.all_to_all(sent, "freq", 0, 0, tiled=True)
    depth_image = call(sum_kernel, (2, 32, 64), [VM], 16)(got)
    return (wave.reshape(2, 1, 32, 512), depth_image)


def solution(mesh):
    return jax.shard_map(
        local,
        mesh=mesh,
        in_specs=(
            P(None, None, ("freq", "lat")),
            P(("freq", "lat"), None),
            P(("freq", "lat")),
            P(None, ("freq", "lat")),
            P(("freq", "lat")),
            P("freq"),
            P(),
            P(None, "lat", None),
        ),
        out_specs=(P(None, "freq", "lat", None), P(None, "lat", "freq")),
        check_vma=False,
    )
```
